256 devices in a mesh: src: 8 (over y, core), obs: 32 (over x, z).
Axes of the slice: x: 4, y: 4, z: 8, core: 2. Of those that a mesh axis runs over, the one named last changes fastest.
Arguments:
- krylov_basis: float32 [16, 2, 8, 1048576], P(None, None, None, ('src', 'obs')), as said below
- near_field: bfloat16 [2, 8192, 128, 128], P(None, ('src', 'obs')), as said below
- leaf_in: bfloat16 [2, 8192, 128, 128], P(None, ('src', 'obs')), may hold values from -0.375 to 0.375
- leaf_out: bfloat16 [2, 8192, 128, 128], P(None, ('src', 'obs')), may hold values from -0.375 to 0.375
- level_mixers: float32 [5, 2, 2, 128, 32768], P(None, None, None, None, ('src', 'obs')), may hold values from -0.25 to 0.25
- block_ranks: int32 [5, 8192], P(None, ('src', 'obs')), may hold values from 64 to 128
- partner_tables: int32 [5, 256, 32], P(None, ('src', 'obs')), may hold values from 0 to 31, each once within a row
Outputs:
- gram_coeffs: float32 [16, 2, 8, 8], replicated
- new_block: float32 [2, 8, 1048576], P(None, None, ('src', 'obs'))
- block_gram: float32 [2, 8, 8], replicated
The draws below stay inside these ranges and needn't reach their ends.
Inputs may be any that keep to these rules, and one draw needn't show every extreme that they name: `krylov_basis`: real and imaginary parts of basis entries; the blocks are not mutually orthogonal. `near_field`: real and imaginary parts of each leaf's self-interaction block. `partner_tables`: each row of 32 entries is a permutation of 0 to 31.
All inputs are finite; a program needn't handle non-finite values.
Results may differ from the reference program's by a relative error of at most 0.0034.
Values sent between devices are 32-bit elements; how exact they have to be, the bound alone decides.
No kernel may reach another device: no remote copies, remote signals or barrier semaphores. Data moves between devices by JAX's collectives and lax.ppermute only.
A program may use at most 128 MiB of HBM per device.

```python
import math
import jax
import jax.numpy as jnp
import numpy as np
from jax import lax

A = 8
K = 16
LEAF = 128
R = 128
LEVELS = 5
NB = 32
BLOCKS = 8192
NUNK = 1048576
N_SRC = 8
N_OBS = 32


def draw_krylov_basis(key, part):
    key = jax.random.fold_in(key, 11)
    first_key, second_key = jax.random.split(key, 2)
    shape = (K, 2, A, NUNK)
    base = jax.random.normal(first_key, shape, jnp.float32) * math.sqrt(0.5)
    common = jax.random.normal(second_key, (1, 2, A, NUNK), jnp.float32) * math.sqrt(0.5)
    return (base + 0.3 * common).astype(jnp.float32)


def draw_near_field(key, part):
    key = jax.random.fold_in(key, 23)
    first_key, second_key = jax.random.split(key)
    shape = (2, BLOCKS, LEAF, LEAF)
    entries = jax.random.normal(first_key, shape, jnp.float32) * math.sqrt(1.0 / (2.0 * LEAF))
    gains = jax.random.uniform(second_key, (1, BLOCKS, LEAF, 1), jnp.float32, 1.0, 2.0)
    rows = jax.lax.broadcasted_iota(jnp.int32, shape, 2)
    columns = jax.lax.broadcasted_iota(jnp.int32, shape, 3)
    layer = jax.lax.broadcasted_iota(jnp.int32, shape, 0)
    diagonal = jnp.where((rows == columns) & (layer == 0), gains, 0.0)
    return (entries + diagonal).astype(jnp.bfloat16)


def set_ends(values, key, smallest, largest):
    index_at = [jax.random.randint(jax.random.fold_in(key, axis), (), 0, length) for axis, length in enumerate(values.shape)]
    main_axis = values.shape.index(max(values.shape))
    beside = index_at[:main_axis] + [(index_at[main_axis] + 1) % values.shape[main_axis]] + index_at[main_axis + 1:]
    return values.at[tuple(index_at)].set(smallest).at[tuple(beside)].set(largest)


def block_scale(stream_key, dims, shards, least, largest):
    loudness = 1.0
    for dim, parts in shards:
        steps = jax.random.uniform(jax.random.fold_in(jax.random.fold_in(stream_key, 6), dim), (parts,), jnp.float32, least / len(shards), largest / len(shards))
        loudness = loudness * jnp.repeat(jnp.exp(steps), dims[dim] // parts).reshape((-1,) + (1,) * (len(dims) - 1 - dim))
    return loudness


def normal_values(stream_key, dims, spread, most, pieces=(), kind=jnp.bfloat16):
    result = spread * jax.random.normal(stream_key, dims, jnp.float32)
    if pieces:
        result = result * block_scale(stream_key, dims, pieces, -0.22, 0.18)
    return jnp.clip(result, -most, most).astype(kind)


def setup_inputs(seed: int = 0) -> dict:
    seeds = jax.random.split(jax.random.key(seed), 8)
    krylov_basis = draw_krylov_basis(jax.random.fold_in(seeds[7], 71), 0)
    near_field = draw_near_field(jax.random.fold_in(seeds[7], 71), 0)
    leaf_in = normal_values(seeds[2], (2, BLOCKS, R, LEAF), (2 * LEAF) ** -0.5, 0.375, ((1, 256),))
    leaf_out = normal_values(seeds[3], (2, BLOCKS, LEAF, R), (2 * R) ** -0.5, 0.375, ((1, 256),))
    level_mixers = normal_values(seeds[4], (LEVELS, 2, 2, R, R * N_SRC * N_OBS), (4 * R) ** -0.5, 0.25, ((4, 256),), jnp.float32)
    block_ranks = set_ends(jax.random.randint(seeds[5], (LEVELS, BLOCKS), R // 2, R + 1), jax.random.fold_in(seeds[5], 1), R // 2, R).astype(jnp.int32)
    partner_tables = jax.vmap(lambda own: jax.random.permutation(own, NB))(jax.random.split(seeds[6], LEVELS * (N_SRC * N_OBS))).reshape((LEVELS, N_SRC * N_OBS, NB)).astype(jnp.int32)
    return {"krylov_basis": krylov_basis, "near_field": near_field, "leaf_in": leaf_in, "leaf_out": leaf_out, "level_mixers": level_mixers, "block_ranks": block_ranks, "partner_tables": partner_tables}


def complex_einsum(form, left, right):
    real_part = jnp.einsum(form, left[0], right[0], precision=lax.Precision.HIGHEST) - jnp.einsum(form, left[1], right[1], precision=lax.Precision.HIGHEST)
    imag_part = jnp.einsum(form, left[0], right[1], precision=lax.Precision.HIGHEST) + jnp.einsum(form, left[1], right[0], precision=lax.Precision.HIGHEST)
    return real_part, imag_part


def conj_einsum(form, left, right):
    real_part = jnp.einsum(form, left[0], right[0], precision=lax.Precision.HIGHEST) + jnp.einsum(form, left[1], right[1], precision=lax.Precision.HIGHEST)
    imag_part = jnp.einsum(form, left[0], right[1], precision=lax.Precision.HIGHEST) - jnp.einsum(form, left[1], right[0], precision=lax.Precision.HIGHEST)
    return real_part, imag_part


def reference(krylov_basis, near_field, leaf_in, leaf_out, level_mixers, block_ranks, partner_tables):
    devices = N_SRC * N_OBS
    newest = krylov_basis[K - 1].astype(jnp.bfloat16)
    vec_blocks = newest.reshape(2, A, devices * NB, LEAF)

    def project_leaves(device):
        start = (device * NB).astype(jnp.int32)
        piece = lax.dynamic_slice_in_dim(vec_blocks, start, NB, 2).astype(jnp.float32)
        basis_in = lax.dynamic_slice_in_dim(leaf_in, start, NB, 1).astype(jnp.float32)
        real_part, imag_part = complex_einsum("abl,brl->abr", (piece[0], piece[1]), (basis_in[0], basis_in[1]))
        return jnp.stack([real_part, imag_part])

    coeffs = lax.map(project_leaves, jnp.arange(devices, dtype=jnp.int32))
    device_ids = np.arange(devices)
    src_ids = device_ids // N_OBS
    obs_ids = device_ids % N_OBS
    src_bits = N_SRC.bit_length() - 1
    obs_bits = N_OBS.bit_length() - 1
    plan = [("src", src_bits - 1), ("src", src_bits - 2), ("obs", obs_bits - 1), ("obs", obs_bits - 2), ("obs", obs_bits - 3)]
    column_ids = jnp.arange(R, dtype=jnp.int32)
    for level_index, (axis_name, bit_number) in enumerate(plan):
        if axis_name == "src":
            partner_ids = (src_ids ^ (1 << bit_number)) * N_OBS + obs_ids
        else:
            partner_ids = src_ids * N_OBS + (obs_ids ^ (1 << bit_number))
        partner = coeffs[jnp.asarray(partner_ids, dtype=jnp.int32)]
        table = partner_tables[level_index]
        index_table = jnp.broadcast_to(table[:, None, None, :, None], partner.shape)
        picked = jnp.take_along_axis(partner, index_table, axis=3)
        mixing = level_mixers[level_index].reshape(2, 2, R, devices, R)
        own = complex_einsum("dabr,rds->dabs", (coeffs[:, 0], coeffs[:, 1]), (mixing[0, 0], mixing[0, 1]))
        cross = complex_einsum("dabr,rds->dabs", (picked[:, 0], picked[:, 1]), (mixing[1, 0], mixing[1, 1]))
        live = column_ids[None, None, :] < block_ranks[level_index].reshape(devices, NB)[:, :, None]
        mixed = jnp.stack([own[0] + cross[0], own[1] + cross[1]], axis=1)
        coeffs = jnp.where(live[:, None, None], mixed, jnp.float32(0.0))
    rounded = coeffs.astype(jnp.bfloat16)

    def expand_leaves(device):
        start = (device * NB).astype(jnp.int32)
        piece = lax.dynamic_slice_in_dim(vec_blocks, start, NB, 2).astype(jnp.float32)
        coeff_here = rounded[device].astype(jnp.float32)
        basis_out = lax.dynamic_slice_in_dim(leaf_out, start, NB, 1).astype(jnp.float32)
        near_here = lax.dynamic_slice_in_dim(near_field, start, NB, 1).astype(jnp.float32)
        far = complex_einsum("abr,blr->abl", (coeff_here[0], coeff_here[1]), (basis_out[0], basis_out[1]))
        close = complex_einsum("abm,blm->abl", (piece[0], piece[1]), (near_here[0], near_here[1]))
        return jnp.stack([far[0] + close[0], far[1] + close[1]])

    image_parts = lax.map(expand_leaves, jnp.arange(devices, dtype=jnp.int32))
    image = jnp.transpose(image_parts, (1, 2, 0, 3, 4)).reshape(2, A, NUNK)
    basis_pair = (krylov_basis[:, 0], krylov_basis[:, 1])

    def project(field):
        real_part, imag_part = conj_einsum("kan,bn->kab", basis_pair, (field[0], field[1]))
        return jnp.stack([real_part, imag_part], axis=1) / jnp.float32(NUNK)

    def remove(field, factors):
        real_part, imag_part = complex_einsum("kan,kab->bn", basis_pair, (factors[:, 0], factors[:, 1]))
        return field - jnp.stack([real_part, imag_part])

    first = project(image)
    after_first = remove(image, first)
    second = project(after_first)
    new_block = remove(after_first, second)
    real_part, imag_part = conj_einsum("an,bn->ab", (new_block[0], new_block[1]), (new_block[0], new_block[1]))
    block_gram = jnp.stack([real_part, imag_part]) / jnp.float32(NUNK)
    return first + second, new_block, block_gram
```

```python
import jax
import jax.numpy as jnp
from jax import lax
from jax.experimental import pallas as pl
from jax.experimental.pallas import tpu as pltpu
from jax.sharding import PartitionSpec as P

NT = (((1,), (1,)), ((), ()))
NN = (((1,), (0,)), ((), ()))
KERNEL_VMEM = 24 * 1024 * 1024


def dot_nt(left, right):
    return lax.dot_general(left, right, NT, preferred_element_type=jnp.float32)


def dot_nn(left, right):
    return lax.dot_general(left, right, NN, preferred_element_type=jnp.float32)


def split3(value):
    high = value.astype(jnp.bfloat16)
    rest = value - high.astype(jnp.float32)
    middle = rest.astype(jnp.bfloat16)
    low = (rest - middle.astype(jnp.float32)).astype(jnp.bfloat16)
    return high, middle, low


def complex_rows(rows):
    real, imag = rows[:8], rows[8:]
    return jnp.concatenate(
        [jnp.concatenate([real, -imag], axis=1), jnp.concatenate([imag, real], axis=1)], axis=0
    )


def leaf_product(rows, real, imag):
    return dot_nt(
        complex_rows(rows).astype(jnp.bfloat16), jnp.concatenate([real, imag], axis=1)
    )


def leaves_kernel(basis_ref, leaf_ref, out_ref):
    count = leaf_ref.shape[1]
    for leaf in range(count):
        rows = basis_ref[0, :, :, leaf * 128 : (leaf + 1) * 128].reshape(16, 128)
        rows = rows.astype(jnp.bfloat16).astype(jnp.float32)
        out_ref[leaf] = leaf_product(rows, leaf_ref[0, leaf], leaf_ref[1, leaf])


def apply_leaves(krylov_basis, leaves, steps):
    last = krylov_basis.shape[0] - 1
    count = leaves.shape[1]
    part = count // steps
    return pl.pallas_call(
        leaves_kernel,
        grid=(steps,),
        in_specs=[
            pl.BlockSpec((1, 2, 8, part * 128), lambda i: (last, 0, 0, i)),
            pl.BlockSpec((2, part, 128, 128), lambda i: (0, i, 0, 0)),
        ],
        out_specs=pl.BlockSpec((part, 16, 128), lambda i: (i, 0, 0)),
        out_shape=jax.ShapeDtypeStruct((count, 16, 128), jnp.float32),
        compiler_params=pltpu.CompilerParams(vmem_limit_bytes=KERNEL_VMEM),
        cost_estimate=pl.CostEstimate(
            flops=count * 16 * 256 * 128 * 2, bytes_accessed=count * 73728, transcendentals=0
        ),
    )(krylov_basis, leaves)


def stacked(basis):
    width = basis.shape[3]
    return jnp.concatenate(
        [basis[:, 0].reshape(128, width), basis[:, 1].reshape(128, width)], axis=0
    )


def basis_gram_kernel(basis_ref, out_ref, even_ref, odd_ref):
    step = pl.program_id(0)

    @pl.when(step == 0)
    def _():
        even_ref[...] = jnp.zeros_like(even_ref)
        odd_ref[...] = jnp.zeros_like(odd_ref)

    high, middle, low = split3(stacked(basis_ref[...]))
    even_ref[...] += dot_nt(high, high) + dot_nt(middle, middle)
    odd_ref[...] += dot_nt(high, middle) + dot_nt(high, low)

    @pl.when(step == pl.num_programs(0) - 1)
    def _():
        gram = even_ref[...] + odd_ref[...] + odd_ref[...].T
        real = gram[:128, :128] + gram[128:, 128:]
        imag = gram[:128, 128:] - gram[128:, :128]
        row = lax.broadcasted_iota(jnp.int32, (128, 128), 0)
        column = lax.broadcasted_iota(jnp.int32, (128, 128), 1)
        out_ref[...] = jnp.where(row <= column, real, imag)


def basis_gram(krylov_basis, steps):
    width = krylov_basis.shape[3] // steps
    return pl.pallas_call(
        basis_gram_kernel,
        grid=(steps,),
        in_specs=[pl.BlockSpec((16, 2, 8, width), lambda i: (0, 0, 0, i))],
        out_specs=pl.BlockSpec((128, 128), lambda i: (0, 0)),
        out_shape=jax.ShapeDtypeStruct((128, 128), jnp.float32),
        scratch_shapes=[pltpu.VMEM((256, 256), jnp.float32)] * 2,
        compiler_params=pltpu.CompilerParams(vmem_limit_bytes=KERNEL_VMEM),
        cost_estimate=pl.CostEstimate(
            flops=4 * 2 * 256 * 256 * 4096, bytes_accessed=4 << 20, transcendentals=0
        ),
    )(krylov_basis)


def mix(level, own_ref, partner_ref, mixer_ref, rank_ref, table_ref, picked_ref, write):
    for leaf in range(32):
        picked_ref[leaf] = partner_ref[table_ref[level, 0, leaf]]
    both = jnp.concatenate(
        [own_ref[...].reshape(512, 128), picked_ref[...].reshape(512, 128)], axis=1
    )
    mixer = mixer_ref[0]
    weights = jnp.concatenate(
        [
            jnp.concatenate([mixer[0, 0], mixer[0, 1]], axis=1),
            jnp.concatenate([mixer[1, 0], mixer[1, 1]], axis=1),
        ],
        axis=0,
    )
    product = jnp.dot(
        both, weights, precision=lax.Precision.HIGHEST, preferred_element_type=jnp.float32
    )
    column = lax.broadcasted_iota(jnp.int32, (16, 128), 1)
    for leaf in range(32):
        by_real = product[leaf * 16 : (leaf + 1) * 16, :128]
        by_imag = product[leaf * 16 : (leaf + 1) * 16, 128:]
        mixed = jnp.concatenate([by_real[:8] - by_imag[8:], by_real[8:] + by_imag[:8]], axis=0)
        write(leaf, jnp.where(column < rank_ref[level, leaf], mixed, 0.0))


def level_kernel(level, own_ref, partner_ref, mixer_ref, rank_ref, table_ref, out_ref, picked_ref):
    def write(leaf, value):
        out_ref[leaf] = value

    mix(level, own_ref, partner_ref, mixer_ref, rank_ref, table_ref, picked_ref, write)


def whole(shape):
    return pl.BlockSpec(shape, lambda i: (0,) * len(shape))


def level_specs(level):
    return [
        whole((32, 16, 128)),
        whole((32, 16, 128)),
        pl.BlockSpec((1, 2, 2, 128, 128), lambda i: (level, 0, 0, 0, 0)),
        pl.BlockSpec(memory_space=pltpu.SMEM),
        pl.BlockSpec(memory_space=pltpu.SMEM),
    ]


def next_level(level, own, partner, level_mixers, block_ranks, partner_tables):
    return pl.pallas_call(
        lambda *refs: level_kernel(level, *refs),
        grid=(1,),
        in_specs=level_specs(level),
        out_specs=whole((32, 16, 128)),
        out_shape=jax.ShapeDtypeStruct((32, 16, 128), jnp.float32),
        scratch_shapes=[pltpu.VMEM((32, 16, 128), jnp.float32)],
        compiler_params=pltpu.CompilerParams(vmem_limit_bytes=KERNEL_VMEM),
        cost_estimate=pl.CostEstimate(
            flops=6 * 512 * 256 * 256 * 2, bytes_accessed=1 << 20, transcendentals=0
        ),
    )(own, partner, level_mixers, block_ranks, partner_tables)


def project_kernel(
    level, own_ref, partner_ref, mixer_ref, rank_ref, table_ref, leaf_ref, close_ref, basis_ref,
    image_ref, sums_ref, picked_ref,
):
    def write(leaf, value):
        rounded = value.astype(jnp.bfloat16).astype(jnp.float32)
        far = leaf_product(rounded, leaf_ref[0, leaf], leaf_ref[1, leaf])
        image_ref[:, leaf * 128 : (leaf + 1) * 128] = far + close_ref[leaf]

    mix(level, own_ref, partner_ref, mixer_ref, rank_ref, table_ref, picked_ref, write)
    image = image_ref[...]
    high, middle, low = split3(image)
    three = jnp.concatenate([high, middle, low], axis=0)
    two = three[:32]
    inner = jnp.zeros((16, 256), jnp.float32)
    width = 1024
    for start in range(0, 4096, width):
        here = slice(start, start + width)
        b_high, b_middle, b_low = split3(stacked(basis_ref[:, :, :, here]))
        one = dot_nt(three[:, here], b_high)
        inner += one[:16] + one[16:32] + one[32:]
        one = dot_nt(two[:, here], b_middle)
        inner += one[:16] + one[16:]
        inner += dot_nt(high[:, here], b_low)
    sums_ref[0:8] = inner[:8, :128] + inner[8:, 128:]
    sums_ref[8:16] = inner[8:, :128] - inner[:8, 128:]
    one = dot_nt(three, high)
    square = one[:16] + one[16:32] + one[32:]
    one = dot_nt(two, middle)
    square += one[:16] + one[16:]
    square += dot_nt(high, low)
    real = square[:8, :8] + square[8:, 8:]
    imag = square[:8, 8:] - square[8:, :8]
    sums_ref[16:24] = jnp.concatenate([real, imag, jnp.zeros((8, 112), jnp.float32)], axis=1)


def project(level, own, partner, level_mixers, block_ranks, partner_tables, leaf_out, close, krylov_basis):
    return pl.pallas_call(
        lambda *refs: project_kernel(level, *refs),
        grid=(1,),
        in_specs=level_specs(level)
        + [whole(leaf_out.shape), whole(close.shape), whole(krylov_basis.shape)],
        out_specs=[whole((16, 4096)), whole((24, 128))],
        out_shape=[
            jax.ShapeDtypeStruct((16, 4096), jnp.float32),
            jax.ShapeDtypeStruct((24, 128), jnp.float32),
        ],
        scratch_shapes=[pltpu.VMEM((32, 16, 128), jnp.float32)],
        compiler_params=pltpu.CompilerParams(vmem_limit_bytes=KERNEL_VMEM),
        cost_estimate=pl.CostEstimate(
            flops=6 * 512 * 256 * 256 * 2, bytes_accessed=8 << 20, transcendentals=0
        ),
    )(own, partner, level_mixers, block_ranks, partner_tables, leaf_out, close, krylov_basis)


def dot_high(left, right, numbers):
    return lax.dot_general(
        left, right, numbers, precision=lax.Precision.HIGHEST, preferred_element_type=jnp.float32
    )


def finish_kernel(scale, sums_ref, gram_ref, image_ref, basis_ref, total_ref, new_ref, block_ref):
    sums = jnp.sum(sums_ref[...], axis=0) * scale
    first = sums[:16]
    packed = gram_ref[...] * scale
    row = lax.broadcasted_iota(jnp.int32, (128, 128), 0)
    column = lax.broadcasted_iota(jnp.int32, (128, 128), 1)
    flipped = packed.T
    gram_real = jnp.where(row <= column, packed, flipped)
    gram_imag = jnp.where(row > column, packed, jnp.where(row < column, -flipped, 0.0))
    gram = jnp.concatenate([gram_real, gram_imag], axis=1)

    def by_gram(rows):
        one = dot_high(rows, gram, NN)
        real = one[:8, :128] + one[8:, 128:]
        imag = one[8:, :128] - one[:8, 128:]
        return jnp.concatenate([real, imag], axis=0)

    total = first + (first - by_gram(first))
    rest = first - by_gram(total)

    def inner(left, right):
        one = dot_high(left, right, NT)
        return one[:8, :8] + one[8:, 8:], one[:8, 8:] - one[8:, :8]

    one_real, one_imag = inner(first, total)
    two_real, two_imag = inner(total, rest)
    block_ref[0] = sums[16:24, 0:8] - one_real - two_real
    block_ref[1] = sums[16:24, 8:16] - one_imag - two_imag
    turned = total.T
    total_ref[:, 0] = turned[:, :8].reshape(16, 8, 8)
    total_ref[:, 1] = turned[:, 8:].reshape(16, 8, 8)
    high, middle, low = split3(complex_rows(total))
    three = jnp.concatenate([high, middle, low], axis=0)
    two = three[:32]
    width = 1024
    for start in range(0, 4096, width):
        here = slice(start, start + width)
        b_high, b_middle, b_low = split3(stacked(basis_ref[:, :, :, here]))
        one = dot_nn(three, b_high)
        taken = one[:16] + one[16:32] + one[32:]
        one = dot_nn(two, b_middle)
        taken += one[:16] + one[16:]
        taken += dot_nn(high, b_low)
        new_ref[:, :, here] = (image_ref[:, here] - taken).reshape(2, 8, width)


def finish(scale, sums, gram, image, krylov_basis):
    return pl.pallas_call(
        lambda *refs: finish_kernel(scale, *refs),
        grid=(1,),
        in_specs=[
            whole(sums.shape),
            whole(gram.shape),
            whole(image.shape),
            whole(krylov_basis.shape),
        ],
        out_specs=[whole((16, 2, 8, 8)), whole((2, 8, 4096)), whole((2, 8, 8))],
        out_shape=[
            jax.ShapeDtypeStruct((16, 2, 8, 8), jnp.float32),
            jax.ShapeDtypeStruct((2, 8, 4096), jnp.float32),
            jax.ShapeDtypeStruct((2, 8, 8), jnp.float32),
        ],
        compiler_params=pltpu.CompilerParams(vmem_limit_bytes=KERNEL_VMEM),
        cost_estimate=pl.CostEstimate(
            flops=6 * 16 * 256 * 4096 * 2, bytes_accessed=6 << 20, transcendentals=0
        ),
    )(sums, gram, image, krylov_basis)


def exchange(value, axis, bit_number):
    pairs = [(source, source ^ (1 << bit_number)) for source in range(lax.axis_size(axis))]
    return lax.ppermute(value, axis, pairs)


def from_all(value, axis):
    copies = jnp.broadcast_to(value[None], (lax.axis_size(axis),) + value.shape)
    return lax.all_to_all(copies, axis, 0, 0)


def per_device(
    krylov_basis, near_field, leaf_in, leaf_out, level_mixers, block_ranks, partner_tables
):
    src_bits = lax.axis_size("src").bit_length() - 1
    obs_bits = lax.axis_size("obs").bit_length() - 1
    plan = [
        ("src", src_bits - 1),
        ("src", src_bits - 2),
        ("obs", obs_bits - 1),
        ("obs", obs_bits - 2),
        ("obs", obs_bits - 3),
    ]
    coeffs = apply_leaves(krylov_basis, leaf_in, 4)
    close = apply_leaves(krylov_basis, near_field, 4)
    gram = basis_gram(krylov_basis, 4)
    for axis, bits in (("src", src_bits), ("obs", obs_bits)):
        for bit in range(bits):
            gram = gram + exchange(gram, axis, bit)
    for level, (axis, bit) in enumerate(plan):
        partner = exchange(coeffs, axis, bit)
        if level < len(plan) - 1:
            coeffs = next_level(level, coeffs, partner, level_mixers, block_ranks, partner_tables)
        else:
            image, sums = project(
                level, coeffs, partner, level_mixers, block_ranks, partner_tables,
                leaf_out, close, krylov_basis,
            )
    sums = jnp.sum(from_all(sums, "src"), axis=0)
    sums = from_all(sums, "obs")
    devices = lax.axis_size("src") * lax.axis_size("obs")
    scale = 1.0 / (krylov_basis.shape[3] * devices)
    return tuple(finish(scale, sums, gram, image, krylov_basis))


def solution(mesh):
    in_specs = (
        P(None, None, None, ("src", "obs")),
        P(None, ("src", "obs"), None, None),
        P(None, ("src", "obs"), None, None),
        P(None, ("src", "obs"), None, None),
        P(None, None, None, None, ("src", "obs")),
        P(None, ("src", "obs")),
        P(None, ("src", "obs"), None),
    )
    out_specs = (P(), P(None, None, ("src", "obs")), P())
    return jax.shard_map(
        per_device, mesh=mesh, in_specs=in_specs, out_specs=out_specs, check_vma=False
    )
```

```python
import jax
import jax.numpy as jnp
from jax import lax
from jax.experimental import pallas as pl
from jax.experimental.pallas import tpu as pltpu
from jax.sharding import PartitionSpec as P

NT = (((1,), (1,)), ((), ()))
NN = (((1,), (0,)), ((), ()))
KERNEL_VMEM = 24 * 1024 * 1024
BASIS_PARTS = 4


def in_hbm(value):
    return pltpu.with_memory_space_constraint(value, pltpu.HBM)


def dot_nt(left, right):
    return lax.dot_general(left, right, NT, preferred_element_type=jnp.float32)


def dot_nn(left, right):
    return lax.dot_general(left, right, NN, preferred_element_type=jnp.float32)


def split3(value):
    high = value.astype(jnp.bfloat16)
    rest = value - high.astype(jnp.float32)
    middle = rest.astype(jnp.bfloat16)
    low = (rest - middle.astype(jnp.float32)).astype(jnp.bfloat16)
    return high, middle, low


def complex_rows(rows):
    real, imag = rows[:8], rows[8:]
    return jnp.concatenate(
        [jnp.concatenate([real, -imag], axis=1), jnp.concatenate([imag, real], axis=1)], axis=0
    )


def leaf_product(rows, real, imag):
    return dot_nt(
        complex_rows(rows).astype(jnp.bfloat16), jnp.concatenate([real, imag], axis=1)
    )


def leaves_kernel(basis_ref, leaf_ref, out_ref, newest_ref, held_ref, newest_sem, held_sems):
    steps = held_sems.shape[0]
    count = held_ref.shape[1]
    part = count // steps
    newest_copy = pltpu.make_async_copy(
        basis_ref.at[basis_ref.shape[0] - 1], newest_ref, newest_sem
    )
    newest_copy.start()
    copies = []
    for step in range(steps):
        here = pl.ds(step * part, part)
        copies.append(
            pltpu.make_async_copy(leaf_ref.at[:, here], held_ref.at[:, here], held_sems.at[step])
        )
        copies[-1].start()
    newest_copy.wait()
    for leaf in range(count):
        if leaf % part == 0:
            copies[leaf // part].wait()
        rows = newest_ref[:, :, leaf * 128 : (leaf + 1) * 128].reshape(16, 128)
        rows = rows.astype(jnp.bfloat16).astype(jnp.float32)
        out_ref[leaf] = leaf_product(rows, held_ref[0, leaf], held_ref[1, leaf])


def apply_leaves(krylov_basis, leaves, steps):
    count = leaves.shape[1]
    return pl.pallas_call(
        leaves_kernel,
        in_specs=[pl.BlockSpec(memory_space=pltpu.HBM)] * 2,
        out_specs=pl.BlockSpec(memory_space=pltpu.VMEM),
        out_shape=jax.ShapeDtypeStruct((count, 16, 128), jnp.float32),
        scratch_shapes=[
            pltpu.VMEM(krylov_basis.shape[1:], jnp.float32),
            pltpu.VMEM(leaves.shape, leaves.dtype),
            pltpu.SemaphoreType.DMA,
            pltpu.SemaphoreType.DMA((steps,)),
        ],
        compiler_params=pltpu.CompilerParams(vmem_limit_bytes=KERNEL_VMEM),
        cost_estimate=pl.CostEstimate(
            flops=count * 16 * 256 * 128 * 2, bytes_accessed=count * 73728, transcendentals=0
        ),
    )(in_hbm(krylov_basis), in_hbm(leaves))


def stacked(basis):
    width = basis.shape[3]
    return jnp.concatenate(
        [basis[:, 0].reshape(128, width), basis[:, 1].reshape(128, width)], axis=0
    )


def basis_copies(basis_ref, held_ref, sems):
    steps = sems.shape[0]
    width = held_ref.shape[3] // steps
    copies = []
    for step in range(steps):
        here = pl.ds(step * width, width)
        copies.append(
            pltpu.make_async_copy(
                basis_ref.at[:, :, :, here], held_ref.at[:, :, :, here], sems.at[step]
            )
        )
        copies[-1].start()
    return copies, width


def basis_scratch(krylov_basis):
    return [pltpu.VMEM(krylov_basis.shape, jnp.float32), pltpu.SemaphoreType.DMA((BASIS_PARTS,))]


def basis_gram_kernel(basis_ref, out_ref, held_ref, sems):
    copies, width = basis_copies(basis_ref, held_ref, sems)
    even = jnp.zeros((256, 256), jnp.float32)
    odd = jnp.zeros((256, 256), jnp.float32)
    for step, copy in enumerate(copies):
        copy.wait()
        here = slice(step * width, (step + 1) * width)
        high, middle, low = split3(stacked(held_ref[:, :, :, here]))
        even += dot_nt(high, high) + dot_nt(middle, middle)
        odd += dot_nt(high, middle) + dot_nt(high, low)
    gram = even + odd + odd.T
    real = gram[:128, :128] + gram[128:, 128:]
    imag = gram[:128, 128:] - gram[128:, :128]
    row = lax.broadcasted_iota(jnp.int32, (128, 128), 0)
    column = lax.broadcasted_iota(jnp.int32, (128, 128), 1)
    out_ref[...] = jnp.where(row <= column, real, imag)


def basis_gram(krylov_basis):
    return pl.pallas_call(
        basis_gram_kernel,
        in_specs=[pl.BlockSpec(memory_space=pltpu.HBM)],
        out_specs=pl.BlockSpec(memory_space=pltpu.VMEM),
        out_shape=jax.ShapeDtypeStruct((128, 128), jnp.float32),
        scratch_shapes=basis_scratch(krylov_basis),
        compiler_params=pltpu.CompilerParams(vmem_limit_bytes=KERNEL_VMEM),
        cost_estimate=pl.CostEstimate(
            flops=4 * 2 * 256 * 256 * 4096, bytes_accessed=4 << 20, transcendentals=0
        ),
    )(in_hbm(krylov_basis))


def mix(level, own_ref, partner_ref, mixer_ref, rank_ref, table_ref, picked_ref, write):
    for leaf in range(32):
        picked_ref[leaf] = partner_ref[table_ref[level, 0, leaf]]
    both = jnp.concatenate(
        [own_ref[0:32].reshape(512, 128), picked_ref[...].reshape(512, 128)], axis=1
    )
    mixer = mixer_ref[0]
    weights = jnp.concatenate(
        [
            jnp.concatenate([mixer[0, 0], mixer[0, 1]], axis=1),
            jnp.concatenate([mixer[1, 0], mixer[1, 1]], axis=1),
        ],
        axis=0,
    )
    product = jnp.dot(
        both, weights, precision=lax.Precision.HIGHEST, preferred_element_type=jnp.float32
    )
    column = lax.broadcasted_iota(jnp.int32, (16, 128), 1)
    for leaf in range(32):
        by_real = product[leaf * 16 : (leaf + 1) * 16, :128]
        by_imag = product[leaf * 16 : (leaf + 1) * 16, 128:]
        mixed = jnp.concatenate([by_real[:8] - by_imag[8:], by_real[8:] + by_imag[:8]], axis=0)
        write(leaf, jnp.where(column < rank_ref[level, leaf], mixed, 0.0))


def first_level_kernel(own_ref, partner_ref, mixer_ref, rank_ref, table_ref, gram_ref, out_ref, picked_ref):
    def write(leaf, value):
        out_ref[leaf] = value

    mix(0, own_ref, partner_ref, mixer_ref, rank_ref, table_ref, picked_ref, write)
    out_ref[32:40] = gram_ref[...]


def level_kernel(level, own_ref, partner_ref, mixer_ref, rank_ref, table_ref, out_ref, picked_ref):
    def write(leaf, value):
        out_ref[leaf] = value

    mix(level, own_ref, partner_ref, mixer_ref, rank_ref, table_ref, picked_ref, write)
    out_ref[32:40] = own_ref[32:40] + partner_ref[32:40]


def whole(shape):
    return pl.BlockSpec(shape, lambda i: (0,) * len(shape))


def level_specs(level, own):
    return [
        whole(own.shape),
        whole(own.shape),
        pl.BlockSpec((1, 2, 2, 128, 128), lambda i: (level, 0, 0, 0, 0)),
        pl.BlockSpec(memory_space=pltpu.SMEM),
        pl.BlockSpec(memory_space=pltpu.SMEM),
    ]


def next_level(level, own, partner, level_mixers, block_ranks, partner_tables, gram=None):
    if gram is None:
        kernel, more, more_specs = lambda *refs: level_kernel(level, *refs), [], []
    else:
        kernel, more, more_specs = first_level_kernel, [gram], [whole(gram.shape)]
    return pl.pallas_call(
        kernel,
        grid=(1,),
        in_specs=level_specs(level, own) + more_specs,
        out_specs=whole((40, 16, 128)),
        out_shape=jax.ShapeDtypeStruct((40, 16, 128), jnp.float32),
        scratch_shapes=[pltpu.VMEM((32, 16, 128), jnp.float32)],
        compiler_params=pltpu.CompilerParams(vmem_limit_bytes=KERNEL_VMEM),
        cost_estimate=pl.CostEstimate(
            flops=6 * 512 * 256 * 256 * 2, bytes_accessed=1 << 20, transcendentals=0
        ),
    )(own, partner, level_mixers, block_ranks, partner_tables, *more)


def project_kernel(
    level, own_ref, partner_ref, mixer_ref, rank_ref, table_ref, close_ref, leaf_ref, basis_ref,
    image_ref, sums_ref, picked_ref, gram_ref, leaf_held_ref, leaf_sem, held_ref, sems,
):
    leaf_copy = pltpu.make_async_copy(leaf_ref, leaf_held_ref, leaf_sem)
    leaf_copy.start()
    copies, width = basis_copies(basis_ref, held_ref, sems)
    values = {}

    def write(leaf, value):
        values[leaf] = value.astype(jnp.bfloat16).astype(jnp.float32)

    mix(level, own_ref, partner_ref, mixer_ref, rank_ref, table_ref, picked_ref, write)
    gram_ref[...] = (own_ref[32:40] + partner_ref[32:40]).reshape(128, 128)
    leaf_copy.wait()
    for leaf in range(32):
        far = leaf_product(values[leaf], leaf_held_ref[0, leaf], leaf_held_ref[1, leaf])
        image_ref[:, leaf * 128 : (leaf + 1) * 128] = far + close_ref[leaf]
    high, middle, low = split3(image_ref[...])
    three = jnp.concatenate([high, middle, low], axis=0)
    two = three[:32]
    inner = jnp.zeros((16, 256), jnp.float32)
    for step, copy in enumerate(copies):
        copy.wait()
        here = slice(step * width, (step + 1) * width)
        b_high, b_middle, b_low = split3(stacked(held_ref[:, :, :, here]))
        one = dot_nt(three[:, here], b_high)
        inner += one[:16] + one[16:32] + one[32:]
        one = dot_nt(two[:, here], b_middle)
        inner += one[:16] + one[16:]
        inner += dot_nt(high[:, here], b_low)
    one = dot_nt(three, high)
    square = one[:16] + one[16:32] + one[32:]
    one = dot_nt(two, middle)
    square += one[:16] + one[16:]
    square += dot_nt(high, low)
    real = square[:8, :8] + square[8:, 8:]
    imag = square[:8, 8:] - square[8:, :8]
    sums = jnp.concatenate(
        [
            inner[:8, :128] + inner[8:, 128:],
            inner[8:, :128] - inner[:8, 128:],
            jnp.concatenate([real, imag, jnp.zeros((8, 112), jnp.float32)], axis=1),
        ],
        axis=0,
    )
    mine = lax.rem(lax.axis_index("src"), 4)
    piece = gram_ref[pl.ds(pl.multiple_of(mine * 32, 32), 32), :]
    for device in range(8):
        sums_ref[device, 0:24] = sums
        sums_ref[device, 24:56] = piece


def project(level, own, partner, level_mixers, block_ranks, partner_tables, close, leaf_out, krylov_basis):
    return pl.pallas_call(
        lambda *refs: project_kernel(level, *refs),
        grid=(1,),
        in_specs=level_specs(level, own)
        + [whole(close.shape)]
        + [pl.BlockSpec(memory_space=pltpu.HBM)] * 2,
        out_specs=[whole((16, 4096)), whole((8, 56, 128))],
        out_shape=[
            jax.ShapeDtypeStruct((16, 4096), jnp.float32),
            jax.ShapeDtypeStruct((8, 56, 128), jnp.float32),
        ],
        scratch_shapes=[
            pltpu.VMEM((32, 16, 128), jnp.float32),
            pltpu.VMEM((128, 128), jnp.float32),
            pltpu.VMEM(leaf_out.shape, leaf_out.dtype),
            pltpu.SemaphoreType.DMA,
        ]
        + basis_scratch(krylov_basis),
        compiler_params=pltpu.CompilerParams(vmem_limit_bytes=KERNEL_VMEM),
        cost_estimate=pl.CostEstimate(
            flops=6 * 512 * 256 * 256 * 2, bytes_accessed=8 << 20, transcendentals=0
        ),
    )(
        own, partner, level_mixers, block_ranks, partner_tables, close, in_hbm(leaf_out),
        in_hbm(krylov_basis),
    )


def relay_kernel(got_ref, out_ref, gram_ref):
    sums = jnp.sum(got_ref[:, 0:24], axis=0)
    for quarter in range(4):
        gram_ref[quarter * 32 : (quarter + 1) * 32] = (
            got_ref[quarter, 24:56] + got_ref[quarter + 4, 24:56]
        )
    mine = lax.div(lax.axis_index("obs"), 4)
    piece = gram_ref[pl.ds(pl.multiple_of(mine * 16, 16), 16), :]
    for device in range(32):
        out_ref[device, 0:24] = sums
        out_ref[device, 24:40] = piece


def relay(got):
    return pl.pallas_call(
        relay_kernel,
        out_shape=jax.ShapeDtypeStruct((32, 40, 128), jnp.float32),
        scratch_shapes=[pltpu.VMEM((128, 128), jnp.float32)],
        compiler_params=pltpu.CompilerParams(vmem_limit_bytes=KERNEL_VMEM),
    )(got)


def dot_high(left, right, numbers):
    return lax.dot_general(
        left, right, numbers, precision=lax.Precision.HIGHEST, preferred_element_type=jnp.float32
    )


def finish_kernel(
    scale, got_ref, image_ref, basis_ref, total_ref, new_ref, block_ref, gram_ref, held_ref, sems
):
    copies, width = basis_copies(basis_ref, held_ref, sems)
    sums = jnp.sum(got_ref[:, 0:24], axis=0) * scale
    first = sums[:16]
    for part in range(8):
        four = got_ref[part * 4 : part * 4 + 4, 24:40]
        gram_ref[part * 16 : (part + 1) * 16] = jnp.sum(four, axis=0) * scale
    packed = gram_ref[...]
    row = lax.broadcasted_iota(jnp.int32, (128, 128), 0)
    column = lax.broadcasted_iota(jnp.int32, (128, 128), 1)
    flipped = packed.T
    gram_real = jnp.where(row <= column, packed, flipped)
    gram_imag = jnp.where(row > column, packed, jnp.where(row < column, -flipped, 0.0))
    gram = jnp.concatenate([gram_real, gram_imag], axis=1)

    def by_gram(rows):
        one = dot_high(rows, gram, NN)
        real = one[:8, :128] + one[8:, 128:]
        imag = one[8:, :128] - one[:8, 128:]
        return jnp.concatenate([real, imag], axis=0)

    total = first + (first - by_gram(first))
    rest = first - by_gram(total)

    def inner(left, right):
        one = dot_high(left, right, NT)
        return one[:8, :8] + one[8:, 8:], one[:8, 8:] - one[8:, :8]

    one_real, one_imag = inner(first, total)
    two_real, two_imag = inner(total, rest)
    block_ref[0] = sums[16:24, 0:8] - one_real - two_real
    block_ref[1] = sums[16:24, 8:16] - one_imag - two_imag
    high, middle, low = split3(complex_rows(total))
    three = jnp.concatenate([high, middle, low], axis=0)
    two = three[:32]
    for step, copy in enumerate(copies):
        copy.wait()
        here = slice(step * width, (step + 1) * width)
        b_high, b_middle, b_low = split3(stacked(held_ref[:, :, :, here]))
        one = dot_nn(three, b_high)
        taken = one[:16] + one[16:32] + one[32:]
        one = dot_nn(two, b_middle)
        taken += one[:16] + one[16:]
        taken += dot_nn(high, b_low)
        new_ref[:, :, here] = (image_ref[:, here] - taken).reshape(2, 8, width)
    turn = jnp.where(row == lax.rem(column, 16) * 8 + lax.div(column, 16), 1.0, 0.0)
    turned = dot_high(total, turn, NN)
    for angle in range(8):
        total_ref[0, angle] = turned[:8, angle * 16 : (angle + 1) * 16]
        total_ref[1, angle] = turned[8:, angle * 16 : (angle + 1) * 16]


def finish(scale, got, image, krylov_basis):
    return pl.pallas_call(
        lambda *refs: finish_kernel(scale, *refs),
        grid=(1,),
        in_specs=[whole(got.shape), whole(image.shape), pl.BlockSpec(memory_space=pltpu.HBM)],
        out_specs=[whole((2, 8, 8, 16)), whole((2, 8, 4096)), whole((2, 8, 8))],
        out_shape=[
            jax.ShapeDtypeStruct((2, 8, 8, 16), jnp.float32),
            jax.ShapeDtypeStruct((2, 8, 4096), jnp.float32),
            jax.ShapeDtypeStruct((2, 8, 8), jnp.float32),
        ],
        scratch_shapes=[pltpu.VMEM((128, 128), jnp.float32)] + basis_scratch(krylov_basis),
        compiler_params=pltpu.CompilerParams(vmem_limit_bytes=KERNEL_VMEM),
        cost_estimate=pl.CostEstimate(
            flops=6 * 16 * 256 * 4096 * 2, bytes_accessed=6 << 20, transcendentals=0
        ),
    )(got, image, in_hbm(krylov_basis))


def exchange(value, axis, bit_number):
    pairs = [(source, source ^ (1 << bit_number)) for source in range(lax.axis_size(axis))]
    return lax.ppermute(value, axis, pairs)


def per_device(
    krylov_basis, near_field, leaf_in, leaf_out, level_mixers, block_ranks, partner_tables
):
    src_bits = lax.axis_size("src").bit_length() - 1
    obs_bits = lax.axis_size("obs").bit_length() - 1
    plan = [
        ("src", src_bits - 1),
        ("src", src_bits - 2),
        ("obs", obs_bits - 1),
        ("obs", obs_bits - 2),
        ("obs", obs_bits - 3),
    ]
    coeffs = apply_leaves(krylov_basis, leaf_in, 4)
    close = apply_leaves(krylov_basis, near_field, 4)
    gram = basis_gram(krylov_basis)
    gram = (gram + exchange(gram, "src", 0)).reshape(8, 16, 128)
    for level, (axis, bit) in enumerate(plan):
        partner = exchange(coeffs, axis, bit)
        operands = (level, coeffs, partner, level_mixers, block_ranks, partner_tables)
        if level == 0:
            coeffs = next_level(*operands, gram)
        elif level < len(plan) - 1:
            coeffs = next_level(*operands)
        else:
            image, sums = project(*operands, close, leaf_out, krylov_basis)
    got = relay(lax.all_to_all(sums, "src", 0, 0))
    got = lax.all_to_all(got, "obs", 0, 0)
    devices = lax.axis_size("src") * lax.axis_size("obs")
    scale = 1.0 / (krylov_basis.shape[3] * devices)
    total, new_block, block_gram = finish(scale, got, image, krylov_basis)
    return jnp.transpose(total, (3, 0, 1, 2)), new_block, block_gram


def solution(mesh):
    in_specs = (
        P(None, None, None, ("src", "obs")),
        P(None, ("src", "obs"), None, None),
        P(None, ("src", "obs"), None, None),
        P(None, ("src", "obs"), None, None),
        P(None, None, None, None, ("src", "obs")),
        P(None, ("src", "obs")),
        P(None, ("src", "obs"), None),
    )
    out_specs = (P(), P(None, None, ("src", "obs")), P())
    return jax.shard_map(
        per_device, mesh=mesh, in_specs=in_specs, out_specs=out_specs, check_vma=False
    )
```

```python
import jax
import jax.numpy as jnp
from jax import lax
from jax.experimental import pallas as pl
from jax.experimental.pallas import tpu as pltpu
from jax.sharding import PartitionSpec as P

NT = (((1,), (1,)), ((), ()))
NN = (((1,), (0,)), ((), ()))
KERNEL_VMEM = 24 * 1024 * 1024
VMEM = pl.BlockSpec(memory_space=pltpu.VMEM)
BASIS_PARTS = 4


def in_hbm(value):
    return pltpu.with_memory_space_constraint(value, pltpu.HBM)


def dot_nt(left, right):
    return lax.dot_general(left, right, NT, preferred_element_type=jnp.float32)


def dot_nn(left, right):
    return lax.dot_general(left, right, NN, preferred_element_type=jnp.float32)


def split3(value):
    high = value.astype(jnp.bfloat16)
    rest = value - high.astype(jnp.float32)
    middle = rest.astype(jnp.bfloat16)
    low = (rest - middle.astype(jnp.float32)).astype(jnp.bfloat16)
    return high, middle, low


def split2(value):
    high = value.astype(jnp.bfloat16)
    return high, (value - high.astype(jnp.float32)).astype(jnp.bfloat16)


def complex_rows(rows):
    real, imag = rows[:8], rows[8:]
    return jnp.concatenate(
        [jnp.concatenate([real, -imag], axis=1), jnp.concatenate([imag, real], axis=1)], axis=0
    )


def leaf_product(rows, real, imag):
    return dot_nt(
        complex_rows(rows).astype(jnp.bfloat16), jnp.concatenate([real, imag], axis=1)
    )


def leaves_kernel(basis_ref, leaf_ref, out_ref, newest_ref, held_ref, newest_sem, held_sems):
    steps = held_sems.shape[0]
    count = held_ref.shape[1]
    part = count // steps
    newest_copy = pltpu.make_async_copy(
        basis_ref.at[basis_ref.shape[0] - 1], newest_ref, newest_sem
    )
    newest_copy.start()
    copies = []
    for step in range(steps):
        here = pl.ds(step * part, part)
        copies.append(
            pltpu.make_async_copy(leaf_ref.at[:, here], held_ref.at[:, here], held_sems.at[step])
        )
        copies[-1].start()
    newest_copy.wait()
    for leaf in range(count):
        if leaf % part == 0:
            copies[leaf // part].wait()
        rows = newest_ref[:, :, leaf * 128 : (leaf + 1) * 128].reshape(16, 128)
        rows = rows.astype(jnp.bfloat16).astype(jnp.float32)
        out_ref[leaf] = leaf_product(rows, held_ref[0, leaf], held_ref[1, leaf])


def apply_leaves(krylov_basis, leaves, steps):
    count = leaves.shape[1]
    return pl.pallas_call(
        leaves_kernel,
        in_specs=[pl.BlockSpec(memory_space=pltpu.HBM)] * 2,
        out_specs=pl.BlockSpec(memory_space=pltpu.VMEM),
        out_shape=jax.ShapeDtypeStruct((count, 16, 128), jnp.float32),
        scratch_shapes=[
            pltpu.VMEM(krylov_basis.shape[1:], jnp.float32),
            pltpu.VMEM(leaves.shape, leaves.dtype),
            pltpu.SemaphoreType.DMA,
            pltpu.SemaphoreType.DMA((steps,)),
        ],
        compiler_params=pltpu.CompilerParams(vmem_limit_bytes=KERNEL_VMEM),
        cost_estimate=pl.CostEstimate(
            flops=count * 16 * 256 * 128 * 2, bytes_accessed=count * 73728, transcendentals=0
        ),
    )(in_hbm(krylov_basis), in_hbm(leaves))


def stacked(basis):
    width = basis.shape[3]
    return jnp.concatenate(
        [basis[:, 0].reshape(128, width), basis[:, 1].reshape(128, width)], axis=0
    )


def basis_gram_kernel(basis_ref, out_ref, high_ref, middle_ref, low_ref, held_ref, sems):
    steps = sems.shape[0]
    width = held_ref.shape[3] // steps
    copies = []
    for step in range(steps):
        here = pl.ds(step * width, width)
        copies.append(
            pltpu.make_async_copy(
                basis_ref.at[:, :, :, here], held_ref.at[:, :, :, here], sems.at[step]
            )
        )
        copies[-1].start()
    even = jnp.zeros((256, 256), jnp.float32)
    odd = jnp.zeros((256, 256), jnp.float32)
    for step, copy in enumerate(copies):
        copy.wait()
        here = slice(step * width, (step + 1) * width)
        high, middle, low = split3(stacked(held_ref[:, :, :, here]))
        high_ref[:, here] = high
        middle_ref[:, here] = middle
        low_ref[:, here] = low
        even += dot_nt(high, high) + dot_nt(middle, middle)
        odd += dot_nt(high, middle) + dot_nt(high, low)
    gram = even + odd + odd.T
    real = gram[:128, :128] + gram[128:, 128:]
    imag = gram[:128, 128:] - gram[128:, :128]
    row = lax.broadcasted_iota(jnp.int32, (128, 128), 0)
    column = lax.broadcasted_iota(jnp.int32, (128, 128), 1)
    out_ref[...] = jnp.where(row <= column, real, imag)


def basis_gram(krylov_basis):
    part = jax.ShapeDtypeStruct((256, krylov_basis.shape[3]), jnp.bfloat16)
    gram, *parts = pl.pallas_call(
        basis_gram_kernel,
        in_specs=[pl.BlockSpec(memory_space=pltpu.HBM)],
        out_specs=[VMEM] * 4,
        out_shape=[jax.ShapeDtypeStruct((128, 128), jnp.float32), part, part, part],
        scratch_shapes=[
            pltpu.VMEM(krylov_basis.shape, jnp.float32),
            pltpu.SemaphoreType.DMA((BASIS_PARTS,)),
        ],
        compiler_params=pltpu.CompilerParams(vmem_limit_bytes=KERNEL_VMEM),
        cost_estimate=pl.CostEstimate(
            flops=4 * 2 * 256 * 256 * 4096, bytes_accessed=10 << 20, transcendentals=0
        ),
    )(in_hbm(krylov_basis))
    return gram, parts


def mix(level, own_ref, partner_ref, mixer_ref, rank_ref, table_ref):
    table = table_ref[level]
    picked = jnp.concatenate([partner_ref[table[0, leaf]] for leaf in range(32)], axis=0)
    both = jnp.concatenate([own_ref[...].reshape(512, 128), picked], axis=1)
    weights = jnp.concatenate(
        [
            jnp.concatenate([mixer_ref[level, 0, 0], mixer_ref[level, 0, 1]], axis=1),
            jnp.concatenate([mixer_ref[level, 1, 0], mixer_ref[level, 1, 1]], axis=1),
        ],
        axis=0,
    )
    high, low = split2(both)
    w_high, w_low = split2(weights)
    product = dot_nn(high, w_high) + dot_nn(high, w_low) + dot_nn(low, w_high)
    column = lax.broadcasted_iota(jnp.int32, (16, 128), 1)
    ranks = rank_ref[level : level + 1]

    def leaf_value(leaf):
        by_real = product[leaf * 16 : (leaf + 1) * 16, :128]
        by_imag = product[leaf * 16 : (leaf + 1) * 16, 128:]
        mixed = jnp.concatenate([by_real[:8] - by_imag[8:], by_real[8:] + by_imag[:8]], axis=0)
        return jnp.where(column < ranks[0, leaf], mixed, 0.0)

    return leaf_value


def level_kernel(level, own_ref, partner_ref, mixer_ref, rank_ref, table_ref, *refs):
    out_ref = refs[-1]
    leaf_value = mix(level, own_ref, partner_ref, mixer_ref, rank_ref, table_ref)
    for leaf in range(32):
        out_ref[leaf] = leaf_value(leaf)


def next_level(level, own, partner, level_mixers, block_ranks, partner_tables, before):
    return pl.pallas_call(
        lambda *refs: level_kernel(level, *refs),
        in_specs=[VMEM] * 5 + [pl.BlockSpec(memory_space=pl.ANY)] * len(before),
        out_specs=VMEM,
        out_shape=jax.ShapeDtypeStruct((32, 16, 128), jnp.float32),
        compiler_params=pltpu.CompilerParams(vmem_limit_bytes=KERNEL_VMEM),
        cost_estimate=pl.CostEstimate(
            flops=3 * 512 * 256 * 256 * 2, bytes_accessed=1 << 20, transcendentals=0
        ),
    )(own, partner, level_mixers, block_ranks, partner_tables, *before)


def project_kernel(
    level, own_ref, partner_ref, mixer_ref, rank_ref, table_ref, close_ref, leaf_ref,
    high_ref, middle_ref, low_ref, before_ref, image_ref, sums_ref,
):
    leaf_value = mix(level, own_ref, partner_ref, mixer_ref, rank_ref, table_ref)
    for leaf in range(32):
        rounded = leaf_value(leaf).astype(jnp.bfloat16).astype(jnp.float32)
        far = leaf_product(rounded, leaf_ref[0, leaf], leaf_ref[1, leaf])
        image_ref[:, leaf * 128 : (leaf + 1) * 128] = far + close_ref[leaf]
    high, middle, low = split3(image_ref[...])
    three = jnp.concatenate([high, middle, low], axis=0)
    two = three[:32]

    def product(first, second, third):
        one = dot_nt(three, first)
        result = one[:16] + one[16:32] + one[32:]
        one = dot_nt(two, second)
        return result + one[:16] + one[16:] + dot_nt(high, third)

    inner = product(high_ref[...], middle_ref[...], low_ref[...])
    square = product(high, middle, low)
    first = jnp.concatenate(
        [inner[:8, :128] + inner[8:, 128:], inner[8:, :128] - inner[:8, 128:]], axis=0
    )
    real = square[:8, :8] + square[8:, 8:]
    imag = square[:8, 8:] - square[8:, :8]
    pieces = [real[row : row + 1] for row in range(8)] + [imag[row : row + 1] for row in range(8)]
    last = jnp.concatenate(pieces, axis=1)
    for device in range(8):
        sums_ref[device, 0:16, 0] = first
        sums_ref[device, 16] = last


def project(
    level, own, partner, level_mixers, block_ranks, partner_tables, close, leaf_out, parts, before
):
    return pl.pallas_call(
        lambda *refs: project_kernel(level, *refs),
        in_specs=[VMEM] * 10 + [pl.BlockSpec(memory_space=pl.ANY)],
        out_specs=[VMEM] * 2,
        out_shape=[
            jax.ShapeDtypeStruct((16, 4096), jnp.float32),
            jax.ShapeDtypeStruct((8, 17, 1, 128), jnp.float32),
        ],
        compiler_params=pltpu.CompilerParams(vmem_limit_bytes=KERNEL_VMEM),
        cost_estimate=pl.CostEstimate(
            flops=6 * 512 * 256 * 256 * 2, bytes_accessed=8 << 20, transcendentals=0
        ),
    )(own, partner, level_mixers, block_ranks, partner_tables, close, leaf_out, *parts, before)


def relay_kernel(got_ref, before_ref, out_ref):
    sums = jnp.sum(got_ref[...], axis=0)
    for device in range(32):
        out_ref[device] = sums


def relay(got, before):
    return pl.pallas_call(
        relay_kernel,
        in_specs=[VMEM, pl.BlockSpec(memory_space=pl.ANY)],
        out_specs=VMEM,
        out_shape=jax.ShapeDtypeStruct((32, 17, 1, 128), jnp.float32),
        compiler_params=pltpu.CompilerParams(vmem_limit_bytes=KERNEL_VMEM),
    )(got, before)


def dot_high(left, right, numbers):
    return lax.dot_general(
        left, right, numbers, precision=lax.Precision.HIGHEST, preferred_element_type=jnp.float32
    )


def finish_kernel(
    scale, got_ref, gram_ref, image_ref, high_ref, middle_ref, low_ref, total_ref, new_ref, block_ref
):
    sums = jnp.concatenate(
        [jnp.sum(got_ref[:, row, 0], axis=0, keepdims=True) for row in range(17)], axis=0
    )
    sums = sums * scale
    first = sums[:16]
    packed = gram_ref[...] * scale
    row = lax.broadcasted_iota(jnp.int32, (128, 128), 0)
    column = lax.broadcasted_iota(jnp.int32, (128, 128), 1)
    flipped = packed.T
    gram_real = jnp.where(row <= column, packed, flipped)
    gram_imag = jnp.where(row > column, packed, jnp.where(row < column, -flipped, 0.0))
    gram = jnp.concatenate([gram_real, gram_imag], axis=1)

    def by_gram(rows):
        one = dot_high(rows, gram, NN)
        real = one[:8, :128] + one[8:, 128:]
        imag = one[8:, :128] - one[:8, 128:]
        return jnp.concatenate([real, imag], axis=0)

    total = first + (first - by_gram(first))
    rest = first - by_gram(total)

    def inner(left, right):
        one = dot_high(left, right, NT)
        return one[:8, :8] + one[8:, 8:], one[:8, 8:] - one[8:, :8]

    one_real, one_imag = inner(first, total)
    two_real, two_imag = inner(total, rest)
    taken_real, taken_imag = one_real + two_real, one_imag + two_imag
    for angle in range(8):
        at = angle * 8
        block_ref[0, angle] = sums[16, at : at + 8] - taken_real[angle]
        block_ref[1, angle] = sums[16, 64 + at : 72 + at] - taken_imag[angle]
    high, middle, low = split3(complex_rows(total))
    three = jnp.concatenate([high, middle, low], axis=0)
    two = three[:32]
    width = 1024
    for start in range(0, 4096, width):
        here = slice(start, start + width)
        one = dot_nn(three, high_ref[:, here])
        taken = one[:16] + one[16:32] + one[32:]
        one = dot_nn(two, middle_ref[:, here])
        taken += one[:16] + one[16:]
        taken += dot_nn(high, low_ref[:, here])
        new_ref[:, :, here] = (image_ref[:, here] - taken).reshape(2, 8, width)
    turn = jnp.where(row == lax.rem(column, 16) * 8 + lax.div(column, 16), 1.0, 0.0)
    turned = dot_high(total, turn, NN)
    for angle in range(8):
        total_ref[0, angle] = turned[:8, angle * 16 : (angle + 1) * 16]
        total_ref[1, angle] = turned[8:, angle * 16 : (angle + 1) * 16]


def finish(scale, got, gram, image, parts):
    return pl.pallas_call(
        lambda *refs: finish_kernel(scale, *refs),
        in_specs=[VMEM] * 6,
        out_specs=[VMEM] * 3,
        out_shape=[
            jax.ShapeDtypeStruct((2, 8, 8, 16), jnp.float32),
            jax.ShapeDtypeStruct((2, 8, 4096), jnp.float32),
            jax.ShapeDtypeStruct((2, 8, 8), jnp.float32),
        ],
        compiler_params=pltpu.CompilerParams(vmem_limit_bytes=KERNEL_VMEM),
        cost_estimate=pl.CostEstimate(
            flops=6 * 16 * 256 * 4096 * 2, bytes_accessed=6 << 20, transcendentals=0
        ),
    )(got, gram, image, *parts)


def add_kernel(left_ref, right_ref, before_ref, out_ref):
    out_ref[...] = left_ref[...] + right_ref[...]


def add_after(left, right, before):
    return pl.pallas_call(
        add_kernel,
        in_specs=[VMEM, VMEM, pl.BlockSpec(memory_space=pl.ANY)],
        out_specs=VMEM,
        out_shape=jax.ShapeDtypeStruct(left.shape, left.dtype),
        compiler_params=pltpu.CompilerParams(vmem_limit_bytes=KERNEL_VMEM),
    )(left, right, before)


def exchange(value, axis, bit_number):
    pairs = [(source, source ^ (1 << bit_number)) for source in range(lax.axis_size(axis))]
    return lax.ppermute(value, axis, pairs)


def per_device(
    krylov_basis, near_field, leaf_in, leaf_out, level_mixers, block_ranks, partner_tables
):
    src_bits = lax.axis_size("src").bit_length() - 1
    obs_bits = lax.axis_size("obs").bit_length() - 1
    plan = [
        ("src", src_bits - 1),
        ("src", src_bits - 2),
        ("obs", obs_bits - 1),
        ("obs", obs_bits - 2),
        ("obs", obs_bits - 3),
    ]
    coeffs = apply_leaves(krylov_basis, leaf_in, 4)
    close = apply_leaves(krylov_basis, near_field, 4)
    gram, parts = basis_gram(krylov_basis)
    beside = [
        [("src", 0)],
        [("obs", obs_bits - 1)],
        [("obs", 1)],
        [("src", src_bits - 1)],
        [("obs", 2), ("obs", 0)],
        [("obs", obs_bits - 2)],
        [("src", 1)],
    ]

    def sum_on(gram, step, before=None):
        for axis, bit in beside[step][:-1]:
            gram = gram + exchange(gram, axis, bit)
        got = exchange(gram, *beside[step][-1])
        return gram + got if before is None else add_after(gram, got, before)

    for level, (axis, bit) in enumerate(plan):
        partner = exchange(coeffs, axis, bit)
        operands = (level, coeffs, partner, level_mixers, block_ranks, partner_tables)
        if level < len(plan) - 1:
            gram = sum_on(gram, level)
            coeffs = next_level(*operands, [gram, close] if level == 2 else [gram])
        else:
            gram = sum_on(gram, level, partner)
            image, sums = project(*operands, close, leaf_out, parts, gram)
    gram = sum_on(gram, 5, image)
    got = lax.all_to_all(sums, "src", 0, 0)
    gram = sum_on(gram, 6)
    got = relay(got, gram)
    got = lax.all_to_all(got, "obs", 0, 0)
    devices = lax.axis_size("src") * lax.axis_size("obs")
    scale = 1.0 / (krylov_basis.shape[3] * devices)
    total, new_block, block_gram = finish(scale, got, gram, image, parts)
    return jnp.transpose(total, (3, 0, 1, 2)), new_block, block_gram


def solution(mesh):
    in_specs = (
        P(None, None, None, ("src", "obs")),
        P(None, ("src", "obs"), None, None),
        P(None, ("src", "obs"), None, None),
        P(None, ("src", "obs"), None, None),
        P(None, None, None, None, ("src", "obs")),
        P(None, ("src", "obs")),
        P(None, ("src", "obs"), None),
    )
    out_specs = (P(), P(None, None, ("src", "obs")), P())
    return jax.shard_map(
        per_device, mesh=mesh, in_specs=in_specs, out_specs=out_specs, check_vma=False
    )
```

```python
import jax
import jax.numpy as jnp
from jax import lax
from jax.experimental import pallas as pl
from jax.experimental.pallas import tpu as pltpu
from jax.sharding import Mesh
from jax.sharding import PartitionSpec as P

NT = (((1,), (1,)), ((), ()))
NN = (((1,), (0,)), ((), ()))
KERNEL_VMEM = 24 * 1024 * 1024
VMEM = pl.BlockSpec(memory_space=pltpu.VMEM)
BASIS_PARTS = 4
AXES = ("y", "core", "x", "z")


def in_hbm(value):
    return pltpu.with_memory_space_constraint(value, pltpu.HBM)


def dot_nt(left, right):
    return lax.dot_general(left, right, NT, preferred_element_type=jnp.float32)


def dot_nn(left, right):
    return lax.dot_general(left, right, NN, preferred_element_type=jnp.float32)


def split3(value):
    high = value.astype(jnp.bfloat16)
    rest = value - high.astype(jnp.float32)
    middle = rest.astype(jnp.bfloat16)
    low = (rest - middle.astype(jnp.float32)).astype(jnp.bfloat16)
    return high, middle, low


def split2(value):
    high = value.astype(jnp.bfloat16)
    return high, (value - high.astype(jnp.float32)).astype(jnp.bfloat16)


def complex_rows(rows):
    real, imag = rows[:8], rows[8:]
    return jnp.concatenate(
        [jnp.concatenate([real, -imag], axis=1), jnp.concatenate([imag, real], axis=1)], axis=0
    )


def leaf_product(rows, real, imag):
    return dot_nt(
        complex_rows(rows).astype(jnp.bfloat16), jnp.concatenate([real, imag], axis=1)
    )


def leaves_in_kernel(
    basis_ref, leaf_ref, out_ref, rows_ref, newest_ref, held_ref, newest_sem, held_sems
):
    steps = held_sems.shape[0]
    count = held_ref.shape[1]
    part = count // steps
    newest_copy = pltpu.make_async_copy(
        basis_ref.at[basis_ref.shape[0] - 1], newest_ref, newest_sem
    )
    newest_copy.start()
    copies = []
    for step in range(steps):
        here = pl.ds(step * part, part)
        copies.append(
            pltpu.make_async_copy(leaf_ref.at[:, here], held_ref.at[:, here], held_sems.at[step])
        )
        copies[-1].start()
    newest_copy.wait()
    for leaf in range(count):
        if leaf % part == 0:
            copies[leaf // part].wait()
        rows = newest_ref[:, :, leaf * 128 : (leaf + 1) * 128].reshape(16, 128)
        rows = rows.astype(jnp.bfloat16).astype(jnp.float32)
        rows_ref[leaf] = rows
        out_ref[leaf] = leaf_product(rows, held_ref[0, leaf], held_ref[1, leaf])


def leaves_in(krylov_basis, leaves, steps):
    count = leaves.shape[1]
    rows = jax.ShapeDtypeStruct((count, 16, 128), jnp.float32)
    return pl.pallas_call(
        leaves_in_kernel,
        in_specs=[pl.BlockSpec(memory_space=pltpu.HBM)] * 2,
        out_specs=[VMEM] * 2,
        out_shape=[rows, rows],
        scratch_shapes=[
            pltpu.VMEM(krylov_basis.shape[1:], jnp.float32),
            pltpu.VMEM(leaves.shape, leaves.dtype),
            pltpu.SemaphoreType.DMA,
            pltpu.SemaphoreType.DMA((steps,)),
        ],
        compiler_params=pltpu.CompilerParams(vmem_limit_bytes=KERNEL_VMEM),
        cost_estimate=pl.CostEstimate(
            flops=count * 16 * 256 * 128 * 2, bytes_accessed=count * 73728, transcendentals=0
        ),
    )(in_hbm(krylov_basis), in_hbm(leaves))


def near_kernel(rows_ref, leaf_ref, out_ref):
    for leaf in range(rows_ref.shape[0]):
        out_ref[leaf] = leaf_product(rows_ref[leaf], leaf_ref[0, leaf], leaf_ref[1, leaf])


def near_product(rows, near_field):
    return pl.pallas_call(
        near_kernel,
        in_specs=[VMEM] * 2,
        out_specs=VMEM,
        out_shape=jax.ShapeDtypeStruct(rows.shape, jnp.float32),
        compiler_params=pltpu.CompilerParams(vmem_limit_bytes=KERNEL_VMEM),
        cost_estimate=pl.CostEstimate(
            flops=rows.shape[0] * 16 * 256 * 128 * 2, bytes_accessed=2 << 20, transcendentals=0
        ),
    )(rows, near_field)


def stacked(basis):
    width = basis.shape[3]
    return jnp.concatenate(
        [basis[:, 0].reshape(128, width), basis[:, 1].reshape(128, width)], axis=0
    )


def basis_gram_kernel(basis_ref, out_ref, high_ref, middle_ref, low_ref, held_ref, sems):
    steps = sems.shape[0]
    width = held_ref.shape[3] // steps
    copies = []
    for step in range(steps):
        here = pl.ds(step * width, width)
        copies.append(
            pltpu.make_async_copy(
                basis_ref.at[:, :, :, here], held_ref.at[:, :, :, here], sems.at[step]
            )
        )
        copies[-1].start()
    even = jnp.zeros((256, 256), jnp.float32)
    odd = jnp.zeros((256, 256), jnp.float32)
    for step, copy in enumerate(copies):
        copy.wait()
        here = slice(step * width, (step + 1) * width)
        high, middle, low = split3(stacked(held_ref[:, :, :, here]))
        high_ref[:, here] = high
        middle_ref[:, here] = middle
        low_ref[:, here] = low
        even += dot_nt(high, high) + dot_nt(middle, middle)
        odd += dot_nt(high, middle) + dot_nt(high, low)
    gram = even + odd + odd.T
    real = gram[:128, :128] + gram[128:, 128:]
    imag = gram[:128, 128:] - gram[128:, :128]
    row = lax.broadcasted_iota(jnp.int32, (128, 128), 0)
    column = lax.broadcasted_iota(jnp.int32, (128, 128), 1)
    out_ref[...] = jnp.where(row <= column, real, imag)


def basis_gram(krylov_basis):
    part = jax.ShapeDtypeStruct((256, krylov_basis.shape[3]), jnp.bfloat16)
    gram, *parts = pl.pallas_call(
        basis_gram_kernel,
        in_specs=[pl.BlockSpec(memory_space=pltpu.HBM)],
        out_specs=[VMEM] * 4,
        out_shape=[jax.ShapeDtypeStruct((128, 128), jnp.float32), part, part, part],
        scratch_shapes=[
            pltpu.VMEM(krylov_basis.shape, jnp.float32),
            pltpu.SemaphoreType.DMA((BASIS_PARTS,)),
        ],
        compiler_params=pltpu.CompilerParams(vmem_limit_bytes=KERNEL_VMEM),
        cost_estimate=pl.CostEstimate(
            flops=4 * 2 * 256 * 256 * 4096, bytes_accessed=10 << 20, transcendentals=0
        ),
    )(in_hbm(krylov_basis))
    return gram, parts


def mix(level, own_ref, partner_ref, mixer_ref, rank_ref, table_ref):
    table = table_ref[level]
    picked = jnp.concatenate([partner_ref[table[0, leaf]] for leaf in range(32)], axis=0)
    both = jnp.concatenate([own_ref[...].reshape(512, 128), picked], axis=1)
    weights = jnp.concatenate(
        [
            jnp.concatenate([mixer_ref[level, 0, 0], mixer_ref[level, 0, 1]], axis=1),
            jnp.concatenate([mixer_ref[level, 1, 0], mixer_ref[level, 1, 1]], axis=1),
        ],
        axis=0,
    )
    high, low = split2(both)
    w_high, w_low = split2(weights)
    product = dot_nn(high, w_high) + dot_nn(high, w_low) + dot_nn(low, w_high)
    column = lax.broadcasted_iota(jnp.int32, (16, 128), 1)
    ranks = rank_ref[level : level + 1]

    def leaf_value(leaf):
        by_real = product[leaf * 16 : (leaf + 1) * 16, :128]
        by_imag = product[leaf * 16 : (leaf + 1) * 16, 128:]
        mixed = jnp.concatenate([by_real[:8] - by_imag[8:], by_real[8:] + by_imag[:8]], axis=0)
        return jnp.where(column < ranks[0, leaf], mixed, 0.0)

    return leaf_value


def level_kernel(level, own_ref, partner_ref, mixer_ref, rank_ref, table_ref, *refs):
    out_ref = refs[-1]
    leaf_value = mix(level, own_ref, partner_ref, mixer_ref, rank_ref, table_ref)
    for leaf in range(32):
        out_ref[leaf] = leaf_value(leaf)


def next_level(level, own, partner, level_mixers, block_ranks, partner_tables, before):
    return pl.pallas_call(
        lambda *refs: level_kernel(level, *refs),
        in_specs=[VMEM] * 5 + [pl.BlockSpec(memory_space=pl.ANY)] * len(before),
        out_specs=VMEM,
        out_shape=jax.ShapeDtypeStruct((32, 16, 128), jnp.float32),
        compiler_params=pltpu.CompilerParams(vmem_limit_bytes=KERNEL_VMEM),
        cost_estimate=pl.CostEstimate(
            flops=3 * 512 * 256 * 256 * 2, bytes_accessed=1 << 20, transcendentals=0
        ),
    )(own, partner, level_mixers, block_ranks, partner_tables, *before)


def project_kernel(
    level, own_ref, partner_ref, mixer_ref, rank_ref, table_ref, close_ref, leaf_ref,
    high_ref, middle_ref, low_ref, before_ref, image_ref, sums_ref,
):
    leaf_value = mix(level, own_ref, partner_ref, mixer_ref, rank_ref, table_ref)
    for leaf in range(32):
        rounded = leaf_value(leaf).astype(jnp.bfloat16).astype(jnp.float32)
        far = leaf_product(rounded, leaf_ref[0, leaf], leaf_ref[1, leaf])
        image_ref[:, leaf * 128 : (leaf + 1) * 128] = far + close_ref[leaf]
    high, middle, low = split3(image_ref[...])
    three = jnp.concatenate([high, middle, low], axis=0)
    two = three[:32]

    def product(first, second, third):
        one = dot_nt(three, first)
        result = one[:16] + one[16:32] + one[32:]
        one = dot_nt(two, second)
        return result + one[:16] + one[16:] + dot_nt(high, third)

    inner = product(high_ref[...], middle_ref[...], low_ref[...])
    square = product(high, middle, low)
    first = jnp.concatenate(
        [inner[:8, :128] + inner[8:, 128:], inner[8:, :128] - inner[:8, 128:]], axis=0
    )
    real = square[:8, :8] + square[8:, 8:]
    imag = square[:8, 8:] - square[8:, :8]
    sums_ref[0:16] = first
    sums_ref[16:24] = jnp.concatenate([real, imag, jnp.zeros((8, 112), jnp.float32)], axis=1)


def project(
    level, own, partner, level_mixers, block_ranks, partner_tables, close, leaf_out, parts, before
):
    return pl.pallas_call(
        lambda *refs: project_kernel(level, *refs),
        in_specs=[VMEM] * 10 + [pl.BlockSpec(memory_space=pl.ANY)],
        out_specs=[VMEM] * 2,
        out_shape=[
            jax.ShapeDtypeStruct((16, 4096), jnp.float32),
            jax.ShapeDtypeStruct((24, 128), jnp.float32),
        ],
        compiler_params=pltpu.CompilerParams(vmem_limit_bytes=KERNEL_VMEM),
        cost_estimate=pl.CostEstimate(
            flops=6 * 512 * 256 * 256 * 2, bytes_accessed=8 << 20, transcendentals=0
        ),
    )(own, partner, level_mixers, block_ranks, partner_tables, close, leaf_out, *parts, before)


def dot_high(left, right, numbers):
    return lax.dot_general(
        left, right, numbers, precision=lax.Precision.HIGHEST, preferred_element_type=jnp.float32
    )


def finish_kernel(
    scale, got_ref, gram_ref, image_ref, high_ref, middle_ref, low_ref, total_ref, new_ref, block_ref
):
    sums = jnp.sum(got_ref[...], axis=0) * scale
    first = sums[:16]
    packed = gram_ref[...] * scale
    row = lax.broadcasted_iota(jnp.int32, (128, 128), 0)
    column = lax.broadcasted_iota(jnp.int32, (128, 128), 1)
    flipped = packed.T
    gram_real = jnp.where(row <= column, packed, flipped)
    gram_imag = jnp.where(row > column, packed, jnp.where(row < column, -flipped, 0.0))
    gram = jnp.concatenate([gram_real, gram_imag], axis=1)

    def by_gram(rows):
        one = dot_high(rows, gram, NN)
        real = one[:8, :128] + one[8:, 128:]
        imag = one[8:, :128] - one[:8, 128:]
        return jnp.concatenate([real, imag], axis=0)

    total = first + (first - by_gram(first))
    rest = first - by_gram(total)

    def inner(left, right):
        one = dot_high(left, right, NT)
        return one[:8, :8] + one[8:, 8:], one[:8, 8:] - one[8:, :8]

    one_real, one_imag = inner(first, total)
    two_real, two_imag = inner(total, rest)
    block_ref[0] = sums[16:24, 0:8] - one_real - two_real
    block_ref[1] = sums[16:24, 8:16] - one_imag - two_imag
    high, middle, low = split3(complex_rows(total))
    three = jnp.concatenate([high, middle, low], axis=0)
    two = three[:32]
    width = 1024
    for start in range(0, 4096, width):
        here = slice(start, start + width)
        one = dot_nn(three, high_ref[:, here])
        taken = one[:16] + one[16:32] + one[32:]
        one = dot_nn(two, middle_ref[:, here])
        taken += one[:16] + one[16:]
        taken += dot_nn(high, low_ref[:, here])
        new_ref[:, :, here] = (image_ref[:, here] - taken).reshape(2, 8, width)
    turn = jnp.where(row == lax.rem(column, 16) * 8 + lax.div(column, 16), 1.0, 0.0)
    turned = dot_high(total, turn, NN)
    for angle in range(8):
        total_ref[0, angle] = turned[:8, angle * 16 : (angle + 1) * 16]
        total_ref[1, angle] = turned[8:, angle * 16 : (angle + 1) * 16]


def finish(scale, got, gram, image, parts):
    return pl.pallas_call(
        lambda *refs: finish_kernel(scale, *refs),
        in_specs=[VMEM] * 6,
        out_specs=[VMEM] * 3,
        out_shape=[
            jax.ShapeDtypeStruct((2, 8, 8, 16), jnp.float32),
            jax.ShapeDtypeStruct((2, 8, 4096), jnp.float32),
            jax.ShapeDtypeStruct((2, 8, 8), jnp.float32),
        ],
        compiler_params=pltpu.CompilerParams(vmem_limit_bytes=KERNEL_VMEM),
        cost_estimate=pl.CostEstimate(
            flops=6 * 16 * 256 * 4096 * 2, bytes_accessed=6 << 20, transcendentals=0
        ),
    )(got, gram, image, *parts)


def add_kernel(left_ref, right_ref, before_ref, out_ref):
    out_ref[...] = left_ref[...] + right_ref[...]


def add_after(left, right, before):
    return pl.pallas_call(
        add_kernel,
        in_specs=[VMEM, VMEM, pl.BlockSpec(memory_space=pl.ANY)],
        out_specs=VMEM,
        out_shape=jax.ShapeDtypeStruct(left.shape, left.dtype),
        compiler_params=pltpu.CompilerParams(vmem_limit_bytes=KERNEL_VMEM),
    )(left, right, before)


def exchange(value, axis, bit_number):
    pairs = [(source, source ^ (1 << bit_number)) for source in range(lax.axis_size(axis))]
    return lax.ppermute(value, axis, pairs)


def sum_of_all(value, axes):
    copies = jnp.broadcast_to(value[None], (lax.axis_size(axes),) + value.shape)
    return jnp.sum(lax.all_to_all(copies, axes, 0, 0), axis=0)


def per_device(
    krylov_basis, near_field, leaf_in, leaf_out, level_mixers, block_ranks, partner_tables
):
    plan = [("y", 1), ("y", 0), ("x", 1), ("x", 0), ("z", 2)]
    beside = [[("core", 0)], [("z", 1)], [("z", 2)], [("y", 1)], [("x", 1), ("x", 0), ("y", 0)]]
    coeffs, rows = leaves_in(krylov_basis, leaf_in, 4)
    gram, parts = basis_gram(krylov_basis)
    close = near_product(rows, near_field)
    for level, (axis, bit) in enumerate(plan):
        partner = exchange(coeffs, axis, bit)
        for gram_axis, gram_bit in beside[level][:-1]:
            gram = gram + exchange(gram, gram_axis, gram_bit)
        got = exchange(gram, *beside[level][-1])
        operands = (level, coeffs, partner, level_mixers, block_ranks, partner_tables)
        if level < len(plan) - 1:
            gram = gram + got
            coeffs = next_level(*operands, [gram, close] if level == 1 else [gram])
        else:
            gram = add_after(gram, got, partner)
            image, sums = project(*operands, close, leaf_out, parts, gram)
    gram = add_after(gram, exchange(gram, "z", 0), image)
    sums = add_after(sums, exchange(sums, "core", 0), gram)
    sums = sum_of_all(sums, ("y", "x"))
    copies = jnp.broadcast_to(sums[None], (lax.axis_size("z"),) + sums.shape)
    got = lax.all_to_all(copies, "z", 0, 0)
    devices = lax.axis_size(AXES)
    scale = 1.0 / (krylov_basis.shape[3] * devices)
    total, new_block, block_gram = finish(scale, got, gram, image, parts)
    return jnp.transpose(total, (3, 0, 1, 2)), new_block, block_gram


def solution(mesh):
    mesh = Mesh(mesh.devices.reshape(4, 2, 4, 8), AXES)
    in_specs = (
        P(None, None, None, AXES),
        P(None, AXES, None, None),
        P(None, AXES, None, None),
        P(None, AXES, None, None),
        P(None, None, None, None, AXES),
        P(None, AXES),
        P(None, AXES, None),
    )
    out_specs = (P(), P(None, None, AXES), P())
    return jax.shard_map(
        per_device, mesh=mesh, in_specs=in_specs, out_specs=out_specs, check_vma=False
    )
```

```python
import jax
import jax.numpy as jnp
from jax import lax
from jax.experimental import pallas as pl
from jax.experimental.pallas import tpu as pltpu
from jax.sharding import Mesh
from jax.sharding import PartitionSpec as P

NT = (((1,), (1,)), ((), ()))
NN = (((1,), (0,)), ((), ()))
KERNEL_VMEM = 24 * 1024 * 1024
VMEM = pl.BlockSpec(memory_space=pltpu.VMEM)
ANYWHERE = pl.BlockSpec(memory_space=pl.ANY)
BASIS_PARTS = 4
AXES = ("y", "core", "x", "z")


def in_hbm(value):
    return pltpu.with_memory_space_constraint(value, pltpu.HBM)


def in_vmem(value):
    return pltpu.with_memory_space_constraint(value, pltpu.VMEM)


def dot_nt(left, right):
    return lax.dot_general(left, right, NT, preferred_element_type=jnp.float32)


def dot_nn(left, right):
    return lax.dot_general(left, right, NN, preferred_element_type=jnp.float32)


def split2(value):
    high = value.astype(jnp.bfloat16)
    return high, (value - high.astype(jnp.float32)).astype(jnp.bfloat16)


def complex_rows(rows):
    real, imag = rows[:8], rows[8:]
    return jnp.concatenate(
        [jnp.concatenate([real, -imag], axis=1), jnp.concatenate([imag, real], axis=1)], axis=0
    )


def leaf_product(rows, real, imag):
    return dot_nt(
        complex_rows(rows).astype(jnp.bfloat16), jnp.concatenate([real, imag], axis=1)
    )


def leaves_in_kernel(
    basis_ref, leaf_ref, out_ref, rows_ref, newest_ref, held_ref, newest_sem, held_sems
):
    steps = held_sems.shape[0]
    count = held_ref.shape[1]
    part = count // steps
    newest_copy = pltpu.make_async_copy(
        basis_ref.at[basis_ref.shape[0] - 1], newest_ref, newest_sem
    )
    newest_copy.start()
    copies = []
    for step in range(steps):
        here = pl.ds(step * part, part)
        copies.append(
            pltpu.make_async_copy(leaf_ref.at[:, here], held_ref.at[:, here], held_sems.at[step])
        )
        copies[-1].start()
    newest_copy.wait()
    for leaf in range(count):
        if leaf % part == 0:
            copies[leaf // part].wait()
        rows = newest_ref[:, :, leaf * 128 : (leaf + 1) * 128].reshape(16, 128)
        rows = rows.astype(jnp.bfloat16).astype(jnp.float32)
        rows_ref[leaf] = rows
        out_ref[leaf] = leaf_product(rows, held_ref[0, leaf], held_ref[1, leaf])


def leaves_in(krylov_basis, leaves, steps):
    count = leaves.shape[1]
    rows = jax.ShapeDtypeStruct((count, 16, 128), jnp.float32)
    return pl.pallas_call(
        leaves_in_kernel,
        in_specs=[pl.BlockSpec(memory_space=pltpu.HBM)] * 2,
        out_specs=[VMEM] * 2,
        out_shape=[rows, rows],
        scratch_shapes=[
            pltpu.VMEM(krylov_basis.shape[1:], jnp.float32),
            pltpu.VMEM(leaves.shape, leaves.dtype),
            pltpu.SemaphoreType.DMA,
            pltpu.SemaphoreType.DMA((steps,)),
        ],
        compiler_params=pltpu.CompilerParams(vmem_limit_bytes=KERNEL_VMEM),
        cost_estimate=pl.CostEstimate(
            flops=count * 16 * 256 * 128 * 2, bytes_accessed=count * 73728, transcendentals=0
        ),
    )(in_hbm(krylov_basis), in_hbm(leaves))


def near_kernel(rows_ref, leaf_ref, out_ref):
    for leaf in range(rows_ref.shape[0]):
        out_ref[leaf] = leaf_product(rows_ref[leaf], leaf_ref[0, leaf], leaf_ref[1, leaf])


def near_product(rows, near_field):
    return pl.pallas_call(
        near_kernel,
        in_specs=[VMEM] * 2,
        out_specs=VMEM,
        out_shape=jax.ShapeDtypeStruct(rows.shape, jnp.float32),
        compiler_params=pltpu.CompilerParams(vmem_limit_bytes=KERNEL_VMEM),
        cost_estimate=pl.CostEstimate(
            flops=rows.shape[0] * 16 * 256 * 128 * 2, bytes_accessed=2 << 20, transcendentals=0
        ),
    )(rows, near_field)


def stacked(basis):
    width = basis.shape[3]
    return jnp.concatenate(
        [basis[:, 0].reshape(128, width), basis[:, 1].reshape(128, width)], axis=0
    )


def basis_gram_kernel(basis_ref, out_ref, high_ref, low_ref, held_ref, sems):
    steps = sems.shape[0]
    width = held_ref.shape[3] // steps
    copies = []
    for step in range(steps):
        here = pl.ds(step * width, width)
        copies.append(
            pltpu.make_async_copy(
                basis_ref.at[:, :, :, here], held_ref.at[:, :, :, here], sems.at[step]
            )
        )
        copies[-1].start()
    even = jnp.zeros((256, 256), jnp.float32)
    odd = jnp.zeros((256, 256), jnp.float32)
    for step, copy in enumerate(copies):
        copy.wait()
        here = slice(step * width, (step + 1) * width)
        high, low = split2(stacked(held_ref[:, :, :, here]))
        high_ref[:, here] = high
        low_ref[:, here] = low
        even += dot_nt(high, high)
        odd += dot_nt(high, low)
    gram = even + odd + odd.T
    real = gram[:128, :128] + gram[128:, 128:]
    imag = gram[:128, 128:] - gram[128:, :128]
    row = lax.broadcasted_iota(jnp.int32, (128, 128), 0)
    column = lax.broadcasted_iota(jnp.int32, (128, 128), 1)
    out_ref[...] = jnp.where(row <= column, real, imag)


def basis_gram(krylov_basis):
    part = pltpu.VMEM((256, krylov_basis.shape[3]), jnp.bfloat16)
    gram, *parts = pl.pallas_call(
        basis_gram_kernel,
        in_specs=[pl.BlockSpec(memory_space=pltpu.HBM)],
        out_specs=[VMEM] * 3,
        out_shape=[jax.ShapeDtypeStruct((128, 128), jnp.float32), part, part],
        scratch_shapes=[
            pltpu.VMEM(krylov_basis.shape, jnp.float32),
            pltpu.SemaphoreType.DMA((BASIS_PARTS,)),
        ],
        compiler_params=pltpu.CompilerParams(vmem_limit_bytes=KERNEL_VMEM),
        cost_estimate=pl.CostEstimate(
            flops=2 * 2 * 256 * 256 * 4096, bytes_accessed=8 << 20, transcendentals=0
        ),
    )(in_hbm(krylov_basis))
    return gram, parts


def mix(level, own_ref, partner_ref, mixer_ref, rank_ref, table_ref):
    table = table_ref[level]
    picked = jnp.concatenate([partner_ref[table[0, leaf]] for leaf in range(32)], axis=0)
    both = jnp.concatenate([own_ref[0:32].reshape(512, 128), picked], axis=1)
    weights = jnp.concatenate(
        [
            jnp.concatenate([mixer_ref[level, 0, 0], mixer_ref[level, 0, 1]], axis=1),
            jnp.concatenate([mixer_ref[level, 1, 0], mixer_ref[level, 1, 1]], axis=1),
        ],
        axis=0,
    )
    high, low = split2(both)
    w_high, w_low = split2(weights)
    product = dot_nn(high, w_high) + dot_nn(high, w_low) + dot_nn(low, w_high)
    column = lax.broadcasted_iota(jnp.int32, (16, 128), 1)
    ranks = rank_ref[level : level + 1]

    def leaf_value(leaf):
        by_real = product[leaf * 16 : (leaf + 1) * 16, :128]
        by_imag = product[leaf * 16 : (leaf + 1) * 16, 128:]
        mixed = jnp.concatenate([by_real[:8] - by_imag[8:], by_real[8:] + by_imag[:8]], axis=0)
        return jnp.where(column < ranks[0, leaf], mixed, 0.0)

    return leaf_value


def level_kernel(level, gram_rows, own_ref, partner_ref, mixer_ref, rank_ref, table_ref, gram_ref, *refs):
    out_ref = refs[-1]
    leaf_value = mix(level, own_ref, partner_ref, mixer_ref, rank_ref, table_ref)
    for leaf in range(32):
        out_ref[leaf] = leaf_value(leaf)
    if gram_rows:
        out_ref[32:40] = gram_ref[...].reshape(8, 16, 128)


def next_level(level, own, partner, level_mixers, block_ranks, partner_tables, gram, with_gram):
    return pl.pallas_call(
        lambda *refs: level_kernel(level, with_gram, *refs),
        in_specs=[VMEM] * 5 + [VMEM if with_gram else ANYWHERE],
        out_specs=VMEM,
        out_shape=jax.ShapeDtypeStruct((40 if with_gram else 32, 16, 128), jnp.float32),
        compiler_params=pltpu.CompilerParams(vmem_limit_bytes=KERNEL_VMEM),
        cost_estimate=pl.CostEstimate(
            flops=3 * 512 * 256 * 256 * 2, bytes_accessed=1 << 20, transcendentals=0
        ),
    )(own, partner, level_mixers, block_ranks, partner_tables, gram)


def project_kernel(
    level, own_ref, partner_ref, mixer_ref, rank_ref, table_ref, close_ref, leaf_ref,
    high_ref, low_ref, image_ref, sums_ref, gram_ref,
):
    leaf_value = mix(level, own_ref, partner_ref, mixer_ref, rank_ref, table_ref)
    for leaf in range(32):
        rounded = leaf_value(leaf).astype(jnp.bfloat16).astype(jnp.float32)
        far = leaf_product(rounded, leaf_ref[0, leaf], leaf_ref[1, leaf])
        image_ref[:, leaf * 128 : (leaf + 1) * 128] = far + close_ref[leaf]
    high, low = split2(image_ref[...])
    two = jnp.concatenate([high, low], axis=0)

    def product(first, second):
        one = dot_nt(two, first)
        return one[:16] + one[16:] + dot_nt(high, second)

    inner = product(high_ref[...], low_ref[...])
    square = product(high, low)
    sums_ref[0:8] = inner[:8, :128] + inner[8:, 128:]
    sums_ref[8:16] = inner[8:, :128] - inner[:8, 128:]
    real = square[:8, :8] + square[8:, 8:]
    imag = square[:8, 8:] - square[8:, :8]
    sums_ref[16:24] = jnp.concatenate([real, imag, jnp.zeros((8, 112), jnp.float32)], axis=1)
    gram_ref[...] = (own_ref[32:40] + partner_ref[32:40]).reshape(128, 128)


def project(level, own, partner, level_mixers, block_ranks, partner_tables, close, leaf_out, parts):
    return pl.pallas_call(
        lambda *refs: project_kernel(level, *refs),
        in_specs=[VMEM] * 9,
        out_specs=[VMEM] * 3,
        out_shape=[
            jax.ShapeDtypeStruct((16, 4096), jnp.float32),
            jax.ShapeDtypeStruct((24, 128), jnp.float32),
            jax.ShapeDtypeStruct((128, 128), jnp.float32),
        ],
        compiler_params=pltpu.CompilerParams(vmem_limit_bytes=KERNEL_VMEM),
        cost_estimate=pl.CostEstimate(
            flops=6 * 512 * 256 * 256 * 2, bytes_accessed=8 << 20, transcendentals=0
        ),
    )(
        own, partner, level_mixers, block_ranks, partner_tables, close, leaf_out,
        *[in_vmem(part) for part in parts],
    )


def merge_kernel(own_ref, other_ref, gram_ref, out_ref):
    sums = own_ref[...] + other_ref[...]
    mine = lax.axis_index("y")
    piece = gram_ref[pl.ds(pl.multiple_of(mine * 32, 32), 32), :]
    for device in range(out_ref.shape[0]):
        out_ref[device, 0:24] = sums
        out_ref[device, 24:56] = piece


def merge(own, other, gram):
    return pl.pallas_call(
        merge_kernel,
        in_specs=[VMEM] * 3,
        out_specs=VMEM,
        out_shape=jax.ShapeDtypeStruct((lax.axis_size(("y", "x")), 56, 128), jnp.float32),
        compiler_params=pltpu.CompilerParams(vmem_limit_bytes=KERNEL_VMEM),
    )(own, other, gram)


def relay_kernel(got_ref, out_ref, gram_ref):
    sums = jnp.sum(got_ref[:, 0:24], axis=0)
    for device in range(out_ref.shape[0]):
        out_ref[device] = sums
    for quarter in range(4):
        gram_ref[quarter * 32 : (quarter + 1) * 32] = jnp.sum(
            got_ref[quarter * 4 : quarter * 4 + 4, 24:56], axis=0
        )


def relay(got):
    return pl.pallas_call(
        relay_kernel,
        in_specs=[VMEM],
        out_specs=[VMEM] * 2,
        out_shape=[
            jax.ShapeDtypeStruct((lax.axis_size("z"), 24, 128), jnp.float32),
            jax.ShapeDtypeStruct((128, 128), jnp.float32),
        ],
        compiler_params=pltpu.CompilerParams(vmem_limit_bytes=KERNEL_VMEM),
    )(got)


def dot_high(left, right, numbers):
    return lax.dot_general(
        left, right, numbers, precision=lax.Precision.HIGHEST, preferred_element_type=jnp.float32
    )


def finish_kernel(
    scale, got_ref, gram_ref, image_ref, high_ref, low_ref, total_ref, new_ref, block_ref
):
    sums = jnp.sum(got_ref[...], axis=0) * scale
    first = sums[:16]
    packed = gram_ref[...] * scale
    row = lax.broadcasted_iota(jnp.int32, (128, 128), 0)
    column = lax.broadcasted_iota(jnp.int32, (128, 128), 1)
    flipped = packed.T
    gram_real = jnp.where(row <= column, packed, flipped)
    gram_imag = jnp.where(row > column, packed, jnp.where(row < column, -flipped, 0.0))
    gram = jnp.concatenate([gram_real, gram_imag], axis=1)

    def by_gram(rows):
        one = dot_high(rows, gram, NN)
        real = one[:8, :128] + one[8:, 128:]
        imag = one[8:, :128] - one[:8, 128:]
        return jnp.concatenate([real, imag], axis=0)

    total = first + (first - by_gram(first))
    rest = first - by_gram(total)

    def inner(left, right):
        one = dot_high(left, right, NT)
        return one[:8, :8] + one[8:, 8:], one[:8, 8:] - one[8:, :8]

    one_real, one_imag = inner(first, total)
    two_real, two_imag = inner(total, rest)
    block_ref[0] = sums[16:24, 0:8] - one_real - two_real
    block_ref[1] = sums[16:24, 8:16] - one_imag - two_imag
    high, low = split2(complex_rows(total))
    two = jnp.concatenate([high, low], axis=0)
    width = 1024
    for start in range(0, 4096, width):
        here = slice(start, start + width)
        one = dot_nn(two, high_ref[:, here])
        taken = one[:16] + one[16:] + dot_nn(high, low_ref[:, here])
        new_ref[:, :, here] = (image_ref[:, here] - taken).reshape(2, 8, width)
    turn = jnp.where(row == lax.rem(column, 16) * 8 + lax.div(column, 16), 1.0, 0.0)
    turned = dot_high(total, turn, NN)
    for angle in range(8):
        total_ref[0, angle] = turned[:8, angle * 16 : (angle + 1) * 16]
        total_ref[1, angle] = turned[8:, angle * 16 : (angle + 1) * 16]


def finish(scale, got, gram, image, parts):
    return pl.pallas_call(
        lambda *refs: finish_kernel(scale, *refs),
        in_specs=[VMEM] * 5,
        out_specs=[VMEM] * 3,
        out_shape=[
            jax.ShapeDtypeStruct((2, 8, 8, 16), jnp.float32),
            jax.ShapeDtypeStruct((2, 8, 4096), jnp.float32),
            jax.ShapeDtypeStruct((2, 8, 8), jnp.float32),
        ],
        compiler_params=pltpu.CompilerParams(vmem_limit_bytes=KERNEL_VMEM),
        cost_estimate=pl.CostEstimate(
            flops=6 * 16 * 256 * 4096 * 2, bytes_accessed=6 << 20, transcendentals=0
        ),
    )(got, gram, image, *[in_vmem(part) for part in parts])


def exchange(value, axis, bit_number):
    pairs = [(source, source ^ (1 << bit_number)) for source in range(lax.axis_size(axis))]
    return lax.ppermute(value, axis, pairs)


def per_device(
    krylov_basis, near_field, leaf_in, leaf_out, level_mixers, block_ranks, partner_tables
):
    plan = [("y", 1), ("y", 0), ("x", 1), ("x", 0), ("z", 2)]
    beside = [[("z", 0)], [("z", 1)], [("y", 0), ("core", 0)], [("y", 1)]]
    coeffs, rows = leaves_in(krylov_basis, leaf_in, 4)
    gram, parts = basis_gram(krylov_basis)
    close = near_product(rows, near_field)
    for level, (axis, bit) in enumerate(plan):
        partner = exchange(coeffs, axis, bit)
        operands = (level, coeffs, partner, level_mixers, block_ranks, partner_tables)
        if level < len(plan) - 1:
            for gram_axis, gram_bit in beside[level]:
                gram = gram + exchange(gram, gram_axis, gram_bit)
            coeffs = next_level(*operands, gram, level == len(plan) - 2)
        else:
            image, sums, gram = project(*operands, close, leaf_out, parts)
    got = merge(sums, exchange(sums, "core", 0), gram)
    got, gram = relay(lax.all_to_all(got, ("y", "x"), 0, 0))
    got = lax.all_to_all(got, "z", 0, 0)
    scale = 1.0 / (krylov_basis.shape[3] * lax.axis_size(AXES))
    total, new_block, block_gram = finish(scale, got, gram, image, parts)
    return jnp.transpose(total, (3, 0, 1, 2)), new_block, block_gram


def solution(mesh):
    mesh = Mesh(mesh.devices.reshape(4, 2, 4, 8), AXES)
    in_specs = (
        P(None, None, None, AXES),
        P(None, AXES, None, None),
        P(None, AXES, None, None),
        P(None, AXES, None, None),
        P(None, None, None, None, AXES),
        P(None, AXES),
        P(None, AXES, None),
    )
    out_specs = (P(), P(None, None, AXES), P())
    return jax.shard_map(
        per_device, mesh=mesh, in_specs=in_specs, out_specs=out_specs, check_vma=False
    )
```

```python
import jax
import jax.numpy as jnp
from jax import lax
from jax.experimental import pallas as pl
from jax.experimental.pallas import tpu as pltpu
from jax.sharding import Mesh
from jax.sharding import PartitionSpec as P

NT = (((1,), (1,)), ((), ()))
NN = (((1,), (0,)), ((), ()))
KERNEL_VMEM = 24 * 1024 * 1024
VMEM = pl.BlockSpec(memory_space=pltpu.VMEM)
ANYWHERE = pl.BlockSpec(memory_space=pl.ANY)
BASIS_PARTS = 4
AXES = ("y", "core", "x", "z")


def in_hbm(value):
    return pltpu.with_memory_space_constraint(value, pltpu.HBM)


def in_vmem(value):
    return pltpu.with_memory_space_constraint(value, pltpu.VMEM)


def dot_nt(left, right):
    return lax.dot_general(left, right, NT, preferred_element_type=jnp.float32)


def dot_nn(left, right):
    return lax.dot_general(left, right, NN, preferred_element_type=jnp.float32)


def split2(value):
    high = value.astype(jnp.bfloat16)
    return high, (value - high.astype(jnp.float32)).astype(jnp.bfloat16)


def complex_rows(rows):
    real, imag = rows[:8], rows[8:]
    return jnp.concatenate(
        [jnp.concatenate([real, -imag], axis=1), jnp.concatenate([imag, real], axis=1)], axis=0
    )


def leaf_product(rows, real, imag):
    return dot_nt(
        complex_rows(rows).astype(jnp.bfloat16), jnp.concatenate([real, imag], axis=1)
    )


def leaves_in_kernel(
    basis_ref, leaf_ref, out_ref, rows_ref, newest_ref, held_ref, newest_sem, held_sems
):
    steps = held_sems.shape[0]
    count = held_ref.shape[1]
    part = count // steps
    newest_copy = pltpu.make_async_copy(
        basis_ref.at[basis_ref.shape[0] - 1], newest_ref, newest_sem
    )
    newest_copy.start()
    copies = []
    for step in range(steps):
        here = pl.ds(step * part, part)
        copies.append(
            pltpu.make_async_copy(leaf_ref.at[:, here], held_ref.at[:, here], held_sems.at[step])
        )
        copies[-1].start()
    newest_copy.wait()
    for leaf in range(count):
        if leaf % part == 0:
            copies[leaf // part].wait()
        rows = newest_ref[:, :, leaf * 128 : (leaf + 1) * 128].reshape(16, 128)
        rows = rows.astype(jnp.bfloat16).astype(jnp.float32)
        rows_ref[leaf] = rows
        out_ref[leaf] = leaf_product(rows, held_ref[0, leaf], held_ref[1, leaf])


def leaves_in(krylov_basis, leaves, steps):
    count = leaves.shape[1]
    rows = jax.ShapeDtypeStruct((count, 16, 128), jnp.float32)
    return pl.pallas_call(
        leaves_in_kernel,
        in_specs=[pl.BlockSpec(memory_space=pltpu.HBM)] * 2,
        out_specs=[VMEM] * 2,
        out_shape=[rows, rows],
        scratch_shapes=[
            pltpu.VMEM(krylov_basis.shape[1:], jnp.float32),
            pltpu.VMEM(leaves.shape, leaves.dtype),
            pltpu.SemaphoreType.DMA,
            pltpu.SemaphoreType.DMA((steps,)),
        ],
        compiler_params=pltpu.CompilerParams(vmem_limit_bytes=KERNEL_VMEM),
        cost_estimate=pl.CostEstimate(
            flops=count * 16 * 256 * 128 * 2, bytes_accessed=count * 73728, transcendentals=0
        ),
    )(in_hbm(krylov_basis), in_hbm(leaves))


def near_kernel(rows_ref, leaf_ref, out_ref):
    for leaf in range(rows_ref.shape[0]):
        out_ref[leaf] = leaf_product(rows_ref[leaf], leaf_ref[0, leaf], leaf_ref[1, leaf])


def near_product(rows, near_field):
    return pl.pallas_call(
        near_kernel,
        in_specs=[VMEM] * 2,
        out_specs=VMEM,
        out_shape=jax.ShapeDtypeStruct(rows.shape, jnp.float32),
        compiler_params=pltpu.CompilerParams(vmem_limit_bytes=KERNEL_VMEM),
        cost_estimate=pl.CostEstimate(
            flops=rows.shape[0] * 16 * 256 * 128 * 2, bytes_accessed=2 << 20, transcendentals=0
        ),
    )(rows, near_field)


def stacked(basis):
    width = basis.shape[3]
    return jnp.concatenate(
        [basis[:, 0].reshape(128, width), basis[:, 1].reshape(128, width)], axis=0
    )


def basis_gram_kernel(basis_ref, out_ref, high_ref, low_ref, held_ref, sems):
    steps = sems.shape[0]
    width = held_ref.shape[3] // steps
    copies = []
    for step in range(steps):
        here = pl.ds(step * width, width)
        copies.append(
            pltpu.make_async_copy(
                basis_ref.at[:, :, :, here], held_ref.at[:, :, :, here], sems.at[step]
            )
        )
        copies[-1].start()
    even = jnp.zeros((256, 256), jnp.float32)
    odd = jnp.zeros((256, 256), jnp.float32)
    for step, copy in enumerate(copies):
        copy.wait()
        here = slice(step * width, (step + 1) * width)
        high, low = split2(stacked(held_ref[:, :, :, here]))
        high_ref[:, here] = high
        low_ref[:, here] = low
        even += dot_nt(high, high)
        odd += dot_nt(high, low)
    gram = even + odd + odd.T
    real = gram[:128, :128] + gram[128:, 128:]
    imag = gram[:128, 128:] - gram[128:, :128]
    row = lax.broadcasted_iota(jnp.int32, (128, 128), 0)
    column = lax.broadcasted_iota(jnp.int32, (128, 128), 1)
    out_ref[...] = jnp.where(row <= column, real, imag)


def basis_gram(krylov_basis):
    part = pltpu.VMEM((256, krylov_basis.shape[3]), jnp.bfloat16)
    gram, *parts = pl.pallas_call(
        basis_gram_kernel,
        in_specs=[pl.BlockSpec(memory_space=pltpu.HBM)],
        out_specs=[VMEM] * 3,
        out_shape=[jax.ShapeDtypeStruct((128, 128), jnp.float32), part, part],
        scratch_shapes=[
            pltpu.VMEM(krylov_basis.shape, jnp.float32),
            pltpu.SemaphoreType.DMA((BASIS_PARTS,)),
        ],
        compiler_params=pltpu.CompilerParams(vmem_limit_bytes=KERNEL_VMEM),
        cost_estimate=pl.CostEstimate(
            flops=2 * 2 * 256 * 256 * 4096, bytes_accessed=8 << 20, transcendentals=0
        ),
    )(in_hbm(krylov_basis))
    return gram, parts


def mix(level, own_ref, partner_ref, mixer_ref, rank_ref, table_ref):
    table = table_ref[level]
    picked = jnp.concatenate([partner_ref[table[0, leaf]] for leaf in range(32)], axis=0)
    both = jnp.concatenate([own_ref[...].reshape(512, 128), picked], axis=1)
    weights = jnp.concatenate(
        [
            jnp.concatenate([mixer_ref[level, 0, 0], mixer_ref[level, 0, 1]], axis=1),
            jnp.concatenate([mixer_ref[level, 1, 0], mixer_ref[level, 1, 1]], axis=1),
        ],
        axis=0,
    )
    high, low = split2(both)
    w_high, w_low = split2(weights)
    product = dot_nn(high, w_high) + dot_nn(high, w_low) + dot_nn(low, w_high)
    column = lax.broadcasted_iota(jnp.int32, (16, 128), 1)
    ranks = rank_ref[level : level + 1]

    def leaf_value(leaf):
        by_real = product[leaf * 16 : (leaf + 1) * 16, :128]
        by_imag = product[leaf * 16 : (leaf + 1) * 16, 128:]
        mixed = jnp.concatenate([by_real[:8] - by_imag[8:], by_real[8:] + by_imag[:8]], axis=0)
        return jnp.where(column < ranks[0, leaf], mixed, 0.0)

    return leaf_value


def level_kernel(level, own_ref, partner_ref, mixer_ref, rank_ref, table_ref, gram_ref, out_ref):
    leaf_value = mix(level, own_ref, partner_ref, mixer_ref, rank_ref, table_ref)
    for leaf in range(32):
        out_ref[leaf] = leaf_value(leaf)


def next_level(level, own, partner, level_mixers, block_ranks, partner_tables, gram):
    return pl.pallas_call(
        lambda *refs: level_kernel(level, *refs),
        in_specs=[VMEM] * 5 + [ANYWHERE],
        out_specs=VMEM,
        out_shape=jax.ShapeDtypeStruct(own.shape, jnp.float32),
        compiler_params=pltpu.CompilerParams(vmem_limit_bytes=KERNEL_VMEM),
        cost_estimate=pl.CostEstimate(
            flops=3 * 512 * 256 * 256 * 2, bytes_accessed=1 << 20, transcendentals=0
        ),
    )(own, partner, level_mixers, block_ranks, partner_tables, gram)


def project_kernel(
    level, own_ref, partner_ref, mixer_ref, rank_ref, table_ref, close_ref, leaf_ref,
    high_ref, low_ref, before_ref, image_ref, sums_ref,
):
    leaf_value = mix(level, own_ref, partner_ref, mixer_ref, rank_ref, table_ref)
    for leaf in range(32):
        rounded = leaf_value(leaf).astype(jnp.bfloat16).astype(jnp.float32)
        far = leaf_product(rounded, leaf_ref[0, leaf], leaf_ref[1, leaf])
        image_ref[:, leaf * 128 : (leaf + 1) * 128] = far + close_ref[leaf]
    high, low = split2(image_ref[...])
    two = jnp.concatenate([high, low], axis=0)

    def product(first, second):
        one = dot_nt(two, first)
        return one[:16] + one[16:] + dot_nt(high, second)

    inner = product(high_ref[...], low_ref[...])
    square = product(high, low)
    sums_ref[0:8] = inner[:8, :128] + inner[8:, 128:]
    sums_ref[8:16] = inner[8:, :128] - inner[:8, 128:]
    real = square[:8, :8] + square[8:, 8:]
    imag = square[:8, 8:] - square[8:, :8]
    sums_ref[16:24] = jnp.concatenate([real, imag, jnp.zeros((8, 112), jnp.float32)], axis=1)


def project(level, own, partner, level_mixers, block_ranks, partner_tables, close, leaf_out, parts, gram):
    return pl.pallas_call(
        lambda *refs: project_kernel(level, *refs),
        in_specs=[VMEM] * 9 + [ANYWHERE],
        out_specs=[VMEM] * 2,
        out_shape=[
            jax.ShapeDtypeStruct((16, 4096), jnp.float32),
            jax.ShapeDtypeStruct((24, 128), jnp.float32),
        ],
        compiler_params=pltpu.CompilerParams(vmem_limit_bytes=KERNEL_VMEM),
        cost_estimate=pl.CostEstimate(
            flops=6 * 512 * 256 * 256 * 2, bytes_accessed=8 << 20, transcendentals=0
        ),
    )(
        own, partner, level_mixers, block_ranks, partner_tables, close, leaf_out,
        *[in_vmem(part) for part in parts], gram,
    )


def merge_kernel(own_ref, other_ref, gram_ref, other_gram_ref, out_ref, gram_sum_ref):
    sums = own_ref[...] + other_ref[...]
    gram_sum_ref[...] = gram_ref[...] + other_gram_ref[...]
    mine = lax.axis_index("y") * 2 + lax.rem(lax.axis_index("x"), 2)
    piece = gram_sum_ref[pl.ds(pl.multiple_of(mine * 16, 16), 16), :]
    for device in range(out_ref.shape[0]):
        out_ref[device, 0:24] = sums
        out_ref[device, 24:40] = piece


def merge(own, other, gram, other_gram):
    return pl.pallas_call(
        merge_kernel,
        in_specs=[VMEM] * 4,
        out_specs=VMEM,
        out_shape=jax.ShapeDtypeStruct((lax.axis_size(("y", "x")), 40, 128), jnp.float32),
        scratch_shapes=[pltpu.VMEM((128, 128), jnp.float32)],
        compiler_params=pltpu.CompilerParams(vmem_limit_bytes=KERNEL_VMEM),
    )(own, other, gram, other_gram)


def relay_kernel(got_ref, out_ref, gram_ref):
    sums = jnp.sum(got_ref[:, 0:24], axis=0)
    for piece in range(8):
        at = piece // 2 * 4 + piece % 2
        gram_ref[piece * 16 : (piece + 1) * 16] = got_ref[at, 24:40] + got_ref[at + 2, 24:40]
    mine = lax.rem(lax.axis_index("z"), 4)
    piece = gram_ref[pl.ds(pl.multiple_of(mine * 32, 32), 32), :]
    for device in range(out_ref.shape[0]):
        out_ref[device, 0:24] = sums
        out_ref[device, 24:56] = piece


def relay(got):
    return pl.pallas_call(
        relay_kernel,
        in_specs=[VMEM],
        out_specs=VMEM,
        out_shape=jax.ShapeDtypeStruct((lax.axis_size("z"), 56, 128), jnp.float32),
        scratch_shapes=[pltpu.VMEM((128, 128), jnp.float32)],
        compiler_params=pltpu.CompilerParams(vmem_limit_bytes=KERNEL_VMEM),
    )(got)


def dot_high(left, right, numbers):
    return lax.dot_general(
        left, right, numbers, precision=lax.Precision.HIGHEST, preferred_element_type=jnp.float32
    )


def finish_kernel(
    scale, got_ref, image_ref, high_ref, low_ref, total_ref, new_ref, block_ref, gram_ref
):
    sums = jnp.sum(got_ref[:, 0:24], axis=0) * scale
    for piece in range(4):
        gram_ref[piece * 32 : (piece + 1) * 32] = got_ref[piece, 24:56] + got_ref[piece + 4, 24:56]
    first = sums[:16]
    packed = gram_ref[...] * scale
    row = lax.broadcasted_iota(jnp.int32, (128, 128), 0)
    column = lax.broadcasted_iota(jnp.int32, (128, 128), 1)
    flipped = packed.T
    gram_real = jnp.where(row <= column, packed, flipped)
    gram_imag = jnp.where(row > column, packed, jnp.where(row < column, -flipped, 0.0))
    gram = jnp.concatenate([gram_real, gram_imag], axis=1)

    def by_gram(rows):
        one = dot_high(rows, gram, NN)
        real = one[:8, :128] + one[8:, 128:]
        imag = one[8:, :128] - one[:8, 128:]
        return jnp.concatenate([real, imag], axis=0)

    total = first + (first - by_gram(first))
    rest = first - by_gram(total)

    def inner(left, right):
        one = dot_high(left, right, NT)
        return one[:8, :8] + one[8:, 8:], one[:8, 8:] - one[8:, :8]

    one_real, one_imag = inner(first, total)
    two_real, two_imag = inner(total, rest)
    block_ref[0] = sums[16:24, 0:8] - one_real - two_real
    block_ref[1] = sums[16:24, 8:16] - one_imag - two_imag
    high, low = split2(complex_rows(total))
    two = jnp.concatenate([high, low], axis=0)
    width = 1024
    for start in range(0, 4096, width):
        here = slice(start, start + width)
        one = dot_nn(two, high_ref[:, here])
        taken = one[:16] + one[16:] + dot_nn(high, low_ref[:, here])
        new_ref[:, :, here] = (image_ref[:, here] - taken).reshape(2, 8, width)
    turn = jnp.where(row == lax.rem(column, 16) * 8 + lax.div(column, 16), 1.0, 0.0)
    turned = dot_high(total, turn, NN)
    for angle in range(8):
        total_ref[0, angle] = turned[:8, angle * 16 : (angle + 1) * 16]
        total_ref[1, angle] = turned[8:, angle * 16 : (angle + 1) * 16]


def finish(scale, got, image, parts):
    return pl.pallas_call(
        lambda *refs: finish_kernel(scale, *refs),
        in_specs=[VMEM] * 4,
        out_specs=[VMEM] * 3,
        out_shape=[
            jax.ShapeDtypeStruct((2, 8, 8, 16), jnp.float32),
            jax.ShapeDtypeStruct((2, 8, 4096), jnp.float32),
            jax.ShapeDtypeStruct((2, 8, 8), jnp.float32),
        ],
        scratch_shapes=[pltpu.VMEM((128, 128), jnp.float32)],
        compiler_params=pltpu.CompilerParams(vmem_limit_bytes=KERNEL_VMEM),
        cost_estimate=pl.CostEstimate(
            flops=6 * 16 * 256 * 4096 * 2, bytes_accessed=6 << 20, transcendentals=0
        ),
    )(got, image, *[in_vmem(part) for part in parts])


def exchange(value, axis, bit_number):
    pairs = [(source, source ^ (1 << bit_number)) for source in range(lax.axis_size(axis))]
    return lax.ppermute(value, axis, pairs)


def per_device(
    krylov_basis, near_field, leaf_in, leaf_out, level_mixers, block_ranks, partner_tables
):
    plan = [("y", 1), ("y", 0), ("x", 1), ("x", 0), ("z", 2)]
    beside = [("core", 0), ("z", 1), ("y", 0), ("y", 1), ("x", 0)]
    coeffs, rows = leaves_in(krylov_basis, leaf_in, 4)
    gram, parts = basis_gram(krylov_basis)
    close = near_product(rows, near_field)
    for level, (axis, bit) in enumerate(plan):
        partner = exchange(coeffs, axis, bit)
        gram = gram + exchange(gram, *beside[level])
        operands = (level, coeffs, partner, level_mixers, block_ranks, partner_tables)
        if level < len(plan) - 1:
            coeffs = next_level(*operands, gram)
        else:
            image, sums = project(*operands, close, leaf_out, parts, gram)
    got = merge(sums, exchange(sums, "core", 0), gram, exchange(gram, "z", 0))
    got = relay(lax.all_to_all(got, ("y", "x"), 0, 0))
    got = lax.all_to_all(got, "z", 0, 0)
    scale = 1.0 / (krylov_basis.shape[3] * lax.axis_size(AXES))
    total, new_block, block_gram = finish(scale, got, image, parts)
    return jnp.transpose(total, (3, 0, 1, 2)), new_block, block_gram


def solution(mesh):
    mesh = Mesh(mesh.devices.reshape(4, 2, 4, 8), AXES)
    in_specs = (
        P(None, None, None, AXES),
        P(None, AXES, None, None),
        P(None, AXES, None, None),
        P(None, AXES, None, None),
        P(None, None, None, None, AXES),
        P(None, AXES),
        P(None, AXES, None),
    )
    out_specs = (P(), P(None, None, AXES), P())
    return jax.shard_map(
        per_device, mesh=mesh, in_specs=in_specs, out_specs=out_specs, check_vma=False
    )
```

```python
import jax
import jax.numpy as jnp
from jax import lax
from jax.experimental import pallas as pl
from jax.experimental.pallas import tpu as pltpu
from jax.sharding import Mesh
from jax.sharding import PartitionSpec as P

NT = (((1,), (1,)), ((), ()))
NN = (((1,), (0,)), ((), ()))
KERNEL_VMEM = 24 * 1024 * 1024
VMEM = pl.BlockSpec(memory_space=pltpu.VMEM)
ANYWHERE = pl.BlockSpec(memory_space=pl.ANY)
BASIS_PARTS = 4
AXES = ("y", "core", "x", "z")


def in_hbm(value):
    return pltpu.with_memory_space_constraint(value, pltpu.HBM)


def in_vmem(value):
    return pltpu.with_memory_space_constraint(value, pltpu.VMEM)


def dot_nt(left, right):
    return lax.dot_general(left, right, NT, preferred_element_type=jnp.float32)


def dot_nn(left, right):
    return lax.dot_general(left, right, NN, preferred_element_type=jnp.float32)


def split2(value):
    high = value.astype(jnp.bfloat16)
    return high, (value - high.astype(jnp.float32)).astype(jnp.bfloat16)


def complex_rows(rows):
    real, imag = rows[:8], rows[8:]
    return jnp.concatenate(
        [jnp.concatenate([real, -imag], axis=1), jnp.concatenate([imag, real], axis=1)], axis=0
    )


def leaf_product(rows, real, imag):
    return dot_nt(
        complex_rows(rows).astype(jnp.bfloat16), jnp.concatenate([real, imag], axis=1)
    )


def leaves_in_kernel(
    basis_ref, leaf_ref, out_ref, rows_ref, newest_ref, held_ref, newest_sem, held_sems
):
    steps = held_sems.shape[0]
    count = held_ref.shape[1]
    part = count // steps
    newest_copy = pltpu.make_async_copy(
        basis_ref.at[basis_ref.shape[0] - 1], newest_ref, newest_sem
    )
    newest_copy.start()
    copies = []
    for step in range(steps):
        here = pl.ds(step * part, part)
        copies.append(
            pltpu.make_async_copy(leaf_ref.at[:, here], held_ref.at[:, here], held_sems.at[step])
        )
        copies[-1].start()
    newest_copy.wait()
    for leaf in range(count):
        if leaf % part == 0:
            copies[leaf // part].wait()
        rows = newest_ref[:, :, leaf * 128 : (leaf + 1) * 128].reshape(16, 128)
        rows = rows.astype(jnp.bfloat16).astype(jnp.float32)
        rows_ref[leaf] = rows
        out_ref[leaf] = leaf_product(rows, held_ref[0, leaf], held_ref[1, leaf])


def leaves_in(krylov_basis, leaves, steps):
    count = leaves.shape[1]
    rows = jax.ShapeDtypeStruct((count, 16, 128), jnp.float32)
    return pl.pallas_call(
        leaves_in_kernel,
        in_specs=[pl.BlockSpec(memory_space=pltpu.HBM)] * 2,
        out_specs=[VMEM] * 2,
        out_shape=[rows, rows],
        scratch_shapes=[
            pltpu.VMEM(krylov_basis.shape[1:], jnp.float32),
            pltpu.VMEM(leaves.shape, leaves.dtype),
            pltpu.SemaphoreType.DMA,
            pltpu.SemaphoreType.DMA((steps,)),
        ],
        compiler_params=pltpu.CompilerParams(vmem_limit_bytes=KERNEL_VMEM),
        cost_estimate=pl.CostEstimate(
            flops=count * 16 * 256 * 128 * 2, bytes_accessed=count * 73728, transcendentals=0
        ),
    )(in_hbm(krylov_basis), in_hbm(leaves))


def near_kernel(rows_ref, leaf_ref, out_ref):
    for leaf in range(rows_ref.shape[0]):
        out_ref[leaf] = leaf_product(rows_ref[leaf], leaf_ref[0, leaf], leaf_ref[1, leaf])


def near_product(rows, near_field):
    return pl.pallas_call(
        near_kernel,
        in_specs=[VMEM] * 2,
        out_specs=VMEM,
        out_shape=jax.ShapeDtypeStruct(rows.shape, jnp.float32),
        compiler_params=pltpu.CompilerParams(vmem_limit_bytes=KERNEL_VMEM),
        cost_estimate=pl.CostEstimate(
            flops=rows.shape[0] * 16 * 256 * 128 * 2, bytes_accessed=2 << 20, transcendentals=0
        ),
    )(rows, near_field)


def stacked(basis):
    width = basis.shape[3]
    return jnp.concatenate(
        [basis[:, 0].reshape(128, width), basis[:, 1].reshape(128, width)], axis=0
    )


def basis_gram_kernel(basis_ref, out_ref, high_ref, low_ref, held_ref, sems):
    steps = sems.shape[0]
    width = held_ref.shape[3] // steps
    copies = []
    for step in range(steps):
        here = pl.ds(step * width, width)
        copies.append(
            pltpu.make_async_copy(
                basis_ref.at[:, :, :, here], held_ref.at[:, :, :, here], sems.at[step]
            )
        )
        copies[-1].start()
    even = jnp.zeros((256, 256), jnp.float32)
    odd = jnp.zeros((256, 256), jnp.float32)
    for step, copy in enumerate(copies):
        copy.wait()
        here = slice(step * width, (step + 1) * width)
        high, low = split2(stacked(held_ref[:, :, :, here]))
        high_ref[:, here] = high
        low_ref[:, here] = low
        even += dot_nt(high, high)
        odd += dot_nt(high, low)
    gram = even + odd + odd.T
    real = gram[:128, :128] + gram[128:, 128:]
    imag = gram[:128, 128:] - gram[128:, :128]
    row = lax.broadcasted_iota(jnp.int32, (128, 128), 0)
    column = lax.broadcasted_iota(jnp.int32, (128, 128), 1)
    out_ref[...] = jnp.where(row <= column, real, imag)


def basis_gram(krylov_basis):
    part = pltpu.VMEM((256, krylov_basis.shape[3]), jnp.bfloat16)
    gram, *parts = pl.pallas_call(
        basis_gram_kernel,
        in_specs=[pl.BlockSpec(memory_space=pltpu.HBM)],
        out_specs=[VMEM] * 3,
        out_shape=[jax.ShapeDtypeStruct((128, 128), jnp.float32), part, part],
        scratch_shapes=[
            pltpu.VMEM(krylov_basis.shape, jnp.float32),
            pltpu.SemaphoreType.DMA((BASIS_PARTS,)),
        ],
        compiler_params=pltpu.CompilerParams(vmem_limit_bytes=KERNEL_VMEM),
        cost_estimate=pl.CostEstimate(
            flops=2 * 2 * 256 * 256 * 4096, bytes_accessed=8 << 20, transcendentals=0
        ),
    )(in_hbm(krylov_basis))
    return gram, parts


def mix(level, own_ref, partner_ref, mixer_ref, rank_ref, table_ref):
    table = table_ref[level]
    picked = jnp.concatenate([partner_ref[table[0, leaf]] for leaf in range(32)], axis=0)
    both = jnp.concatenate([own_ref[...].reshape(512, 128), picked], axis=1)
    weights = jnp.concatenate(
        [
            jnp.concatenate([mixer_ref[level, 0, 0], mixer_ref[level, 0, 1]], axis=1),
            jnp.concatenate([mixer_ref[level, 1, 0], mixer_ref[level, 1, 1]], axis=1),
        ],
        axis=0,
    )
    high, low = split2(both)
    w_high, w_low = split2(weights)
    product = dot_nn(high, w_high) + dot_nn(high, w_low) + dot_nn(low, w_high)
    column = lax.broadcasted_iota(jnp.int32, (16, 128), 1)
    ranks = rank_ref[level : level + 1]

    def leaf_value(leaf):
        by_real = product[leaf * 16 : (leaf + 1) * 16, :128]
        by_imag = product[leaf * 16 : (leaf + 1) * 16, 128:]
        mixed = jnp.concatenate([by_real[:8] - by_imag[8:], by_real[8:] + by_imag[:8]], axis=0)
        return jnp.where(column < ranks[0, leaf], mixed, 0.0)

    return leaf_value


def level_kernel(level, own_ref, partner_ref, mixer_ref, rank_ref, table_ref, gram_ref, out_ref):
    leaf_value = mix(level, own_ref, partner_ref, mixer_ref, rank_ref, table_ref)
    for leaf in range(32):
        out_ref[leaf] = leaf_value(leaf)


def next_level(level, own, partner, level_mixers, block_ranks, partner_tables, gram):
    return pl.pallas_call(
        lambda *refs: level_kernel(level, *refs),
        in_specs=[VMEM] * 5 + [ANYWHERE],
        out_specs=VMEM,
        out_shape=jax.ShapeDtypeStruct(own.shape, jnp.float32),
        compiler_params=pltpu.CompilerParams(vmem_limit_bytes=KERNEL_VMEM),
        cost_estimate=pl.CostEstimate(
            flops=3 * 512 * 256 * 256 * 2, bytes_accessed=1 << 20, transcendentals=0
        ),
    )(own, partner, level_mixers, block_ranks, partner_tables, gram)


def project_kernel(
    level, own_ref, partner_ref, mixer_ref, rank_ref, table_ref, close_ref, leaf_ref,
    high_ref, low_ref, before_ref, image_ref, sums_ref,
):
    leaf_value = mix(level, own_ref, partner_ref, mixer_ref, rank_ref, table_ref)
    for leaf in range(32):
        rounded = leaf_value(leaf).astype(jnp.bfloat16).astype(jnp.float32)
        far = leaf_product(rounded, leaf_ref[0, leaf], leaf_ref[1, leaf])
        image_ref[:, leaf * 128 : (leaf + 1) * 128] = far + close_ref[leaf]
    high, low = split2(image_ref[...])
    two = jnp.concatenate([high, low], axis=0)

    def product(first, second):
        one = dot_nt(two, first)
        return one[:16] + one[16:] + dot_nt(high, second)

    inner = product(high_ref[...], low_ref[...])
    square = product(high, low)
    sums_ref[0:8] = inner[:8, :128] + inner[8:, 128:]
    sums_ref[8:16] = inner[8:, :128] - inner[:8, 128:]
    real = square[:8, :8] + square[8:, 8:]
    imag = square[:8, 8:] - square[8:, :8]
    sums_ref[16:24] = jnp.concatenate([real, imag, jnp.zeros((8, 112), jnp.float32)], axis=1)


def project(level, own, partner, level_mixers, block_ranks, partner_tables, close, leaf_out, parts, gram):
    return pl.pallas_call(
        lambda *refs: project_kernel(level, *refs),
        in_specs=[VMEM] * 9 + [ANYWHERE],
        out_specs=[VMEM] * 2,
        out_shape=[
            jax.ShapeDtypeStruct((16, 4096), jnp.float32),
            jax.ShapeDtypeStruct((24, 128), jnp.float32),
        ],
        compiler_params=pltpu.CompilerParams(vmem_limit_bytes=KERNEL_VMEM),
        cost_estimate=pl.CostEstimate(
            flops=6 * 512 * 256 * 256 * 2, bytes_accessed=8 << 20, transcendentals=0
        ),
    )(
        own, partner, level_mixers, block_ranks, partner_tables, close, leaf_out,
        *[in_vmem(part) for part in parts], gram,
    )


def merge_kernel(own_ref, other_ref, gram_ref, other_gram_ref, out_ref, gram_sum_ref):
    sums = own_ref[...] + other_ref[...]
    gram_sum_ref[...] = gram_ref[...] + other_gram_ref[...]
    mine = lax.rem(lax.axis_index("y"), 2) * 2 + lax.rem(lax.axis_index("x"), 2)
    piece = gram_sum_ref[pl.ds(pl.multiple_of(mine * 32, 32), 32), :]
    for device in range(out_ref.shape[0]):
        out_ref[device, 0:24] = sums
        out_ref[device, 24:56] = piece


def merge(own, other, gram, other_gram):
    return pl.pallas_call(
        merge_kernel,
        in_specs=[VMEM] * 4,
        out_specs=VMEM,
        out_shape=jax.ShapeDtypeStruct((lax.axis_size(("y", "x")), 56, 128), jnp.float32),
        scratch_shapes=[pltpu.VMEM((128, 128), jnp.float32)],
        compiler_params=pltpu.CompilerParams(vmem_limit_bytes=KERNEL_VMEM),
    )(own, other, gram, other_gram)


def relay_kernel(got_ref, out_ref, gram_ref):
    sums = jnp.sum(got_ref[:, 0:24], axis=0)
    for device in range(out_ref.shape[0]):
        out_ref[device] = sums
    for quarter in range(4):
        at = quarter // 2 * 4 + quarter % 2
        gram_ref[quarter * 32 : (quarter + 1) * 32] = (got_ref[at, 24:56] + got_ref[at + 2, 24:56]) + (
            got_ref[at + 8, 24:56] + got_ref[at + 10, 24:56]
        )


def relay(got):
    return pl.pallas_call(
        relay_kernel,
        in_specs=[VMEM],
        out_specs=[VMEM] * 2,
        out_shape=[
            jax.ShapeDtypeStruct((lax.axis_size("z"), 24, 128), jnp.float32),
            jax.ShapeDtypeStruct((128, 128), jnp.float32),
        ],
        compiler_params=pltpu.CompilerParams(vmem_limit_bytes=KERNEL_VMEM),
    )(got)


def dot_high(left, right, numbers):
    return lax.dot_general(
        left, right, numbers, precision=lax.Precision.HIGHEST, preferred_element_type=jnp.float32
    )


def finish_kernel(
    scale, got_ref, gram_ref, image_ref, high_ref, low_ref, total_ref, new_ref, block_ref
):
    sums = jnp.sum(got_ref[...], axis=0) * scale
    first = sums[:16]
    packed = gram_ref[...] * scale
    row = lax.broadcasted_iota(jnp.int32, (128, 128), 0)
    column = lax.broadcasted_iota(jnp.int32, (128, 128), 1)
    flipped = packed.T
    gram_real = jnp.where(row <= column, packed, flipped)
    gram_imag = jnp.where(row > column, packed, jnp.where(row < column, -flipped, 0.0))
    gram = jnp.concatenate([gram_real, gram_imag], axis=1)

    def by_gram(rows):
        one = dot_high(rows, gram, NN)
        real = one[:8, :128] + one[8:, 128:]
        imag = one[8:, :128] - one[:8, 128:]
        return jnp.concatenate([real, imag], axis=0)

    total = first + (first - by_gram(first))
    rest = first - by_gram(total)

    def inner(left, right):
        one = dot_high(left, right, NT)
        return one[:8, :8] + one[8:, 8:], one[:8, 8:] - one[8:, :8]

    one_real, one_imag = inner(first, total)
    two_real, two_imag = inner(total, rest)
    block_ref[0] = sums[16:24, 0:8] - one_real - two_real
    block_ref[1] = sums[16:24, 8:16] - one_imag - two_imag
    high, low = split2(complex_rows(total))
    two = jnp.concatenate([high, low], axis=0)
    width = 1024
    for start in range(0, 4096, width):
        here = slice(start, start + width)
        one = dot_nn(two, high_ref[:, here])
        taken = one[:16] + one[16:] + dot_nn(high, low_ref[:, here])
        new_ref[:, :, here] = (image_ref[:, here] - taken).reshape(2, 8, width)
    turn = jnp.where(row == lax.rem(column, 16) * 8 + lax.div(column, 16), 1.0, 0.0)
    turned = dot_high(total, turn, NN)
    for angle in range(8):
        total_ref[0, angle] = turned[:8, angle * 16 : (angle + 1) * 16]
        total_ref[1, angle] = turned[8:, angle * 16 : (angle + 1) * 16]


def finish(scale, got, gram, image, parts):
    return pl.pallas_call(
        lambda *refs: finish_kernel(scale, *refs),
        in_specs=[VMEM] * 5,
        out_specs=[VMEM] * 3,
        out_shape=[
            jax.ShapeDtypeStruct((2, 8, 8, 16), jnp.float32),
            jax.ShapeDtypeStruct((2, 8, 4096), jnp.float32),
            jax.ShapeDtypeStruct((2, 8, 8), jnp.float32),
        ],
        compiler_params=pltpu.CompilerParams(vmem_limit_bytes=KERNEL_VMEM),
        cost_estimate=pl.CostEstimate(
            flops=6 * 16 * 256 * 4096 * 2, bytes_accessed=6 << 20, transcendentals=0
        ),
    )(got, gram, image, *[in_vmem(part) for part in parts])


def exchange(value, axis, bit_number):
    pairs = [(source, source ^ (1 << bit_number)) for source in range(lax.axis_size(axis))]
    return lax.ppermute(value, axis, pairs)


def per_device(
    krylov_basis, near_field, leaf_in, leaf_out, level_mixers, block_ranks, partner_tables
):
    plan = [("y", 1), ("y", 0), ("x", 1), ("x", 0), ("z", 2)]
    beside = [("core", 0), ("z", 1), ("z", 0), ("y", 0), ("x", 0)]
    coeffs, rows = leaves_in(krylov_basis, leaf_in, 4)
    gram, parts = basis_gram(krylov_basis)
    close = near_product(rows, near_field)
    for level, (axis, bit) in enumerate(plan):
        partner = exchange(coeffs, axis, bit)
        gram = gram + exchange(gram, *beside[level])
        operands = (level, coeffs, partner, level_mixers, block_ranks, partner_tables)
        if level < len(plan) - 1:
            coeffs = next_level(*operands, gram)
        else:
            image, sums = project(*operands, close, leaf_out, parts, gram)
    got = merge(sums, exchange(sums, "core", 0), gram, exchange(gram, "z", 2))
    got, gram = relay(lax.all_to_all(got, ("y", "x"), 0, 0))
    got = lax.all_to_all(got, "z", 0, 0)
    scale = 1.0 / (krylov_basis.shape[3] * lax.axis_size(AXES))
    total, new_block, block_gram = finish(scale, got, gram, image, parts)
    return jnp.transpose(total, (3, 0, 1, 2)), new_block, block_gram


def solution(mesh):
    mesh = Mesh(mesh.devices.reshape(4, 2, 4, 8), AXES)
    in_specs = (
        P(None, None, None, AXES),
        P(None, AXES, None, None),
        P(None, AXES, None, None),
        P(None, AXES, None, None),
        P(None, None, None, None, AXES),
        P(None, AXES),
        P(None, AXES, None),
    )
    out_specs = (P(), P(None, None, AXES), P())
    return jax.shard_map(
        per_device, mesh=mesh, in_specs=in_specs, out_specs=out_specs, check_vma=False
    )
```

```python
import jax
import jax.numpy as jnp
from jax import lax
from jax.experimental import pallas as pl
from jax.experimental.pallas import tpu as pltpu
from jax.sharding import Mesh
from jax.sharding import PartitionSpec as P

NT = (((1,), (1,)), ((), ()))
NN = (((1,), (0,)), ((), ()))
KERNEL_VMEM = 24 * 1024 * 1024
VMEM = pl.BlockSpec(memory_space=pltpu.VMEM)
ANYWHERE = pl.BlockSpec(memory_space=pl.ANY)
BASIS_PARTS = 4
LEVEL_FLOPS = 1_000_000_000
AXES = ("y", "core", "x", "z")


def in_hbm(value):
    return pltpu.with_memory_space_constraint(value, pltpu.HBM)


def in_vmem(value):
    return pltpu.with_memory_space_constraint(value, pltpu.VMEM)


def dot_nt(left, right):
    return lax.dot_general(left, right, NT, preferred_element_type=jnp.float32)


def dot_nn(left, right):
    return lax.dot_general(left, right, NN, preferred_element_type=jnp.float32)


def split2(value):
    high = value.astype(jnp.bfloat16)
    return high, (value - high.astype(jnp.float32)).astype(jnp.bfloat16)


def complex_rows(rows):
    real, imag = rows[:8], rows[8:]
    return jnp.concatenate(
        [jnp.concatenate([real, -imag], axis=1), jnp.concatenate([imag, real], axis=1)], axis=0
    )


def times_i(rows):
    turned = pltpu.roll(rows, 4, 0)
    upper = lax.broadcasted_iota(jnp.int32, rows.shape, 0) < 4
    return jnp.where(upper, -turned, turned)


def halves(rows):
    return [
        jnp.concatenate([rows[at : at + 4], rows[8 + at : 12 + at]], axis=0) for at in (0, 4)
    ]


def leaf_product(rows, real, imag):
    return dot_nt(
        complex_rows(rows).astype(jnp.bfloat16), jnp.concatenate([real, imag], axis=1)
    )


def leaves_in_kernel(
    basis_ref, leaf_ref, first_ref, second_ref, rows_ref, newest_ref, held_ref, newest_sem, held_sems
):
    steps = held_sems.shape[0]
    count = held_ref.shape[1]
    part = count // steps
    newest_copy = pltpu.make_async_copy(
        basis_ref.at[basis_ref.shape[0] - 1], newest_ref, newest_sem
    )
    newest_copy.start()
    copies = []
    for step in range(steps):
        here = pl.ds(step * part, part)
        copies.append(
            pltpu.make_async_copy(leaf_ref.at[:, here], held_ref.at[:, here], held_sems.at[step])
        )
        copies[-1].start()
    newest_copy.wait()
    for leaf in range(count):
        if leaf % part == 0:
            copies[leaf // part].wait()
        rows = newest_ref[:, :, leaf * 128 : (leaf + 1) * 128].reshape(16, 128)
        rows = rows.astype(jnp.bfloat16).astype(jnp.float32)
        rows_ref[leaf] = rows
        both = [jnp.concatenate([half, times_i(half)], axis=1) for half in halves(rows)]
        product = dot_nt(
            jnp.concatenate(both, axis=0).astype(jnp.bfloat16),
            jnp.concatenate([held_ref[0, leaf], held_ref[1, leaf]], axis=1),
        )
        first_ref[leaf] = product[:8]
        second_ref[leaf] = product[8:]


def leaves_in(krylov_basis, leaves, steps):
    count = leaves.shape[1]
    half = jax.ShapeDtypeStruct((count, 8, 128), jnp.float32)
    rows = jax.ShapeDtypeStruct((count, 16, 128), jnp.float32)
    return pl.pallas_call(
        leaves_in_kernel,
        in_specs=[pl.BlockSpec(memory_space=pltpu.HBM)] * 2,
        out_specs=[VMEM] * 3,
        out_shape=[half, half, rows],
        scratch_shapes=[
            pltpu.VMEM(krylov_basis.shape[1:], jnp.float32),
            pltpu.VMEM(leaves.shape, leaves.dtype),
            pltpu.SemaphoreType.DMA,
            pltpu.SemaphoreType.DMA((steps,)),
        ],
        compiler_params=pltpu.CompilerParams(vmem_limit_bytes=KERNEL_VMEM),
        cost_estimate=pl.CostEstimate(
            flops=count * 16 * 256 * 128 * 2, bytes_accessed=count * 73728, transcendentals=0
        ),
    )(in_hbm(krylov_basis), in_hbm(leaves))


def near_kernel(rows_ref, leaf_ref, before_ref, out_ref):
    for leaf in range(rows_ref.shape[0]):
        out_ref[leaf] = leaf_product(rows_ref[leaf], leaf_ref[0, leaf], leaf_ref[1, leaf])


def near_product(rows, near_field, before):
    return pl.pallas_call(
        near_kernel,
        in_specs=[VMEM] * 2 + [ANYWHERE],
        out_specs=VMEM,
        out_shape=jax.ShapeDtypeStruct(rows.shape, jnp.float32),
        compiler_params=pltpu.CompilerParams(vmem_limit_bytes=KERNEL_VMEM),
        cost_estimate=pl.CostEstimate(
            flops=rows.shape[0] * 16 * 256 * 128 * 2, bytes_accessed=2 << 20, transcendentals=0
        ),
    )(rows, near_field, before)


def stacked(basis):
    width = basis.shape[3]
    return jnp.concatenate(
        [basis[:, 0].reshape(128, width), basis[:, 1].reshape(128, width)], axis=0
    )


def basis_gram_kernel(basis_ref, before_ref, out_ref, high_ref, low_ref):
    width = basis_ref.shape[3] // BASIS_PARTS
    even = jnp.zeros((256, 256), jnp.float32)
    odd = jnp.zeros((256, 256), jnp.float32)
    for step in range(BASIS_PARTS):
        here = slice(step * width, (step + 1) * width)
        high, low = split2(stacked(basis_ref[:, :, :, here]))
        high_ref[:, here] = high
        low_ref[:, here] = low
        even += dot_nt(high, high)
        odd += dot_nt(high, low)
    gram = even + odd + odd.T
    real = gram[:128, :128] + gram[128:, 128:]
    imag = gram[:128, 128:] - gram[128:, :128]
    row = lax.broadcasted_iota(jnp.int32, (128, 128), 0)
    column = lax.broadcasted_iota(jnp.int32, (128, 128), 1)
    out_ref[...] = jnp.where(row <= column, real, imag)


def basis_gram(krylov_basis, before):
    part = pltpu.VMEM((256, krylov_basis.shape[3]), jnp.bfloat16)
    gram, *parts = pl.pallas_call(
        basis_gram_kernel,
        in_specs=[VMEM, ANYWHERE],
        out_specs=[VMEM] * 3,
        out_shape=[jax.ShapeDtypeStruct((128, 128), jnp.float32), part, part],
        compiler_params=pltpu.CompilerParams(vmem_limit_bytes=KERNEL_VMEM),
        cost_estimate=pl.CostEstimate(
            flops=2 * 2 * 256 * 256 * 4096, bytes_accessed=8 << 20, transcendentals=0
        ),
    )(in_vmem(krylov_basis), before)
    return gram, parts


def mix(level, own_ref, partner_ref, mixer_ref, rank_ref, table_ref):
    table = table_ref[level]
    picked = jnp.concatenate([partner_ref[table[0, leaf]] for leaf in range(32)], axis=0)
    weights = jnp.concatenate(
        [
            jnp.concatenate([mixer_ref[level, 0, 0], mixer_ref[level, 0, 1]], axis=1),
            jnp.concatenate([mixer_ref[level, 1, 0], mixer_ref[level, 1, 1]], axis=1),
        ],
        axis=0,
    )
    high, low = split2(jnp.concatenate([own_ref[...].reshape(256, 128), picked], axis=1))
    w_high, w_low = split2(weights)
    product = dot_nn(high, w_high) + dot_nn(high, w_low) + dot_nn(low, w_high)
    column = lax.broadcasted_iota(jnp.int32, (8, 128), 1)
    ranks = rank_ref[level : level + 1]

    def leaf_value(leaf):
        at = leaf * 8
        mixed = product[at : at + 8, :128] + times_i(product[at : at + 8, 128:])
        return jnp.where(column < ranks[0, leaf], mixed, 0.0)

    return leaf_value


def level_kernel(level, own_ref, partner_ref, mixer_ref, rank_ref, table_ref, *refs):
    out_ref = refs[-1]
    leaf_value = mix(level, own_ref, partner_ref, mixer_ref, rank_ref, table_ref)
    for leaf in range(32):
        out_ref[leaf] = leaf_value(leaf)


def next_level(level, own, partner, tables, before):
    return pl.pallas_call(
        lambda *refs: level_kernel(level, *refs),
        in_specs=[VMEM] * 5 + [ANYWHERE] * len(before),
        out_specs=VMEM,
        out_shape=jax.ShapeDtypeStruct(own.shape, jnp.float32),
        compiler_params=pltpu.CompilerParams(vmem_limit_bytes=KERNEL_VMEM),
        cost_estimate=pl.CostEstimate(
            flops=LEVEL_FLOPS, bytes_accessed=1 << 20, transcendentals=0
        ),
    )(own, partner, *tables, *before)


def project_kernel(
    level, lower_ref, own_ref, partner_ref, mixer_ref, rank_ref, table_ref,
    close_ref, leaf_ref, high_ref, low_ref, image_ref, sums_ref,
):
    leaf_value = mix(level, own_ref, partner_ref, mixer_ref, rank_ref, table_ref)
    for leaf in range(32):
        one, two = lower_ref[leaf], leaf_value(leaf)
        rows = jnp.concatenate([one[:4], two[:4], one[4:], two[4:]], axis=0)
        rounded = rows.astype(jnp.bfloat16).astype(jnp.float32)
        far = leaf_product(rounded, leaf_ref[0, leaf], leaf_ref[1, leaf])
        image_ref[:, leaf * 128 : (leaf + 1) * 128] = far + close_ref[leaf]
    high, low = split2(image_ref[...])
    two = jnp.concatenate([high, low], axis=0)

    def product(first, second):
        one = dot_nt(two, first)
        return one[:16] + one[16:] + dot_nt(high, second)

    inner = product(high_ref[...], low_ref[...])
    square = product(high, low)
    sums_ref[0:8] = inner[:8, :128] + inner[8:, 128:]
    sums_ref[8:16] = inner[8:, :128] - inner[:8, 128:]
    real = square[:8, :8] + square[8:, 8:]
    imag = square[:8, 8:] - square[8:, :8]
    sums_ref[16:24] = jnp.concatenate([real, imag, jnp.zeros((8, 112), jnp.float32)], axis=1)


def project(level, lower, own, partner, tables, close, leaf_out, parts):
    return pl.pallas_call(
        lambda *refs: project_kernel(level, *refs),
        in_specs=[VMEM] * 10,
        out_specs=[VMEM] * 2,
        out_shape=[
            jax.ShapeDtypeStruct((16, 4096), jnp.float32),
            jax.ShapeDtypeStruct((24, 128), jnp.float32),
        ],
        compiler_params=pltpu.CompilerParams(vmem_limit_bytes=KERNEL_VMEM),
        cost_estimate=pl.CostEstimate(
            flops=6 * 512 * 256 * 256 * 2, bytes_accessed=8 << 20, transcendentals=0
        ),
    )(lower, own, partner, *tables, close, leaf_out, *[in_vmem(part) for part in parts])


def stack_kernel(sums_ref, gram_ref, other_ref, out_ref):
    out_ref[0:24] = sums_ref[...]
    out_ref[24:152] = gram_ref[...] + other_ref[...]


def stack(sums, gram, other):
    return pl.pallas_call(
        stack_kernel,
        in_specs=[VMEM] * 3,
        out_specs=VMEM,
        out_shape=jax.ShapeDtypeStruct((152, 128), jnp.float32),
        compiler_params=pltpu.CompilerParams(vmem_limit_bytes=KERNEL_VMEM),
    )(sums, gram, other)


def merge_kernel(own_ref, other_ref, out_ref, sum_ref):
    sum_ref[...] = own_ref[...] + other_ref[...]
    mine = lax.rem(lax.axis_index("y"), 2) * 2 + lax.rem(lax.axis_index("x"), 2)
    sums = sum_ref[0:24]
    piece = sum_ref[pl.ds(pl.multiple_of(24 + mine * 32, 8), 32), :]
    for device in range(out_ref.shape[0]):
        out_ref[device, 0:24] = sums
        out_ref[device, 24:56] = piece


def merge(own, other):
    return pl.pallas_call(
        merge_kernel,
        in_specs=[VMEM] * 2,
        out_specs=VMEM,
        out_shape=jax.ShapeDtypeStruct((lax.axis_size(("y", "x")), 56, 128), jnp.float32),
        scratch_shapes=[pltpu.VMEM((152, 128), jnp.float32)],
        compiler_params=pltpu.CompilerParams(vmem_limit_bytes=KERNEL_VMEM),
    )(own, other)


def relay_kernel(got_ref, out_ref, gram_ref):
    sums = jnp.sum(got_ref[:, 0:24], axis=0)
    for device in range(out_ref.shape[0]):
        out_ref[device] = sums
    for quarter in range(4):
        at = quarter // 2 * 4 + quarter % 2
        gram_ref[quarter * 32 : (quarter + 1) * 32] = (got_ref[at, 24:56] + got_ref[at + 2, 24:56]) + (
            got_ref[at + 8, 24:56] + got_ref[at + 10, 24:56]
        )


def relay(got):
    return pl.pallas_call(
        relay_kernel,
        in_specs=[VMEM],
        out_specs=[VMEM] * 2,
        out_shape=[
            jax.ShapeDtypeStruct((lax.axis_size("z"), 24, 128), jnp.float32),
            jax.ShapeDtypeStruct((128, 128), jnp.float32),
        ],
        compiler_params=pltpu.CompilerParams(vmem_limit_bytes=KERNEL_VMEM),
    )(got)


def dot_high(left, right, numbers):
    return lax.dot_general(
        left, right, numbers, precision=lax.Precision.HIGHEST, preferred_element_type=jnp.float32
    )


def finish_kernel(
    scale, got_ref, gram_ref, image_ref, high_ref, low_ref, total_ref, new_ref, block_ref
):
    sums = jnp.sum(got_ref[...], axis=0) * scale
    first = sums[:16]
    packed = gram_ref[...] * scale
    row = lax.broadcasted_iota(jnp.int32, (128, 128), 0)
    column = lax.broadcasted_iota(jnp.int32, (128, 128), 1)
    flipped = packed.T
    gram_real = jnp.where(row <= column, packed, flipped)
    gram_imag = jnp.where(row > column, packed, jnp.where(row < column, -flipped, 0.0))
    gram = jnp.concatenate([gram_real, gram_imag], axis=1)

    def by_gram(rows):
        one = dot_high(rows, gram, NN)
        real = one[:8, :128] + one[8:, 128:]
        imag = one[8:, :128] - one[:8, 128:]
        return jnp.concatenate([real, imag], axis=0)

    total = first + (first - by_gram(first))
    rest = first - by_gram(total)

    def inner(left, right):
        one = dot_high(left, right, NT)
        return one[:8, :8] + one[8:, 8:], one[:8, 8:] - one[8:, :8]

    one_real, one_imag = inner(first, total)
    two_real, two_imag = inner(total, rest)
    block_ref[0] = sums[16:24, 0:8] - one_real - two_real
    block_ref[1] = sums[16:24, 8:16] - one_imag - two_imag
    high, low = split2(complex_rows(total))
    two = jnp.concatenate([high, low], axis=0)
    width = 1024
    for start in range(0, 4096, width):
        here = slice(start, start + width)
        one = dot_nn(two, high_ref[:, here])
        taken = one[:16] + one[16:] + dot_nn(high, low_ref[:, here])
        new_ref[:, :, here] = (image_ref[:, here] - taken).reshape(2, 8, width)
    turn = jnp.where(row == lax.rem(column, 16) * 8 + lax.div(column, 16), 1.0, 0.0)
    turned = dot_high(total, turn, NN)
    for angle in range(8):
        total_ref[0, angle] = turned[:8, angle * 16 : (angle + 1) * 16]
        total_ref[1, angle] = turned[8:, angle * 16 : (angle + 1) * 16]


def finish(scale, got, gram, image, parts):
    return pl.pallas_call(
        lambda *refs: finish_kernel(scale, *refs),
        in_specs=[VMEM] * 5,
        out_specs=[VMEM] * 3,
        out_shape=[
            jax.ShapeDtypeStruct((2, 8, 8, 16), jnp.float32),
            jax.ShapeDtypeStruct((2, 8, 4096), jnp.float32),
            jax.ShapeDtypeStruct((2, 8, 8), jnp.float32),
        ],
        compiler_params=pltpu.CompilerParams(vmem_limit_bytes=KERNEL_VMEM),
        cost_estimate=pl.CostEstimate(
            flops=6 * 16 * 256 * 4096 * 2, bytes_accessed=6 << 20, transcendentals=0
        ),
    )(got, gram, image, *[in_vmem(part) for part in parts])


def add_kernel(left_ref, right_ref, before_ref, out_ref):
    out_ref[...] = left_ref[...] + right_ref[...]


def add_after(left, right, before):
    return pl.pallas_call(
        add_kernel,
        in_specs=[VMEM, VMEM, ANYWHERE],
        out_specs=VMEM,
        out_shape=jax.ShapeDtypeStruct(left.shape, left.dtype),
        compiler_params=pltpu.CompilerParams(vmem_limit_bytes=KERNEL_VMEM),
    )(left, right, before)


def exchange(value, axis, bit_number):
    pairs = [(source, source ^ (1 << bit_number)) for source in range(lax.axis_size(axis))]
    return lax.ppermute(value, axis, pairs)


def per_device(
    krylov_basis, near_field, leaf_in, leaf_out, level_mixers, block_ranks, partner_tables
):
    plan = [("y", 1), ("y", 0), ("x", 1), ("x", 0), ("z", 2)]
    *coeffs, rows = leaves_in(krylov_basis, leaf_in, 2)
    gram, parts = basis_gram(krylov_basis, coeffs[0])
    tables = (level_mixers, block_ranks, partner_tables)
    gram_bits = [("x", 0), ("z", 0), ("z", 1), ("y", 0)]
    for level, (axis, bit) in enumerate(plan):
        partner = [exchange(half, axis, bit) for half in coeffs]
        before = [gram] if level == 0 else []
        lower = next_level(level, coeffs[0], partner[0], tables, before)
        if level < len(plan) - 1:
            moved = exchange(gram, *gram_bits[level])
            upper = next_level(level, coeffs[1], partner[1], tables, [lower, moved])
            gram = add_after(gram, moved, upper)
            coeffs = [lower, upper]
        else:
            close = near_product(rows, near_field, gram)
            image, sums = project(
                level, lower, coeffs[1], partner[1], tables, close, leaf_out, parts
            )
    sums = stack(sums, gram, exchange(gram, "z", 2))
    got = merge(sums, exchange(sums, "core", 0))
    got, gram = relay(lax.all_to_all(got, ("y", "x"), 0, 0))
    got = lax.all_to_all(got, "z", 0, 0)
    scale = 1.0 / (krylov_basis.shape[3] * lax.axis_size(AXES))
    total, new_block, block_gram = finish(scale, got, gram, image, parts)
    return jnp.transpose(total, (3, 0, 1, 2)), new_block, block_gram


def solution(mesh):
    mesh = Mesh(mesh.devices.reshape(4, 2, 4, 8), AXES)
    in_specs = (
        P(None, None, None, AXES),
        P(None, AXES, None, None),
        P(None, AXES, None, None),
        P(None, AXES, None, None),
        P(None, None, None, None, AXES),
        P(None, AXES),
        P(None, AXES, None),
    )
    out_specs = (P(), P(None, None, AXES), P())
    return jax.shard_map(
        per_device, mesh=mesh, in_specs=in_specs, out_specs=out_specs, check_vma=False
    )
```

```python
import jax
import jax.numpy as jnp
from jax import lax
from jax.experimental import pallas as pl
from jax.experimental.pallas import tpu as pltpu
from jax.sharding import Mesh
from jax.sharding import PartitionSpec as P

NT = (((1,), (1,)), ((), ()))
NN = (((1,), (0,)), ((), ()))
KERNEL_VMEM = 24 * 1024 * 1024
VMEM = pl.BlockSpec(memory_space=pltpu.VMEM)
ANYWHERE = pl.BlockSpec(memory_space=pl.ANY)
BASIS_PARTS = 4
LEVEL_FLOPS = 1_000_000_000
AXES = ("y", "core", "x", "z")


def in_hbm(value):
    return pltpu.with_memory_space_constraint(value, pltpu.HBM)


def in_vmem(value):
    return pltpu.with_memory_space_constraint(value, pltpu.VMEM)


def dot_nt(left, right):
    return lax.dot_general(left, right, NT, preferred_element_type=jnp.float32)


def dot_nn(left, right):
    return lax.dot_general(left, right, NN, preferred_element_type=jnp.float32)


def split2(value):
    high = value.astype(jnp.bfloat16)
    return high, (value - high.astype(jnp.float32)).astype(jnp.bfloat16)


def complex_rows(rows):
    real, imag = rows[:8], rows[8:]
    return jnp.concatenate(
        [jnp.concatenate([real, -imag], axis=1), jnp.concatenate([imag, real], axis=1)], axis=0
    )


def times_i(rows):
    turned = pltpu.roll(rows, 4, 0)
    upper = lax.broadcasted_iota(jnp.int32, rows.shape, 0) < 4
    return jnp.where(upper, -turned, turned)


def halves(rows):
    return [
        jnp.concatenate([rows[at : at + 4], rows[8 + at : 12 + at]], axis=0) for at in (0, 4)
    ]


def leaf_product(rows, real, imag):
    return dot_nt(
        complex_rows(rows).astype(jnp.bfloat16), jnp.concatenate([real, imag], axis=1)
    )


def leaves_in_kernel(
    basis_ref, leaf_ref, first_ref, second_ref, rows_ref, newest_ref, held_ref, newest_sem, held_sems
):
    steps = held_sems.shape[0]
    count = held_ref.shape[1]
    part = count // steps
    newest_copy = pltpu.make_async_copy(
        basis_ref.at[basis_ref.shape[0] - 1], newest_ref, newest_sem
    )
    newest_copy.start()
    copies = []
    for step in range(steps):
        here = pl.ds(step * part, part)
        copies.append(
            pltpu.make_async_copy(leaf_ref.at[:, here], held_ref.at[:, here], held_sems.at[step])
        )
        copies[-1].start()
    newest_copy.wait()
    for leaf in range(count):
        if leaf % part == 0:
            copies[leaf // part].wait()
        rows = newest_ref[:, :, leaf * 128 : (leaf + 1) * 128].reshape(16, 128)
        rows = rows.astype(jnp.bfloat16).astype(jnp.float32)
        rows_ref[leaf] = rows
        both = [jnp.concatenate([half, times_i(half)], axis=1) for half in halves(rows)]
        product = dot_nt(
            jnp.concatenate(both, axis=0).astype(jnp.bfloat16),
            jnp.concatenate([held_ref[0, leaf], held_ref[1, leaf]], axis=1),
        )
        first_ref[leaf] = product[:8]
        second_ref[leaf] = product[8:]


def leaves_in(krylov_basis, leaves, steps):
    count = leaves.shape[1]
    half = jax.ShapeDtypeStruct((count, 8, 128), jnp.float32)
    rows = jax.ShapeDtypeStruct((count, 16, 128), jnp.float32)
    return pl.pallas_call(
        leaves_in_kernel,
        in_specs=[pl.BlockSpec(memory_space=pltpu.HBM)] * 2,
        out_specs=[VMEM] * 3,
        out_shape=[half, half, rows],
        scratch_shapes=[
            pltpu.VMEM(krylov_basis.shape[1:], jnp.float32),
            pltpu.VMEM(leaves.shape, leaves.dtype),
            pltpu.SemaphoreType.DMA,
            pltpu.SemaphoreType.DMA((steps,)),
        ],
        compiler_params=pltpu.CompilerParams(vmem_limit_bytes=KERNEL_VMEM),
        cost_estimate=pl.CostEstimate(
            flops=count * 16 * 256 * 128 * 2, bytes_accessed=count * 73728, transcendentals=0
        ),
    )(in_hbm(krylov_basis), in_hbm(leaves))


def near_kernel(rows_ref, leaf_ref, before_ref, out_ref):
    for leaf in range(rows_ref.shape[0]):
        out_ref[leaf] = leaf_product(rows_ref[leaf], leaf_ref[0, leaf], leaf_ref[1, leaf])


def near_product(rows, near_field, before):
    return pl.pallas_call(
        near_kernel,
        in_specs=[VMEM] * 2 + [ANYWHERE],
        out_specs=VMEM,
        out_shape=jax.ShapeDtypeStruct(rows.shape, jnp.float32),
        compiler_params=pltpu.CompilerParams(vmem_limit_bytes=KERNEL_VMEM),
        cost_estimate=pl.CostEstimate(
            flops=rows.shape[0] * 16 * 256 * 128 * 2, bytes_accessed=2 << 20, transcendentals=0
        ),
    )(rows, near_field, before)


def stacked(basis):
    width = basis.shape[3]
    return jnp.concatenate(
        [basis[:, 0].reshape(128, width), basis[:, 1].reshape(128, width)], axis=0
    )


def basis_gram_kernel(basis_ref, before_ref, out_ref, high_ref, low_ref):
    width = basis_ref.shape[3] // BASIS_PARTS
    even = jnp.zeros((256, 256), jnp.float32)
    odd = jnp.zeros((256, 256), jnp.float32)
    for step in range(BASIS_PARTS):
        here = slice(step * width, (step + 1) * width)
        high, low = split2(stacked(basis_ref[:, :, :, here]))
        high_ref[:, here] = high
        low_ref[:, here] = low
        even += dot_nt(high, high)
        odd += dot_nt(high, low)
    gram = even + odd + odd.T
    real = gram[:128, :128] + gram[128:, 128:]
    imag = gram[:128, 128:] - gram[128:, :128]
    row = lax.broadcasted_iota(jnp.int32, (128, 128), 0)
    column = lax.broadcasted_iota(jnp.int32, (128, 128), 1)
    out_ref[...] = jnp.where(row <= column, real, imag)


def basis_gram(krylov_basis, before):
    part = pltpu.VMEM((256, krylov_basis.shape[3]), jnp.bfloat16)
    gram, *parts = pl.pallas_call(
        basis_gram_kernel,
        in_specs=[VMEM, ANYWHERE],
        out_specs=[VMEM] * 3,
        out_shape=[jax.ShapeDtypeStruct((128, 128), jnp.float32), part, part],
        compiler_params=pltpu.CompilerParams(vmem_limit_bytes=KERNEL_VMEM),
        cost_estimate=pl.CostEstimate(
            flops=2 * 2 * 256 * 256 * 4096, bytes_accessed=8 << 20, transcendentals=0
        ),
    )(in_vmem(krylov_basis), before)
    return gram, parts


def mix(level, own_ref, partner_ref, mixer_ref, rank_ref, table_ref):
    table = table_ref[level]
    picked = jnp.concatenate([partner_ref[table[0, leaf]] for leaf in range(32)], axis=0)
    weights = jnp.concatenate(
        [
            jnp.concatenate([mixer_ref[level, 0, 0], mixer_ref[level, 0, 1]], axis=1),
            jnp.concatenate([mixer_ref[level, 1, 0], mixer_ref[level, 1, 1]], axis=1),
        ],
        axis=0,
    )
    high, low = split2(jnp.concatenate([own_ref[...].reshape(256, 128), picked], axis=1))
    w_high, w_low = split2(weights)
    product = dot_nn(high, w_high) + dot_nn(high, w_low) + dot_nn(low, w_high)
    column = lax.broadcasted_iota(jnp.int32, (8, 128), 1)
    ranks = rank_ref[level : level + 1]

    def leaf_value(leaf):
        at = leaf * 8
        mixed = product[at : at + 8, :128] + times_i(product[at : at + 8, 128:])
        return jnp.where(column < ranks[0, leaf], mixed, 0.0)

    return leaf_value


def level_kernel(level, own_ref, partner_ref, mixer_ref, rank_ref, table_ref, *refs):
    out_ref = refs[-1]
    leaf_value = mix(level, own_ref, partner_ref, mixer_ref, rank_ref, table_ref)
    for leaf in range(32):
        out_ref[leaf] = leaf_value(leaf)


def next_level(level, own, partner, tables, before):
    return pl.pallas_call(
        lambda *refs: level_kernel(level, *refs),
        in_specs=[VMEM] * 5 + [ANYWHERE] * len(before),
        out_specs=VMEM,
        out_shape=jax.ShapeDtypeStruct(own.shape, jnp.float32),
        compiler_params=pltpu.CompilerParams(vmem_limit_bytes=KERNEL_VMEM),
        cost_estimate=pl.CostEstimate(
            flops=LEVEL_FLOPS, bytes_accessed=1 << 20, transcendentals=0
        ),
    )(own, partner, *tables, *before)


def project_kernel(
    level, lower_ref, own_ref, partner_ref, mixer_ref, rank_ref, table_ref,
    close_ref, leaf_ref, high_ref, low_ref, image_ref, sums_ref,
):
    leaf_value = mix(level, own_ref, partner_ref, mixer_ref, rank_ref, table_ref)
    for leaf in range(32):
        one, two = lower_ref[leaf], leaf_value(leaf)
        rows = jnp.concatenate([one[:4], two[:4], one[4:], two[4:]], axis=0)
        rounded = rows.astype(jnp.bfloat16).astype(jnp.float32)
        far = leaf_product(rounded, leaf_ref[0, leaf], leaf_ref[1, leaf])
        image_ref[:, leaf * 128 : (leaf + 1) * 128] = far + close_ref[leaf]
    high, low = split2(image_ref[...])
    two = jnp.concatenate([high, low], axis=0)

    def product(first, second):
        one = dot_nt(two, first)
        return one[:16] + one[16:] + dot_nt(high, second)

    inner = product(high_ref[...], low_ref[...])
    square = product(high, low)
    sums_ref[0:8] = inner[:8, :128] + inner[8:, 128:]
    sums_ref[8:16] = inner[8:, :128] - inner[:8, 128:]
    real = square[:8, :8] + square[8:, 8:]
    imag = square[:8, 8:] - square[8:, :8]
    sums_ref[16:24] = jnp.concatenate([real, imag, jnp.zeros((8, 112), jnp.float32)], axis=1)


def project(level, lower, own, partner, tables, close, leaf_out, parts):
    return pl.pallas_call(
        lambda *refs: project_kernel(level, *refs),
        in_specs=[VMEM] * 10,
        out_specs=[VMEM] * 2,
        out_shape=[
            jax.ShapeDtypeStruct((16, 4096), jnp.float32),
            jax.ShapeDtypeStruct((24, 128), jnp.float32),
        ],
        compiler_params=pltpu.CompilerParams(vmem_limit_bytes=KERNEL_VMEM),
        cost_estimate=pl.CostEstimate(
            flops=6 * 512 * 256 * 256 * 2, bytes_accessed=8 << 20, transcendentals=0
        ),
    )(lower, own, partner, *tables, close, leaf_out, *[in_vmem(part) for part in parts])


def stack_kernel(sums_ref, gram_ref, other_ref, out_ref):
    out_ref[0:24] = sums_ref[...]
    out_ref[24:152] = gram_ref[...] + other_ref[...]


def stack(sums, gram, other):
    return pl.pallas_call(
        stack_kernel,
        in_specs=[VMEM] * 3,
        out_specs=VMEM,
        out_shape=jax.ShapeDtypeStruct((152, 128), jnp.float32),
        compiler_params=pltpu.CompilerParams(vmem_limit_bytes=KERNEL_VMEM),
    )(sums, gram, other)


def merge_kernel(own_ref, other_ref, out_ref, sum_ref):
    sum_ref[...] = own_ref[...] + other_ref[...]
    mine = lax.rem(lax.axis_index("y"), 2) * 2 + lax.rem(lax.axis_index("x"), 2)
    sums = sum_ref[0:24]
    piece = sum_ref[pl.ds(pl.multiple_of(24 + mine * 32, 8), 32), :]
    for device in range(out_ref.shape[0]):
        out_ref[device, 0:24] = sums
        out_ref[device, 24:56] = piece


def merge(own, other):
    return pl.pallas_call(
        merge_kernel,
        in_specs=[VMEM] * 2,
        out_specs=VMEM,
        out_shape=jax.ShapeDtypeStruct((lax.axis_size(("y", "x")), 56, 128), jnp.float32),
        scratch_shapes=[pltpu.VMEM((152, 128), jnp.float32)],
        compiler_params=pltpu.CompilerParams(vmem_limit_bytes=KERNEL_VMEM),
    )(own, other)


def relay_kernel(got_ref, out_ref, gram_ref):
    sums = jnp.sum(got_ref[:, 0:24], axis=0)
    for device in range(out_ref.shape[0]):
        out_ref[device] = sums
    for quarter in range(4):
        at = quarter // 2 * 4 + quarter % 2
        gram_ref[quarter * 32 : (quarter + 1) * 32] = (got_ref[at, 24:56] + got_ref[at + 2, 24:56]) + (
            got_ref[at + 8, 24:56] + got_ref[at + 10, 24:56]
        )


def relay(got):
    return pl.pallas_call(
        relay_kernel,
        in_specs=[VMEM],
        out_specs=[VMEM] * 2,
        out_shape=[
            jax.ShapeDtypeStruct((lax.axis_size("z"), 24, 128), jnp.float32),
            jax.ShapeDtypeStruct((128, 128), jnp.float32),
        ],
        compiler_params=pltpu.CompilerParams(vmem_limit_bytes=KERNEL_VMEM),
    )(got)


def dot_high(left, right, numbers):
    return lax.dot_general(
        left, right, numbers, precision=lax.Precision.HIGHEST, preferred_element_type=jnp.float32
    )


def finish_kernel(
    scale, got_ref, gram_ref, image_ref, high_ref, low_ref, total_ref, new_ref, block_ref
):
    sums = jnp.sum(got_ref[...], axis=0) * scale
    first = sums[:16]
    packed = gram_ref[...] * scale
    row = lax.broadcasted_iota(jnp.int32, (128, 128), 0)
    column = lax.broadcasted_iota(jnp.int32, (128, 128), 1)
    flipped = packed.T
    gram_real = jnp.where(row <= column, packed, flipped)
    gram_imag = jnp.where(row > column, packed, jnp.where(row < column, -flipped, 0.0))
    gram = jnp.concatenate([gram_real, gram_imag], axis=1)

    gram_high, gram_low = split2(gram)

    def by_gram(rows):
        high, low = split2(rows)
        one = dot_nn(high, gram_high) + dot_nn(high, gram_low) + dot_nn(low, gram_high)
        real = one[:8, :128] + one[8:, 128:]
        imag = one[8:, :128] - one[:8, 128:]
        return jnp.concatenate([real, imag], axis=0)

    total = first + (first - by_gram(first))
    rest = first - by_gram(total)

    def inner(left, right):
        one = dot_high(left, right, NT)
        return one[:8, :8] + one[8:, 8:], one[:8, 8:] - one[8:, :8]

    one_real, one_imag = inner(first, total)
    two_real, two_imag = inner(total, rest)
    block_ref[0] = sums[16:24, 0:8] - one_real - two_real
    block_ref[1] = sums[16:24, 8:16] - one_imag - two_imag
    high, low = split2(complex_rows(total))
    two = jnp.concatenate([high, low], axis=0)
    width = 1024
    for start in range(0, 4096, width):
        here = slice(start, start + width)
        one = dot_nn(two, high_ref[:, here])
        taken = one[:16] + one[16:] + dot_nn(high, low_ref[:, here])
        new_ref[:, :, here] = (image_ref[:, here] - taken).reshape(2, 8, width)
    turn = jnp.where(row == lax.rem(column, 16) * 8 + lax.div(column, 16), 1.0, 0.0)
    turned = dot_high(total, turn, NN)
    for angle in range(8):
        total_ref[0, angle] = turned[:8, angle * 16 : (angle + 1) * 16]
        total_ref[1, angle] = turned[8:, angle * 16 : (angle + 1) * 16]


def finish(scale, got, gram, image, parts):
    return pl.pallas_call(
        lambda *refs: finish_kernel(scale, *refs),
        in_specs=[VMEM] * 5,
        out_specs=[VMEM] * 3,
        out_shape=[
            jax.ShapeDtypeStruct((2, 8, 8, 16), jnp.float32),
            jax.ShapeDtypeStruct((2, 8, 4096), jnp.float32),
            jax.ShapeDtypeStruct((2, 8, 8), jnp.float32),
        ],
        compiler_params=pltpu.CompilerParams(vmem_limit_bytes=KERNEL_VMEM),
        cost_estimate=pl.CostEstimate(
            flops=6 * 16 * 256 * 4096 * 2, bytes_accessed=6 << 20, transcendentals=0
        ),
    )(got, gram, image, *[in_vmem(part) for part in parts])


def add_kernel(left_ref, right_ref, before_ref, out_ref):
    out_ref[...] = left_ref[...] + right_ref[...]


def add_after(left, right, before):
    return pl.pallas_call(
        add_kernel,
        in_specs=[VMEM, VMEM, ANYWHERE],
        out_specs=VMEM,
        out_shape=jax.ShapeDtypeStruct(left.shape, left.dtype),
        compiler_params=pltpu.CompilerParams(vmem_limit_bytes=KERNEL_VMEM),
    )(left, right, before)


def exchange(value, axis, bit_number):
    pairs = [(source, source ^ (1 << bit_number)) for source in range(lax.axis_size(axis))]
    return lax.ppermute(value, axis, pairs)


def per_device(
    krylov_basis, near_field, leaf_in, leaf_out, level_mixers, block_ranks, partner_tables
):
    plan = [("y", 1), ("y", 0), ("x", 1), ("x", 0), ("z", 2)]
    *coeffs, rows = leaves_in(krylov_basis, leaf_in, 2)
    gram, parts = basis_gram(krylov_basis, coeffs[0])
    tables = (level_mixers, block_ranks, partner_tables)
    gram_bits = [("x", 0), ("z", 0), ("z", 1), ("y", 0)]
    for level, (axis, bit) in enumerate(plan):
        partner = [exchange(half, axis, bit) for half in coeffs]
        before = [gram] if level == 0 else []
        lower = next_level(level, coeffs[0], partner[0], tables, before)
        if level < len(plan) - 1:
            moved = exchange(gram, *gram_bits[level])
            before = [lower, moved] if level < len(plan) - 2 else [lower]
            upper = next_level(level, coeffs[1], partner[1], tables, before)
            gram = add_after(gram, moved, upper)
            coeffs = [lower, upper]
        else:
            close = near_product(rows, near_field, gram)
            image, sums = project(
                level, lower, coeffs[1], partner[1], tables, close, leaf_out, parts
            )
    sums = stack(sums, gram, exchange(gram, "z", 2))
    got = merge(sums, exchange(sums, "core", 0))
    got, gram = relay(lax.all_to_all(got, ("y", "x"), 0, 0))
    got = lax.all_to_all(got, "z", 0, 0)
    scale = 1.0 / (krylov_basis.shape[3] * lax.axis_size(AXES))
    total, new_block, block_gram = finish(scale, got, gram, image, parts)
    return jnp.transpose(total, (3, 0, 1, 2)), new_block, block_gram


def solution(mesh):
    mesh = Mesh(mesh.devices.reshape(4, 2, 4, 8), AXES)
    in_specs = (
        P(None, None, None, AXES),
        P(None, AXES, None, None),
        P(None, AXES, None, None),
        P(None, AXES, None, None),
        P(None, None, None, None, AXES),
        P(None, AXES),
        P(None, AXES, None),
    )
    out_specs = (P(), P(None, None, AXES), P())
    return jax.shard_map(
        per_device, mesh=mesh, in_specs=in_specs, out_specs=out_specs, check_vma=False
    )
```

```python
import jax
import jax.numpy as jnp
from jax import lax
from jax.experimental import pallas as pl
from jax.experimental.pallas import tpu as pltpu
from jax.sharding import Mesh
from jax.sharding import PartitionSpec as P

NT = (((1,), (1,)), ((), ()))
NN = (((1,), (0,)), ((), ()))
KERNEL_VMEM = 24 * 1024 * 1024
VMEM = pl.BlockSpec(memory_space=pltpu.VMEM)
ANYWHERE = pl.BlockSpec(memory_space=pl.ANY)
BASIS_PARTS = 4
LEVEL_FLOPS = 1_000_000_000
AXES = ("y", "core", "x", "z")


def in_hbm(value):
    return pltpu.with_memory_space_constraint(value, pltpu.HBM)


def in_vmem(value):
    return pltpu.with_memory_space_constraint(value, pltpu.VMEM)


def dot_nt(left, right):
    return lax.dot_general(left, right, NT, preferred_element_type=jnp.float32)


def dot_nn(left, right):
    return lax.dot_general(left, right, NN, preferred_element_type=jnp.float32)


def split2(value):
    high = value.astype(jnp.bfloat16)
    return high, (value - high.astype(jnp.float32)).astype(jnp.bfloat16)


def complex_rows(rows):
    real, imag = rows[:8], rows[8:]
    return jnp.concatenate(
        [jnp.concatenate([real, -imag], axis=1), jnp.concatenate([imag, real], axis=1)], axis=0
    )


def times_i(rows):
    turned = pltpu.roll(rows, 4, 0)
    upper = lax.broadcasted_iota(jnp.int32, rows.shape, 0) < 4
    return jnp.where(upper, -turned, turned)


def halves(rows):
    return [
        jnp.concatenate([rows[at : at + 4], rows[8 + at : 12 + at]], axis=0) for at in (0, 4)
    ]


def leaf_product(rows, real, imag):
    return dot_nt(
        complex_rows(rows).astype(jnp.bfloat16), jnp.concatenate([real, imag], axis=1)
    )


def leaves_in_kernel(
    basis_ref, leaf_ref, first_ref, second_ref, rows_ref, newest_ref, held_ref, newest_sem, held_sems
):
    steps = held_sems.shape[0]
    count = held_ref.shape[1]
    part = count // steps
    newest_copy = pltpu.make_async_copy(
        basis_ref.at[basis_ref.shape[0] - 1], newest_ref, newest_sem
    )
    newest_copy.start()
    copies = []
    for step in range(steps):
        here = pl.ds(step * part, part)
        copies.append(
            pltpu.make_async_copy(leaf_ref.at[:, here], held_ref.at[:, here], held_sems.at[step])
        )
        copies[-1].start()
    newest_copy.wait()
    for leaf in range(count):
        if leaf % part == 0:
            copies[leaf // part].wait()
        rows = newest_ref[:, :, leaf * 128 : (leaf + 1) * 128].reshape(16, 128)
        rows = rows.astype(jnp.bfloat16).astype(jnp.float32)
        rows_ref[leaf] = rows
        both = [jnp.concatenate([half, times_i(half)], axis=1) for half in halves(rows)]
        product = dot_nt(
            jnp.concatenate(both, axis=0).astype(jnp.bfloat16),
            jnp.concatenate([held_ref[0, leaf], held_ref[1, leaf]], axis=1),
        )
        first_ref[leaf] = product[:8]
        second_ref[leaf] = product[8:]


def leaves_in(krylov_basis, leaves, steps):
    count = leaves.shape[1]
    half = jax.ShapeDtypeStruct((count, 8, 128), jnp.float32)
    rows = jax.ShapeDtypeStruct((count, 16, 128), jnp.float32)
    return pl.pallas_call(
        leaves_in_kernel,
        in_specs=[pl.BlockSpec(memory_space=pltpu.HBM)] * 2,
        out_specs=[VMEM] * 3,
        out_shape=[half, half, rows],
        scratch_shapes=[
            pltpu.VMEM(krylov_basis.shape[1:], jnp.float32),
            pltpu.VMEM(leaves.shape, leaves.dtype),
            pltpu.SemaphoreType.DMA,
            pltpu.SemaphoreType.DMA((steps,)),
        ],
        compiler_params=pltpu.CompilerParams(vmem_limit_bytes=KERNEL_VMEM),
        cost_estimate=pl.CostEstimate(
            flops=count * 16 * 256 * 128 * 2, bytes_accessed=count * 73728, transcendentals=0
        ),
    )(in_hbm(krylov_basis), in_hbm(leaves))


def near_kernel(rows_ref, leaf_ref, before_ref, out_ref):
    for leaf in range(rows_ref.shape[0]):
        out_ref[leaf] = leaf_product(rows_ref[leaf], leaf_ref[0, leaf], leaf_ref[1, leaf])


def near_product(rows, near_field, before):
    return pl.pallas_call(
        near_kernel,
        in_specs=[VMEM] * 2 + [ANYWHERE],
        out_specs=VMEM,
        out_shape=jax.ShapeDtypeStruct(rows.shape, jnp.float32),
        compiler_params=pltpu.CompilerParams(vmem_limit_bytes=KERNEL_VMEM),
        cost_estimate=pl.CostEstimate(
            flops=rows.shape[0] * 16 * 256 * 128 * 2, bytes_accessed=2 << 20, transcendentals=0
        ),
    )(rows, near_field, before)


def stacked(basis):
    width = basis.shape[3]
    return jnp.concatenate(
        [basis[:, 0].reshape(128, width), basis[:, 1].reshape(128, width)], axis=0
    )


def basis_gram_kernel(basis_ref, before_ref, out_ref, high_ref, low_ref):
    width = basis_ref.shape[3] // BASIS_PARTS
    even = jnp.zeros((256, 256), jnp.float32)
    odd = jnp.zeros((256, 256), jnp.float32)
    for step in range(BASIS_PARTS):
        here = slice(step * width, (step + 1) * width)
        high, low = split2(stacked(basis_ref[:, :, :, here]))
        high_ref[:, here] = high
        low_ref[:, here] = low
        even += dot_nt(high, high)
        odd += dot_nt(high, low)
    gram = even + odd + odd.T
    real = gram[:128, :128] + gram[128:, 128:]
    imag = gram[:128, 128:] - gram[128:, :128]
    row = lax.broadcasted_iota(jnp.int32, (128, 128), 0)
    column = lax.broadcasted_iota(jnp.int32, (128, 128), 1)
    out_ref[...] = jnp.where(row <= column, real, imag)


def basis_gram(krylov_basis, before):
    part = pltpu.VMEM((256, krylov_basis.shape[3]), jnp.bfloat16)
    gram, *parts = pl.pallas_call(
        basis_gram_kernel,
        in_specs=[VMEM, ANYWHERE],
        out_specs=[VMEM] * 3,
        out_shape=[jax.ShapeDtypeStruct((128, 128), jnp.float32), part, part],
        compiler_params=pltpu.CompilerParams(vmem_limit_bytes=KERNEL_VMEM),
        cost_estimate=pl.CostEstimate(
            flops=2 * 2 * 256 * 256 * 4096, bytes_accessed=8 << 20, transcendentals=0
        ),
    )(in_vmem(krylov_basis), before)
    return gram, parts


def mix(level, own_ref, partner_ref, mixer_ref, rank_ref, table_ref):
    table = table_ref[level]
    picked = jnp.concatenate([partner_ref[table[0, leaf]] for leaf in range(32)], axis=0)
    weights = jnp.concatenate(
        [
            jnp.concatenate([mixer_ref[level, 0, 0], mixer_ref[level, 0, 1]], axis=1),
            jnp.concatenate([mixer_ref[level, 1, 0], mixer_ref[level, 1, 1]], axis=1),
        ],
        axis=0,
    )
    high, low = split2(jnp.concatenate([own_ref[...].reshape(256, 128), picked], axis=1))
    w_high, w_low = split2(weights)
    product = dot_nn(high, w_high) + dot_nn(high, w_low) + dot_nn(low, w_high)
    column = lax.broadcasted_iota(jnp.int32, (8, 128), 1)
    ranks = rank_ref[level : level + 1]

    def leaf_value(leaf):
        at = leaf * 8
        mixed = product[at : at + 8, :128] + times_i(product[at : at + 8, 128:])
        return jnp.where(column < ranks[0, leaf], mixed, 0.0)

    return leaf_value


def level_kernel(level, own_ref, partner_ref, mixer_ref, rank_ref, table_ref, *refs):
    out_ref = refs[-1]
    leaf_value = mix(level, own_ref, partner_ref, mixer_ref, rank_ref, table_ref)
    for leaf in range(32):
        out_ref[leaf] = leaf_value(leaf)


def next_level(level, own, partner, tables, before):
    return pl.pallas_call(
        lambda *refs: level_kernel(level, *refs),
        in_specs=[VMEM] * 5 + [ANYWHERE] * len(before),
        out_specs=VMEM,
        out_shape=jax.ShapeDtypeStruct(own.shape, jnp.float32),
        compiler_params=pltpu.CompilerParams(vmem_limit_bytes=KERNEL_VMEM),
        cost_estimate=pl.CostEstimate(
            flops=LEVEL_FLOPS, bytes_accessed=1 << 20, transcendentals=0
        ),
    )(own, partner, *tables, *before)


def project_kernel(
    level, lower_ref, own_ref, partner_ref, mixer_ref, rank_ref, table_ref,
    close_ref, leaf_ref, high_ref, low_ref, image_ref, sums_ref,
):
    leaf_value = mix(level, own_ref, partner_ref, mixer_ref, rank_ref, table_ref)
    for leaf in range(32):
        one, two = lower_ref[leaf], leaf_value(leaf)
        rows = jnp.concatenate([one[:4], two[:4], one[4:], two[4:]], axis=0)
        rounded = rows.astype(jnp.bfloat16).astype(jnp.float32)
        far = leaf_product(rounded, leaf_ref[0, leaf], leaf_ref[1, leaf])
        image_ref[:, leaf * 128 : (leaf + 1) * 128] = far + close_ref[leaf]
    high, low = split2(image_ref[...])
    two = jnp.concatenate([high, low], axis=0)

    def product(first, second):
        one = dot_nt(two, first)
        return one[:16] + one[16:] + dot_nt(high, second)

    inner = product(high_ref[...], low_ref[...])
    square = product(high, low)
    sums_ref[0:8] = inner[:8, :128] + inner[8:, 128:]
    sums_ref[8:16] = inner[8:, :128] - inner[:8, 128:]
    real = square[:8, :8] + square[8:, 8:]
    imag = square[:8, 8:] - square[8:, :8]
    sums_ref[16:24] = jnp.concatenate([real, imag, jnp.zeros((8, 112), jnp.float32)], axis=1)


def project(level, lower, own, partner, tables, close, leaf_out, parts):
    return pl.pallas_call(
        lambda *refs: project_kernel(level, *refs),
        in_specs=[VMEM] * 10,
        out_specs=[VMEM] * 2,
        out_shape=[
            jax.ShapeDtypeStruct((16, 4096), jnp.float32),
            jax.ShapeDtypeStruct((24, 128), jnp.float32),
        ],
        compiler_params=pltpu.CompilerParams(vmem_limit_bytes=KERNEL_VMEM),
        cost_estimate=pl.CostEstimate(
            flops=6 * 512 * 256 * 256 * 2, bytes_accessed=8 << 20, transcendentals=0
        ),
    )(lower, own, partner, *tables, close, leaf_out, *[in_vmem(part) for part in parts])


def stack_kernel(sums_ref, gram_ref, other_ref, out_ref):
    out_ref[0:24] = sums_ref[...]
    out_ref[24:152] = gram_ref[...] + other_ref[...]


def stack(sums, gram, other):
    return pl.pallas_call(
        stack_kernel,
        in_specs=[VMEM] * 3,
        out_specs=VMEM,
        out_shape=jax.ShapeDtypeStruct((152, 128), jnp.float32),
        compiler_params=pltpu.CompilerParams(vmem_limit_bytes=KERNEL_VMEM),
    )(sums, gram, other)


def merge_kernel(own_ref, other_ref, out_ref, gram_ref):
    sums = own_ref[0:24] + other_ref[0:24]
    for device in range(out_ref.shape[0]):
        out_ref[device] = sums
    gram_ref[...] = own_ref[24:152] + other_ref[24:152]


def merge(own, other):
    return pl.pallas_call(
        merge_kernel,
        in_specs=[VMEM] * 2,
        out_specs=[VMEM] * 2,
        out_shape=[
            jax.ShapeDtypeStruct((lax.axis_size("z"), 24, 128), jnp.float32),
            jax.ShapeDtypeStruct((128, 128), jnp.float32),
        ],
        compiler_params=pltpu.CompilerParams(vmem_limit_bytes=KERNEL_VMEM),
    )(own, other)


def relay_kernel(got_ref, gram_ref, out_ref):
    sums = jnp.sum(got_ref[...], axis=0)
    mine = lax.rem(lax.axis_index("y"), 2) * 2 + lax.rem(lax.axis_index("x"), 2)
    piece = gram_ref[pl.ds(pl.multiple_of(mine * 32, 32), 32), :]
    for device in range(out_ref.shape[0]):
        out_ref[device, 0:24] = sums
        out_ref[device, 24:56] = piece


def relay(got, gram):
    return pl.pallas_call(
        relay_kernel,
        in_specs=[VMEM] * 2,
        out_specs=VMEM,
        out_shape=jax.ShapeDtypeStruct((lax.axis_size(("y", "x")), 56, 128), jnp.float32),
        compiler_params=pltpu.CompilerParams(vmem_limit_bytes=KERNEL_VMEM),
    )(got, gram)


def dot_high(left, right, numbers):
    return lax.dot_general(
        left, right, numbers, precision=lax.Precision.HIGHEST, preferred_element_type=jnp.float32
    )


def finish_kernel(
    scale, got_ref, image_ref, high_ref, low_ref, total_ref, new_ref, block_ref, gram_ref
):
    sums = jnp.sum(got_ref[:, 0:24], axis=0) * scale
    for quarter in range(4):
        at = quarter // 2 * 4 + quarter % 2
        gram_ref[quarter * 32 : (quarter + 1) * 32] = (got_ref[at, 24:56] + got_ref[at + 2, 24:56]) + (
            got_ref[at + 8, 24:56] + got_ref[at + 10, 24:56]
        )
    first = sums[:16]
    packed = gram_ref[...] * scale
    row = lax.broadcasted_iota(jnp.int32, (128, 128), 0)
    column = lax.broadcasted_iota(jnp.int32, (128, 128), 1)
    flipped = packed.T
    gram_real = jnp.where(row <= column, packed, flipped)
    gram_imag = jnp.where(row > column, packed, jnp.where(row < column, -flipped, 0.0))
    gram = jnp.concatenate([gram_real, gram_imag], axis=1)

    gram_high, gram_low = split2(gram)

    def by_gram(rows):
        high, low = split2(rows)
        one = dot_nn(high, gram_high) + dot_nn(high, gram_low) + dot_nn(low, gram_high)
        real = one[:8, :128] + one[8:, 128:]
        imag = one[8:, :128] - one[:8, 128:]
        return jnp.concatenate([real, imag], axis=0)

    total = first + (first - by_gram(first))
    rest = first - by_gram(total)

    def inner(left, right):
        one = dot_high(left, right, NT)
        return one[:8, :8] + one[8:, 8:], one[:8, 8:] - one[8:, :8]

    one_real, one_imag = inner(first, total)
    two_real, two_imag = inner(total, rest)
    block_ref[0] = sums[16:24, 0:8] - one_real - two_real
    block_ref[1] = sums[16:24, 8:16] - one_imag - two_imag
    high, low = split2(complex_rows(total))
    two = jnp.concatenate([high, low], axis=0)
    width = 1024
    for start in range(0, 4096, width):
        here = slice(start, start + width)
        one = dot_nn(two, high_ref[:, here])
        taken = one[:16] + one[16:] + dot_nn(high, low_ref[:, here])
        new_ref[:, :, here] = (image_ref[:, here] - taken).reshape(2, 8, width)
    turn = jnp.where(row == lax.rem(column, 16) * 8 + lax.div(column, 16), 1.0, 0.0)
    turned = dot_high(total, turn, NN)
    for angle in range(8):
        total_ref[0, angle] = turned[:8, angle * 16 : (angle + 1) * 16]
        total_ref[1, angle] = turned[8:, angle * 16 : (angle + 1) * 16]


def finish(scale, got, image, parts):
    return pl.pallas_call(
        lambda *refs: finish_kernel(scale, *refs),
        in_specs=[VMEM] * 4,
        out_specs=[VMEM] * 3,
        out_shape=[
            jax.ShapeDtypeStruct((2, 8, 8, 16), jnp.float32),
            jax.ShapeDtypeStruct((2, 8, 4096), jnp.float32),
            jax.ShapeDtypeStruct((2, 8, 8), jnp.float32),
        ],
        scratch_shapes=[pltpu.VMEM((128, 128), jnp.float32)],
        compiler_params=pltpu.CompilerParams(vmem_limit_bytes=KERNEL_VMEM),
        cost_estimate=pl.CostEstimate(
            flops=6 * 16 * 256 * 4096 * 2, bytes_accessed=6 << 20, transcendentals=0
        ),
    )(got, image, *[in_vmem(part) for part in parts])


def add_kernel(left_ref, right_ref, before_ref, out_ref):
    out_ref[...] = left_ref[...] + right_ref[...]


def add_after(left, right, before):
    return pl.pallas_call(
        add_kernel,
        in_specs=[VMEM, VMEM, ANYWHERE],
        out_specs=VMEM,
        out_shape=jax.ShapeDtypeStruct(left.shape, left.dtype),
        compiler_params=pltpu.CompilerParams(vmem_limit_bytes=KERNEL_VMEM),
    )(left, right, before)


def exchange(value, axis, bit_number):
    pairs = [(source, source ^ (1 << bit_number)) for source in range(lax.axis_size(axis))]
    return lax.ppermute(value, axis, pairs)


def per_device(
    krylov_basis, near_field, leaf_in, leaf_out, level_mixers, block_ranks, partner_tables
):
    plan = [("y", 1), ("y", 0), ("x", 1), ("x", 0), ("z", 2)]
    *coeffs, rows = leaves_in(krylov_basis, leaf_in, 2)
    gram, parts = basis_gram(krylov_basis, coeffs[0])
    tables = (level_mixers, block_ranks, partner_tables)
    gram_bits = [("x", 0), ("z", 0), ("z", 1), ("y", 0)]
    for level, (axis, bit) in enumerate(plan):
        partner = [exchange(half, axis, bit) for half in coeffs]
        before = [gram] if level == 0 else []
        lower = next_level(level, coeffs[0], partner[0], tables, before)
        if level < len(plan) - 1:
            moved = exchange(gram, *gram_bits[level])
            before = [lower, moved] if level < len(plan) - 2 else [lower]
            upper = next_level(level, coeffs[1], partner[1], tables, before)
            gram = add_after(gram, moved, upper)
            coeffs = [lower, upper]
        else:
            close = near_product(rows, near_field, gram)
            image, sums = project(
                level, lower, coeffs[1], partner[1], tables, close, leaf_out, parts
            )
    sums = stack(sums, gram, exchange(gram, "z", 2))
    got, gram = merge(sums, exchange(sums, "core", 0))
    got = relay(lax.all_to_all(got, "z", 0, 0), gram)
    got = lax.all_to_all(got, ("y", "x"), 0, 0)
    scale = 1.0 / (krylov_basis.shape[3] * lax.axis_size(AXES))
    total, new_block, block_gram = finish(scale, got, image, parts)
    return jnp.transpose(total, (3, 0, 1, 2)), new_block, block_gram


def solution(mesh):
    mesh = Mesh(mesh.devices.reshape(4, 2, 4, 8), AXES)
    in_specs = (
        P(None, None, None, AXES),
        P(None, AXES, None, None),
        P(None, AXES, None, None),
        P(None, AXES, None, None),
        P(None, None, None, None, AXES),
        P(None, AXES),
        P(None, AXES, None),
    )
    out_specs = (P(), P(None, None, AXES), P())
    return jax.shard_map(
        per_device, mesh=mesh, in_specs=in_specs, out_specs=out_specs, check_vma=False
    )
```

```python
import jax
import jax.numpy as jnp
from jax import lax
from jax.experimental import pallas as pl
from jax.experimental.pallas import tpu as pltpu
from jax.sharding import Mesh
from jax.sharding import PartitionSpec as P

NT = (((1,), (1,)), ((), ()))
NN = (((1,), (0,)), ((), ()))
KERNEL_VMEM = 24 * 1024 * 1024
VMEM = pl.BlockSpec(memory_space=pltpu.VMEM)
ANYWHERE = pl.BlockSpec(memory_space=pl.ANY)
BASIS_PARTS = 4
LEVEL_FLOPS = 1_000_000_000
AXES = ("y", "core", "x", "z")


def in_hbm(value):
    return pltpu.with_memory_space_constraint(value, pltpu.HBM)


def in_vmem(value):
    return pltpu.with_memory_space_constraint(value, pltpu.VMEM)


def dot_nt(left, right):
    return lax.dot_general(left, right, NT, preferred_element_type=jnp.float32)


def dot_nn(left, right):
    return lax.dot_general(left, right, NN, preferred_element_type=jnp.float32)


def split2(value):
    high = value.astype(jnp.bfloat16)
    return high, (value - high.astype(jnp.float32)).astype(jnp.bfloat16)


def complex_rows(rows):
    real, imag = rows[:8], rows[8:]
    return jnp.concatenate(
        [jnp.concatenate([real, -imag], axis=1), jnp.concatenate([imag, real], axis=1)], axis=0
    )


def times_i(rows):
    turned = pltpu.roll(rows, 4, 0)
    upper = lax.broadcasted_iota(jnp.int32, rows.shape, 0) < 4
    return jnp.where(upper, -turned, turned)


def halves(rows):
    return [
        jnp.concatenate([rows[at : at + 4], rows[8 + at : 12 + at]], axis=0) for at in (0, 4)
    ]


def leaf_product(rows, real, imag):
    return dot_nt(
        complex_rows(rows).astype(jnp.bfloat16), jnp.concatenate([real, imag], axis=1)
    )


def leaves_in_kernel(
    basis_ref, leaf_ref, first_ref, second_ref, rows_ref, newest_ref, held_ref, newest_sem, held_sems
):
    steps = held_sems.shape[0]
    count = held_ref.shape[1]
    part = count // steps
    newest_copy = pltpu.make_async_copy(
        basis_ref.at[basis_ref.shape[0] - 1], newest_ref, newest_sem
    )
    newest_copy.start()
    copies = []
    for step in range(steps):
        here = pl.ds(step * part, part)
        copies.append(
            pltpu.make_async_copy(leaf_ref.at[:, here], held_ref.at[:, here], held_sems.at[step])
        )
        copies[-1].start()
    newest_copy.wait()
    for leaf in range(count):
        if leaf % part == 0:
            copies[leaf // part].wait()
        rows = newest_ref[:, :, leaf * 128 : (leaf + 1) * 128].reshape(16, 128)
        rows = rows.astype(jnp.bfloat16).astype(jnp.float32)
        rows_ref[leaf] = rows
        both = [jnp.concatenate([half, times_i(half)], axis=1) for half in halves(rows)]
        product = dot_nt(
            jnp.concatenate(both, axis=0).astype(jnp.bfloat16),
            jnp.concatenate([held_ref[0, leaf], held_ref[1, leaf]], axis=1),
        )
        first_ref[leaf] = product[:8]
        second_ref[leaf] = product[8:]


def leaves_in(krylov_basis, leaves, steps):
    count = leaves.shape[1]
    half = jax.ShapeDtypeStruct((count, 8, 128), jnp.float32)
    rows = jax.ShapeDtypeStruct((count, 16, 128), jnp.float32)
    return pl.pallas_call(
        leaves_in_kernel,
        in_specs=[pl.BlockSpec(memory_space=pltpu.HBM)] * 2,
        out_specs=[VMEM] * 3,
        out_shape=[half, half, rows],
        scratch_shapes=[
            pltpu.VMEM(krylov_basis.shape[1:], jnp.float32),
            pltpu.VMEM(leaves.shape, leaves.dtype),
            pltpu.SemaphoreType.DMA,
            pltpu.SemaphoreType.DMA((steps,)),
        ],
        compiler_params=pltpu.CompilerParams(vmem_limit_bytes=KERNEL_VMEM),
        cost_estimate=pl.CostEstimate(
            flops=count * 16 * 256 * 128 * 2, bytes_accessed=count * 73728, transcendentals=0
        ),
    )(in_hbm(krylov_basis), in_hbm(leaves))


def near_kernel(rows_ref, leaf_ref, before_ref, out_ref):
    for leaf in range(rows_ref.shape[0]):
        out_ref[leaf] = leaf_product(rows_ref[leaf], leaf_ref[0, leaf], leaf_ref[1, leaf])


def near_product(rows, near_field, before):
    return pl.pallas_call(
        near_kernel,
        in_specs=[VMEM] * 2 + [ANYWHERE],
        out_specs=VMEM,
        out_shape=jax.ShapeDtypeStruct(rows.shape, jnp.float32),
        compiler_params=pltpu.CompilerParams(vmem_limit_bytes=KERNEL_VMEM),
        cost_estimate=pl.CostEstimate(
            flops=rows.shape[0] * 16 * 256 * 128 * 2, bytes_accessed=2 << 20, transcendentals=0
        ),
    )(rows, near_field, before)


def stacked(basis):
    width = basis.shape[3]
    return jnp.concatenate(
        [basis[:, 0].reshape(128, width), basis[:, 1].reshape(128, width)], axis=0
    )


def basis_gram_kernel(basis_ref, before_ref, out_ref, high_ref, low_ref):
    width = basis_ref.shape[3] // BASIS_PARTS
    even = jnp.zeros((256, 256), jnp.float32)
    odd = jnp.zeros((256, 256), jnp.float32)
    for step in range(BASIS_PARTS):
        here = slice(step * width, (step + 1) * width)
        high, low = split2(stacked(basis_ref[:, :, :, here]))
        high_ref[:, here] = high
        low_ref[:, here] = low
        even += dot_nt(high, high)
        odd += dot_nt(high, low)
    gram = even + odd + odd.T
    real = gram[:128, :128] + gram[128:, 128:]
    imag = gram[:128, 128:] - gram[128:, :128]
    row = lax.broadcasted_iota(jnp.int32, (128, 128), 0)
    column = lax.broadcasted_iota(jnp.int32, (128, 128), 1)
    out_ref[...] = jnp.where(row <= column, real, imag)


def basis_gram(krylov_basis, before):
    part = pltpu.VMEM((256, krylov_basis.shape[3]), jnp.bfloat16)
    gram, *parts = pl.pallas_call(
        basis_gram_kernel,
        in_specs=[VMEM, ANYWHERE],
        out_specs=[VMEM] * 3,
        out_shape=[jax.ShapeDtypeStruct((128, 128), jnp.float32), part, part],
        compiler_params=pltpu.CompilerParams(vmem_limit_bytes=KERNEL_VMEM),
        cost_estimate=pl.CostEstimate(
            flops=2 * 2 * 256 * 256 * 4096, bytes_accessed=8 << 20, transcendentals=0
        ),
    )(in_vmem(krylov_basis), before)
    return gram, parts


def mix(level, own_ref, partner_ref, mixer_ref, rank_ref, table_ref):
    table = table_ref[level]
    picked = jnp.concatenate([partner_ref[table[0, leaf]] for leaf in range(32)], axis=0)
    weights = jnp.concatenate(
        [
            jnp.concatenate([mixer_ref[level, 0, 0], mixer_ref[level, 0, 1]], axis=1),
            jnp.concatenate([mixer_ref[level, 1, 0], mixer_ref[level, 1, 1]], axis=1),
        ],
        axis=0,
    )
    high, low = split2(jnp.concatenate([own_ref[...].reshape(256, 128), picked], axis=1))
    w_high, w_low = split2(weights)
    product = dot_nn(high, w_high) + dot_nn(high, w_low) + dot_nn(low, w_high)
    column = lax.broadcasted_iota(jnp.int32, (8, 128), 1)
    ranks = rank_ref[level : level + 1]

    def leaf_value(leaf):
        at = leaf * 8
        mixed = product[at : at + 8, :128] + times_i(product[at : at + 8, 128:])
        return jnp.where(column < ranks[0, leaf], mixed, 0.0)

    return leaf_value


def level_kernel(level, own_ref, partner_ref, mixer_ref, rank_ref, table_ref, *refs):
    out_ref = refs[-1]
    leaf_value = mix(level, own_ref, partner_ref, mixer_ref, rank_ref, table_ref)
    for leaf in range(32):
        out_ref[leaf] = leaf_value(leaf)


def next_level(level, own, partner, tables, before):
    return pl.pallas_call(
        lambda *refs: level_kernel(level, *refs),
        in_specs=[VMEM] * 5 + [ANYWHERE] * len(before),
        out_specs=VMEM,
        out_shape=jax.ShapeDtypeStruct(own.shape, jnp.float32),
        compiler_params=pltpu.CompilerParams(vmem_limit_bytes=KERNEL_VMEM),
        cost_estimate=pl.CostEstimate(
            flops=LEVEL_FLOPS, bytes_accessed=1 << 20, transcendentals=0
        ),
    )(own, partner, *tables, *before)


def project_kernel(
    level, lower_ref, own_ref, partner_ref, mixer_ref, rank_ref, table_ref,
    close_ref, leaf_ref, high_ref, low_ref, image_ref, sums_ref,
):
    leaf_value = mix(level, own_ref, partner_ref, mixer_ref, rank_ref, table_ref)
    for leaf in range(32):
        one, two = lower_ref[leaf], leaf_value(leaf)
        rows = jnp.concatenate([one[:4], two[:4], one[4:], two[4:]], axis=0)
        rounded = rows.astype(jnp.bfloat16).astype(jnp.float32)
        far = leaf_product(rounded, leaf_ref[0, leaf], leaf_ref[1, leaf])
        image_ref[:, leaf * 128 : (leaf + 1) * 128] = far + close_ref[leaf]
    high, low = split2(image_ref[...])
    two = jnp.concatenate([high, low], axis=0)

    def product(first, second):
        one = dot_nt(two, first)
        return one[:16] + one[16:] + dot_nt(high, second)

    inner = product(high_ref[...], low_ref[...])
    square = product(high, low)
    sums_ref[0:8] = inner[:8, :128] + inner[8:, 128:]
    sums_ref[8:16] = inner[8:, :128] - inner[:8, 128:]
    real = square[:8, :8] + square[8:, 8:]
    imag = square[:8, 8:] - square[8:, :8]
    sums_ref[16:24] = jnp.concatenate([real, imag, jnp.zeros((8, 112), jnp.float32)], axis=1)


def project(level, lower, own, partner, tables, close, leaf_out, parts):
    return pl.pallas_call(
        lambda *refs: project_kernel(level, *refs),
        in_specs=[VMEM] * 10,
        out_specs=[VMEM] * 2,
        out_shape=[
            jax.ShapeDtypeStruct((16, 4096), jnp.float32),
            jax.ShapeDtypeStruct((24, 128), jnp.float32),
        ],
        compiler_params=pltpu.CompilerParams(vmem_limit_bytes=KERNEL_VMEM),
        cost_estimate=pl.CostEstimate(
            flops=6 * 512 * 256 * 256 * 2, bytes_accessed=8 << 20, transcendentals=0
        ),
    )(lower, own, partner, *tables, close, leaf_out, *[in_vmem(part) for part in parts])


def stack_kernel(sums_ref, gram_ref, other_ref, out_ref):
    out_ref[0:24] = sums_ref[...]
    out_ref[24:152] = gram_ref[...] + other_ref[...]


def stack(sums, gram, other):
    return pl.pallas_call(
        stack_kernel,
        in_specs=[VMEM] * 3,
        out_specs=VMEM,
        out_shape=jax.ShapeDtypeStruct((152, 128), jnp.float32),
        compiler_params=pltpu.CompilerParams(vmem_limit_bytes=KERNEL_VMEM),
    )(sums, gram, other)


def merge_kernel(own_ref, other_ref, out_ref, gram_ref):
    sums = own_ref[0:24] + other_ref[0:24]
    for device in range(out_ref.shape[0]):
        out_ref[device] = sums
    gram_ref[...] = own_ref[24:152] + other_ref[24:152]


def merge(own, other):
    return pl.pallas_call(
        merge_kernel,
        in_specs=[VMEM] * 2,
        out_specs=[VMEM] * 2,
        out_shape=[
            jax.ShapeDtypeStruct((lax.axis_size("z"), 24, 128), jnp.float32),
            jax.ShapeDtypeStruct((128, 128), jnp.float32),
        ],
        compiler_params=pltpu.CompilerParams(vmem_limit_bytes=KERNEL_VMEM),
    )(own, other)


def relay_kernel(got_ref, gram_ref, out_ref):
    sums = jnp.sum(got_ref[...], axis=0)
    mine = lax.rem(lax.axis_index("y"), 2) * 2 + lax.rem(lax.axis_index("x"), 2)
    piece = gram_ref[pl.ds(pl.multiple_of(mine * 32, 32), 32), :]
    for device in range(out_ref.shape[0]):
        out_ref[device, 0:24] = sums
        out_ref[device, 24:56] = piece


def relay(got, gram):
    return pl.pallas_call(
        relay_kernel,
        in_specs=[VMEM] * 2,
        out_specs=VMEM,
        out_shape=jax.ShapeDtypeStruct((lax.axis_size(("y", "x")), 56, 128), jnp.float32),
        compiler_params=pltpu.CompilerParams(vmem_limit_bytes=KERNEL_VMEM),
    )(got, gram)


def dot_high(left, right, numbers):
    return lax.dot_general(
        left, right, numbers, precision=lax.Precision.HIGHEST, preferred_element_type=jnp.float32
    )


def finish_kernel(
    scale, got_ref, image_ref, high_ref, low_ref, total_ref, new_ref, block_ref, gram_ref
):
    sums = jnp.sum(got_ref[:, 0:24], axis=0) * scale
    for quarter in range(4):
        at = quarter // 2 * 4 + quarter % 2
        gram_ref[quarter * 32 : (quarter + 1) * 32] = (got_ref[at, 24:56] + got_ref[at + 2, 24:56]) + (
            got_ref[at + 8, 24:56] + got_ref[at + 10, 24:56]
        )
    first = sums[:16]
    packed = gram_ref[...] * scale
    row = lax.broadcasted_iota(jnp.int32, (128, 128), 0)
    column = lax.broadcasted_iota(jnp.int32, (128, 128), 1)
    flipped = packed.T
    gram_real = jnp.where(row <= column, packed, flipped)
    gram_imag = jnp.where(row > column, packed, jnp.where(row < column, -flipped, 0.0))
    gram = jnp.concatenate([gram_real, gram_imag], axis=1)

    gram_high, gram_low = split2(gram)

    def by_gram(rows):
        high, low = split2(rows)
        one = dot_nn(high, gram_high) + dot_nn(high, gram_low) + dot_nn(low, gram_high)
        real = one[:8, :128] + one[8:, 128:]
        imag = one[8:, :128] - one[:8, 128:]
        return jnp.concatenate([real, imag], axis=0)

    total = first + (first - by_gram(first))
    rest = first - by_gram(total)

    def inner(left, right):
        one = dot_high(left, right, NT)
        return one[:8, :8] + one[8:, 8:], one[:8, 8:] - one[8:, :8]

    one_real, one_imag = inner(first, total)
    two_real, two_imag = inner(total, rest)
    block_ref[0] = sums[16:24, 0:8] - one_real - two_real
    block_ref[1] = sums[16:24, 8:16] - one_imag - two_imag
    high, low = split2(complex_rows(total))
    two = jnp.concatenate([high, low], axis=0)
    width = 1024
    for start in range(0, 4096, width):
        here = slice(start, start + width)
        one = dot_nn(two, high_ref[:, here])
        taken = one[:16] + one[16:] + dot_nn(high, low_ref[:, here])
        new_ref[:, :, here] = (image_ref[:, here] - taken).reshape(2, 8, width)
    turn = jnp.where(row == lax.rem(column, 16) * 8 + lax.div(column, 16), 1.0, 0.0)
    upper, middle = split2(total)
    lower = (total - upper.astype(jnp.float32)) - middle.astype(jnp.float32)
    parts = jnp.concatenate([upper, middle, lower.astype(jnp.bfloat16)], axis=0)
    parts = dot_nn(parts, turn.astype(jnp.bfloat16))
    turned = parts[:16] + parts[16:32] + parts[32:]
    for angle in range(8):
        total_ref[0, angle] = turned[:8, angle * 16 : (angle + 1) * 16]
        total_ref[1, angle] = turned[8:, angle * 16 : (angle + 1) * 16]


def finish(scale, got, image, parts):
    return pl.pallas_call(
        lambda *refs: finish_kernel(scale, *refs),
        in_specs=[VMEM] * 4,
        out_specs=[VMEM] * 3,
        out_shape=[
            jax.ShapeDtypeStruct((2, 8, 8, 16), jnp.float32),
            jax.ShapeDtypeStruct((2, 8, 4096), jnp.float32),
            jax.ShapeDtypeStruct((2, 8, 8), jnp.float32),
        ],
        scratch_shapes=[pltpu.VMEM((128, 128), jnp.float32)],
        compiler_params=pltpu.CompilerParams(vmem_limit_bytes=KERNEL_VMEM),
        cost_estimate=pl.CostEstimate(
            flops=6 * 16 * 256 * 4096 * 2, bytes_accessed=6 << 20, transcendentals=0
        ),
    )(got, image, *[in_vmem(part) for part in parts])


def add_kernel(left_ref, right_ref, before_ref, out_ref):
    out_ref[...] = left_ref[...] + right_ref[...]


def add_after(left, right, before):
    return pl.pallas_call(
        add_kernel,
        in_specs=[VMEM, VMEM, ANYWHERE],
        out_specs=VMEM,
        out_shape=jax.ShapeDtypeStruct(left.shape, left.dtype),
        compiler_params=pltpu.CompilerParams(vmem_limit_bytes=KERNEL_VMEM),
    )(left, right, before)


def exchange(value, axis, bit_number):
    pairs = [(source, source ^ (1 << bit_number)) for source in range(lax.axis_size(axis))]
    return lax.ppermute(value, axis, pairs)


def per_device(
    krylov_basis, near_field, leaf_in, leaf_out, level_mixers, block_ranks, partner_tables
):
    plan = [("y", 1), ("y", 0), ("x", 1), ("x", 0), ("z", 2)]
    *coeffs, rows = leaves_in(krylov_basis, leaf_in, 2)
    gram, parts = basis_gram(krylov_basis, coeffs[0])
    tables = (level_mixers, block_ranks, partner_tables)
    gram_bits = [("x", 0), ("z", 0), ("z", 1), ("y", 0)]
    for level, (axis, bit) in enumerate(plan):
        partner = [exchange(half, axis, bit) for half in coeffs]
        before = [gram] if level == 0 else []
        lower = next_level(level, coeffs[0], partner[0], tables, before)
        if level < len(plan) - 1:
            moved = exchange(gram, *gram_bits[level])
            before = [lower, moved] if level < len(plan) - 2 else [lower]
            upper = next_level(level, coeffs[1], partner[1], tables, before)
            gram = add_after(gram, moved, upper)
            coeffs = [lower, upper]
        else:
            close = near_product(rows, near_field, gram)
            image, sums = project(
                level, lower, coeffs[1], partner[1], tables, close, leaf_out, parts
            )
    sums = stack(sums, gram, exchange(gram, "z", 2))
    got, gram = merge(sums, exchange(sums, "core", 0))
    got = relay(lax.all_to_all(got, "z", 0, 0), gram)
    got = lax.all_to_all(got, ("y", "x"), 0, 0)
    scale = 1.0 / (krylov_basis.shape[3] * lax.axis_size(AXES))
    total, new_block, block_gram = finish(scale, got, image, parts)
    return jnp.transpose(total, (3, 0, 1, 2)), new_block, block_gram


def solution(mesh):
    mesh = Mesh(mesh.devices.reshape(4, 2, 4, 8), AXES)
    in_specs = (
        P(None, None, None, AXES),
        P(None, AXES, None, None),
        P(None, AXES, None, None),
        P(None, AXES, None, None),
        P(None, None, None, None, AXES),
        P(None, AXES),
        P(None, AXES, None),
    )
    out_specs = (P(), P(None, None, AXES), P())
    return jax.shard_map(
        per_device, mesh=mesh, in_specs=in_specs, out_specs=out_specs, check_vma=False
    )
```
